32 devices in a mesh: blk: 16 (over z, y, core), rep: 2 (over x).
Axes of the slice: x: 2, y: 2, z: 4, core: 2. Of those that a mesh axis runs over, the one named last changes fastest.
Arguments:
- points: float32 [16, 5120], P(None, ('blk', 'rep')), may hold values from -3 to 3
- vectors: float32 [32, 5120], P(None, ('blk', 'rep')), may hold values from -1.2 to 1.2
- lengthscales: float32 [16], replicated, may hold values from 0.6 to 1.6
Outputs:
- product: float32 [32, 5120], P(None, ('blk', 'rep'))
The draws below stay inside these ranges and needn't reach their ends.
All inputs are finite; a program needn't handle non-finite values.
Results may differ from the reference program's by a relative error of at most 0.0003.
Values sent between devices are 32-bit elements; how exact they have to be, the bound alone decides.
No kernel may reach another device: no remote copies, remote signals or barrier semaphores. Data moves between devices by JAX's collectives and lax.ppermute only.
A program may use at most 64 MiB of HBM per device.

```python
import math
import jax
import jax.numpy as jnp
from jax import lax

FEAT = 16
NVEC = 32
NPTS = 5120


def draw_points(key, part):
    clusters = max(NPTS // 128, 1)
    base = jax.random.fold_in(key, 7301)
    key_member, key_centre, key_spread, key_noise = jax.random.split(base, 4)
    membership = jax.random.randint(key_member, (NPTS,), 0, clusters)
    centres = 0.55 * jax.random.normal(key_centre, (FEAT, clusters), jnp.float32)
    spread = jnp.exp(jax.random.uniform(key_spread, (clusters,), jnp.float32, math.log(0.1), math.log(0.2)))
    noise = jax.random.normal(key_noise, (FEAT, NPTS), jnp.float32)
    placed = jnp.take(centres, membership, axis=1) + jnp.take(spread, membership)[None, :] * noise
    return jnp.clip(placed, -3.0, 3.0)


def draw_lengthscales(key, part):
    base = jax.random.fold_in(key, 5113)
    raw = jnp.exp(jax.random.uniform(base, (FEAT,), jnp.float32, math.log(0.6), math.log(1.6)))
    return jnp.clip(raw, 0.6, 1.6)


def shard_levels(stream_key, dims, pieces, smallest, high):
    def one(position, parts):
        draws = jax.random.uniform(jax.random.fold_in(jax.random.fold_in(stream_key, 6), position), (parts,), jnp.float32, smallest / len(pieces), high / len(pieces))
        return jnp.repeat(jnp.exp(draws), dims[position] // parts).reshape((-1,) + (1,) * (len(dims) - position - 1))

    gain = one(*pieces[0])
    for cut in pieces[1:]:
        gain = gain * one(*cut)
    return gain


def bell_draw(key, shape, deviation, most, cuts=(), held_as=jnp.bfloat16):
    level = shard_levels(key, shape, cuts, -0.22, 0.18) if cuts else 1.0
    result = jax.random.normal(key, shape, jnp.float32) * deviation * level
    return jnp.minimum(jnp.maximum(result, -most), most).astype(held_as)


def setup_inputs(seed: int = 0) -> dict:
    arg_keys = jax.random.split(jax.random.key(seed), 4)
    return {
        "points": draw_points(jax.random.fold_in(arg_keys[3], 71), 0),
        "vectors": bell_draw(arg_keys[1], (NVEC, NPTS), 0.2, 1.2, ((1, 32),), jnp.float32),
        "lengthscales": draw_lengthscales(jax.random.fold_in(arg_keys[3], 71), 0),
    }


def matern_block(row_z, row_sq, all_z, all_sq):
    cross = lax.dot_general(row_z, all_z, (((0,), (0,)), ((), ())), precision=lax.Precision.HIGHEST, preferred_element_type=jnp.float32)
    sqdist = jnp.maximum(row_sq[:, None] + all_sq[None, :] - 2.0 * cross, 0.0)
    svalue = jnp.sqrt(5.0 * sqdist)
    return (1.0 + svalue + svalue * svalue / 3.0) * jnp.exp(-svalue)

def reference(points, vectors, lengthscales):
    scaled = points / lengthscales[:, None]
    squares = lax.optimization_barrier(jnp.sum(scaled * scaled, axis=0))
    total = scaled.shape[1]
    width = math.gcd(total, 512)
    count = total // width

    def one_block(index):
        start = (index * width).astype(jnp.int32)
        row_z = lax.dynamic_slice_in_dim(scaled, start, width, 1)
        row_sq = lax.dynamic_slice_in_dim(squares, start, width, 0)
        kernel = matern_block(row_z, row_sq, scaled, squares)
        return lax.dot_general(vectors, kernel, (((1,), (1,)), ((), ())), precision=lax.Precision.HIGHEST, preferred_element_type=jnp.float32)
    blocks = lax.map(one_block, jnp.arange(count, dtype=jnp.int32))
    return jnp.transpose(blocks, (1, 0, 2)).reshape(vectors.shape[0], total)
```

```python
import functools

import jax
import jax.numpy as jnp
from jax import lax
from jax.experimental import pallas as pl
from jax.experimental.pallas import tpu as pltpu
from jax.sharding import PartitionSpec as P

AXES = ("blk", "rep")


def split_blocks(blk, rep):
    for low in range(1, blk + 1):
        if blk % low == 0 and low * rep * low >= 2 * blk:
            return low
    return blk


def partner(index, step, size):
    return index ^ step if size & (size - 1) == 0 else (index + step) % size


def column_perm(blk, rep, low, step):
    perm = []
    for b in range(blk):
        for q in range(rep):
            other = partner((b % low) * rep + q, step, low * rep)
            source = (b // low * low + other // rep) * rep + other % rep
            perm.append((source, b * rep + q))
    return perm


def row_perm(blk, rep, low, step):
    perm = []
    for b in range(blk):
        for q in range(rep):
            other = partner(b // low, step, blk // low)
            perm.append(((other * low + b % low) * rep + q, b * rep + q))
    return perm


def three_parts(value):
    first = value.astype(jnp.bfloat16)
    rest = value - first.astype(jnp.float32)
    second = rest.astype(jnp.bfloat16)
    third = (rest - second.astype(jnp.float32)).astype(jnp.bfloat16)
    return first, second, third


def norm_rows(square, ones_first):
    first, second, third = (part.astype(jnp.float32) for part in three_parts(square))
    line = lax.broadcasted_iota(jnp.int32, (16, square.shape[1]), 0)
    at = line - 3 if ones_first else line
    rows = jnp.where(at == 0, first, jnp.where(at == 1, second, jnp.where(at == 2, third, 0.0)))
    ones = (line < 3) if ones_first else (line >= 3) & (line < 6)
    return jnp.where(ones, 1.0, rows).astype(jnp.bfloat16)


def column_stack(z):
    a, b, c = three_parts(z)
    square = jnp.sum(z * z, axis=0, keepdims=True)
    return jnp.concatenate([a, a, b, a, c, b, norm_rows(square, False)], axis=0)


def row_stack(z):
    a, b, c = three_parts(z * -2.0)
    square = jnp.sum(z * z, axis=0, keepdims=True)
    return jnp.concatenate([a, b, a, c, a, b, norm_rows(square, True)], axis=0)


def tile_of(total, most):
    size = most
    while size >= 128:
        if total % size == 0:
            return size
        size -= 128
    return total


def kernel(nrow, ncol, *refs):
    scale_ref = refs[0]
    row_refs = refs[1 : 1 + nrow]
    col_refs = refs[1 + nrow : 1 + nrow + ncol]
    vec_refs = refs[1 + nrow + ncol : 1 + nrow + 2 * ncol]
    out_refs = refs[1 + nrow + 2 * ncol : 1 + 2 * nrow + 2 * ncol]
    row_feat, col_feat, vec_feat, both_acc, low_acc = refs[1 + 2 * nrow + 2 * ncol :]
    width = row_refs[0].shape[1]
    nvec = vec_refs[0].shape[0]
    scale = jnp.sqrt(jnp.float32(5.0)) / scale_ref[...]
    row_z = jnp.concatenate([ref[...] for ref in row_refs], axis=1) * scale
    row_feat[...] = row_stack(row_z)
    col_z = jnp.concatenate([ref[...] for ref in col_refs], axis=1) * scale
    col_feat[...] = column_stack(col_z)
    vec = jnp.concatenate([ref[...] for ref in vec_refs], axis=1)
    vec_high = vec.astype(jnp.bfloat16)
    vec_low = (vec - vec_high.astype(jnp.float32)).astype(jnp.bfloat16)
    vec_feat[...] = jnp.concatenate([vec_high, vec_low], axis=0)
    rows, cols = nrow * width, ncol * width
    row_tile, col_tile = tile_of(rows, 640), tile_of(cols, 256)

    for row_at in range(0, rows, row_tile):
        here = pl.ds(row_at, row_tile)

        def add(number, carry):
            both, low = carry
            there = pl.ds(pl.multiple_of(number * col_tile, col_tile), col_tile)
            square = lax.dot_general(
                col_feat[:, there],
                row_feat[:, here],
                (((0,), (0,)), ((), ())),
                preferred_element_type=jnp.float32,
            )
            square = jnp.maximum(square, 1e-30)
            svalue = square * lax.rsqrt(square)
            value = (1.0 + svalue + square * (1.0 / 3.0)) * jnp.exp(-svalue)
            high = value.astype(jnp.bfloat16)
            rest = (value - high.astype(jnp.float32)).astype(jnp.bfloat16)
            both = both + jnp.dot(vec_feat[:, there], high, preferred_element_type=jnp.float32)
            low = low + jnp.dot(vec_feat[:nvec, there], rest, preferred_element_type=jnp.float32)
            return both, low

        both, low = lax.fori_loop(
            0,
            cols // col_tile,
            add,
            (jnp.zeros((2 * nvec, row_tile), jnp.float32), jnp.zeros((nvec, row_tile), jnp.float32)),
        )
        both_acc[:, here] = both
        low_acc[:, here] = low
    total = both_acc[:nvec, :] + both_acc[nvec:, :] + low_acc[...]
    for number, ref in enumerate(out_refs):
        ref[...] = total[:, number * width : (number + 1) * width]


def per_device(blk, rep, points, vectors, lengthscales):
    low = split_blocks(blk, rep)
    nrow, ncol = blk // low, low * rep
    width, nvec = points.shape[1], vectors.shape[0]
    row_p = [points] + [lax.ppermute(points, AXES, row_perm(blk, rep, low, k)) for k in range(1, nrow)]
    col_p, col_v = [points], [vectors]
    for k in range(1, ncol):
        perm = column_perm(blk, rep, low, k)
        col_p.append(lax.ppermute(points, AXES, perm))
        col_v.append(lax.ppermute(vectors, AXES, perm))
    rows, cols = nrow * width, ncol * width
    parts = pl.pallas_call(
        functools.partial(kernel, nrow, ncol),
        out_shape=[jax.ShapeDtypeStruct((nvec, width), jnp.float32)] * nrow,
        scratch_shapes=[
            pltpu.VMEM((112, rows), jnp.bfloat16),
            pltpu.VMEM((112, cols), jnp.bfloat16),
            pltpu.VMEM((2 * nvec, cols), jnp.bfloat16),
            pltpu.VMEM((2 * nvec, rows), jnp.float32),
            pltpu.VMEM((nvec, rows), jnp.float32),
        ],
        compiler_params=pltpu.CompilerParams(vmem_limit_bytes=32 * 1024 * 1024),
    )(lengthscales[:, None], *row_p, *col_p, *col_v)
    total = parts[0]
    for k in range(1, nrow):
        back = [(target, source) for source, target in row_perm(blk, rep, low, k)]
        total = total + lax.ppermute(parts[k], AXES, back)
    return total


def solution(mesh):
    return jax.shard_map(
        functools.partial(per_device, mesh.shape["blk"], mesh.shape["rep"]),
        mesh=mesh,
        in_specs=(P(None, AXES), P(None, AXES), P()),
        out_specs=P(None, AXES),
        check_vma=False,
    )
```

```python
import jax
import jax.numpy as jnp
from jax import lax
from jax.experimental import pallas as pl
from jax.experimental.pallas import tpu as pltpu
from jax.sharding import Mesh
from jax.sharding import PartitionSpec as P


def split_blocks(blk, rep):
    for low in range(1, blk + 1):
        if blk % low == 0 and low * rep * low >= 2 * blk:
            return low
    return blk


def three_parts(value):
    first = value.astype(jnp.bfloat16)
    rest = value - first.astype(jnp.float32)
    second = rest.astype(jnp.bfloat16)
    third = (rest - second.astype(jnp.float32)).astype(jnp.bfloat16)
    return first, second, third


def norm_rows(square, ones_first):
    first, second, third = (part.astype(jnp.float32) for part in three_parts(square))
    line = lax.broadcasted_iota(jnp.int32, (16, square.shape[1]), 0)
    at = line - 3 if ones_first else line
    rows = jnp.where(at == 0, first, jnp.where(at == 1, second, jnp.where(at == 2, third, 0.0)))
    ones = (line < 3) if ones_first else (line >= 3) & (line < 6)
    return jnp.where(ones, 1.0, rows).astype(jnp.bfloat16)


def column_stack(z):
    a, b, c = three_parts(z)
    square = jnp.sum(z * z, axis=0, keepdims=True)
    return jnp.concatenate([a, a, b, a, c, b, norm_rows(square, False)], axis=0)


def row_stack(z):
    a, b, c = three_parts(z * -2.0)
    square = jnp.sum(z * z, axis=0, keepdims=True)
    return jnp.concatenate([a, b, a, c, a, b, norm_rows(square, True)], axis=0)


def tile_of(total, most):
    size = most
    while size >= 128:
        if total % size == 0:
            return size
        size -= 128
    return total


def kernel(scale_ref, row_ref, col_ref, out_ref, row_feat, col_feat, vec_feat, both_acc, low_acc):
    nrow, feat, width = row_ref.shape
    ncol = col_ref.shape[0]
    nvec = col_ref.shape[1] - feat
    scale = jnp.sqrt(jnp.float32(5.0)) / scale_ref[...]
    row_z = jnp.concatenate([row_ref[k] for k in range(nrow)], axis=1) * scale
    row_feat[...] = row_stack(row_z)
    col_z = jnp.concatenate([col_ref[k, :feat] for k in range(ncol)], axis=1) * scale
    col_feat[...] = column_stack(col_z)
    vec = jnp.concatenate([col_ref[k, feat:] for k in range(ncol)], axis=1)
    vec_high = vec.astype(jnp.bfloat16)
    vec_low = (vec - vec_high.astype(jnp.float32)).astype(jnp.bfloat16)
    vec_feat[...] = jnp.concatenate([vec_high, vec_low], axis=0)
    rows, cols = nrow * width, ncol * width
    row_tile, col_tile = tile_of(rows, 640), tile_of(cols, 256)

    for row_at in range(0, rows, row_tile):
        here = pl.ds(row_at, row_tile)

        def add(number, carry):
            both, low = carry
            there = pl.ds(pl.multiple_of(number * col_tile, col_tile), col_tile)
            square = lax.dot_general(
                col_feat[:, there],
                row_feat[:, here],
                (((0,), (0,)), ((), ())),
                preferred_element_type=jnp.float32,
            )
            square = jnp.maximum(square, 1e-30)
            svalue = square * lax.rsqrt(square)
            value = (1.0 + svalue + square * (1.0 / 3.0)) * jnp.exp(-svalue)
            high = value.astype(jnp.bfloat16)
            rest = (value - high.astype(jnp.float32)).astype(jnp.bfloat16)
            both = both + jnp.dot(vec_feat[:, there], high, preferred_element_type=jnp.float32)
            low = low + jnp.dot(vec_feat[:nvec, there], rest, preferred_element_type=jnp.float32)
            return both, low

        both, low = lax.fori_loop(
            0,
            cols // col_tile,
            add,
            (jnp.zeros((2 * nvec, row_tile), jnp.float32), jnp.zeros((nvec, row_tile), jnp.float32)),
        )
        both_acc[:, here] = both
        low_acc[:, here] = low
    total = both_acc[:nvec, :] + both_acc[nvec:, :] + low_acc[...]
    for k in range(nrow):
        out_ref[k] = total[:, k * width : (k + 1) * width]


def per_device(points, vectors, lengthscales):
    nrow, ncol = lax.axis_size("far"), lax.axis_size("near")
    feat, width = points.shape
    nvec = vectors.shape[0]
    block = jnp.concatenate([points, vectors], axis=0)
    cols = lax.all_to_all(jnp.broadcast_to(block, (ncol,) + block.shape), "near", 0, 0)
    rows = lax.all_to_all(jnp.broadcast_to(points, (nrow,) + points.shape), "far", 0, 0)
    row_count, col_count = nrow * width, ncol * width
    parts = pl.pallas_call(
        kernel,
        out_shape=jax.ShapeDtypeStruct((nrow, nvec, width), jnp.float32),
        scratch_shapes=[
            pltpu.VMEM((112, row_count), jnp.bfloat16),
            pltpu.VMEM((112, col_count), jnp.bfloat16),
            pltpu.VMEM((2 * nvec, col_count), jnp.bfloat16),
            pltpu.VMEM((2 * nvec, row_count), jnp.float32),
            pltpu.VMEM((nvec, row_count), jnp.float32),
        ],
        compiler_params=pltpu.CompilerParams(vmem_limit_bytes=32 * 1024 * 1024),
    )(lengthscales[:, None], rows, cols)
    return jnp.sum(lax.all_to_all(parts, "far", 0, 0), axis=0)


def solution(mesh):
    blk, rep = mesh.shape["blk"], mesh.shape["rep"]
    low = split_blocks(blk, rep)
    grid = Mesh(mesh.devices.reshape(blk // low, low * rep), ("far", "near"))
    both = P(None, ("far", "near"))
    return jax.shard_map(
        per_device, mesh=grid, in_specs=(both, both, P()), out_specs=both, check_vma=False
    )
```

```python
import functools

import jax
import jax.numpy as jnp
from jax import lax
from jax.experimental import pallas as pl
from jax.experimental.pallas import tpu as pltpu
from jax.sharding import PartitionSpec as P

AXES = ("blk", "rep")


def split_blocks(blk):
    pair = 2 if blk % 2 == 0 else 1
    mid = max(d for d in range(1, blk // pair + 1) if (blk // pair) % d == 0 and d * d <= blk // pair)
    return blk // pair // mid, mid, pair


def partner(index, step, size):
    return index ^ step if size & (size - 1) == 0 else (index + step) % size


def permutation(sizes, axis, step):
    far, mid, pair, rep = sizes
    pairs = []
    for f in range(far):
        for m in range(mid):
            for p in range(pair):
                for q in range(rep):
                    sf, sm, sp, sq = f, m, p, q
                    if axis == "far":
                        sf = partner(f, step, far)
                    elif axis == "pair":
                        sp = partner(p, step, pair)
                    else:
                        sm, sq = divmod(partner(m * rep + q, step, mid * rep), rep)
                    source = ((sf * mid + sm) * pair + sp) * rep + sq
                    pairs.append((source, ((f * mid + m) * pair + p) * rep + q))
    return pairs


def three_parts(value):
    first = value.astype(jnp.bfloat16)
    rest = value - first.astype(jnp.float32)
    second = rest.astype(jnp.bfloat16)
    third = (rest - second.astype(jnp.float32)).astype(jnp.bfloat16)
    return first, second, third


def norm_rows(square, ones_first):
    first, second, third = (part.astype(jnp.float32) for part in three_parts(square))
    line = lax.broadcasted_iota(jnp.int32, (16, square.shape[1]), 0)
    at = line - 3 if ones_first else line
    rows = jnp.where(at == 0, first, jnp.where(at == 1, second, jnp.where(at == 2, third, 0.0)))
    ones = (line < 3) if ones_first else (line >= 3) & (line < 6)
    return jnp.where(ones, 1.0, rows).astype(jnp.bfloat16)


def column_stack(z):
    a, b, c = three_parts(z)
    square = jnp.sum(z * z, axis=0, keepdims=True)
    return jnp.concatenate([a, a, b, a, c, b, norm_rows(square, False)], axis=0)


def row_stack(z):
    a, b, c = three_parts(z * -2.0)
    square = jnp.sum(z * z, axis=0, keepdims=True)
    return jnp.concatenate([a, b, a, c, a, b, norm_rows(square, True)], axis=0)


def tile_of(total, most):
    size = most
    while size >= 128:
        if total % size == 0:
            return size
        size -= 128
    return total


def kernel(nrow, ncol, *refs):
    scale_ref = refs[0]
    row_refs = refs[1 : 1 + nrow]
    col_refs = refs[1 + nrow : 1 + nrow + ncol]
    out_refs = refs[1 + nrow + ncol : 1 + 2 * nrow + ncol]
    row_feat, col_feat, vec_feat, both_acc, low_acc = refs[1 + 2 * nrow + ncol :]
    feat, width = row_refs[0].shape
    nvec = col_refs[0].shape[0] - feat
    scale = jnp.sqrt(jnp.float32(5.0)) / scale_ref[...]
    row_z = jnp.concatenate([ref[...] for ref in row_refs], axis=1) * scale
    row_feat[...] = row_stack(row_z)
    col_z = jnp.concatenate([ref[:feat, :] for ref in col_refs], axis=1) * scale
    col_feat[...] = column_stack(col_z)
    vec = jnp.concatenate([ref[feat:, :] for ref in col_refs], axis=1)
    vec_high = vec.astype(jnp.bfloat16)
    vec_low = (vec - vec_high.astype(jnp.float32)).astype(jnp.bfloat16)
    vec_feat[...] = jnp.concatenate([vec_high, vec_low], axis=0)
    rows, cols = nrow * width, ncol * width
    row_tile, col_tile = tile_of(rows, 640), tile_of(cols, 256)

    for row_at in range(0, rows, row_tile):
        here = pl.ds(row_at, row_tile)

        def add(number, carry):
            both, low = carry
            there = pl.ds(pl.multiple_of(number * col_tile, col_tile), col_tile)
            square = lax.dot_general(
                col_feat[:, there],
                row_feat[:, here],
                (((0,), (0,)), ((), ())),
                preferred_element_type=jnp.float32,
            )
            square = jnp.maximum(square, 1e-30)
            svalue = square * lax.rsqrt(square)
            value = (1.0 + svalue + square * (1.0 / 3.0)) * jnp.exp(-svalue)
            high = value.astype(jnp.bfloat16)
            rest = (value - high.astype(jnp.float32)).astype(jnp.bfloat16)
            both = both + jnp.dot(vec_feat[:, there], high, preferred_element_type=jnp.float32)
            low = low + jnp.dot(vec_feat[:nvec, there], rest, preferred_element_type=jnp.float32)
            return both, low

        both, low = lax.fori_loop(
            0,
            cols // col_tile,
            add,
            (jnp.zeros((2 * nvec, row_tile), jnp.float32), jnp.zeros((nvec, row_tile), jnp.float32)),
        )
        both_acc[:, here] = both
        low_acc[:, here] = low
    total = both_acc[:nvec, :] + both_acc[nvec:, :] + low_acc[...]
    for number, ref in enumerate(out_refs):
        ref[...] = total[:, number * width : (number + 1) * width]


def per_device(sizes, points, vectors, lengthscales):
    far, mid, pair, rep = sizes
    nrow, ncol = mid * rep, far * pair
    width, nvec = points.shape[1], vectors.shape[0]
    row_p = [points] + [lax.ppermute(points, AXES, permutation(sizes, "mid", k)) for k in range(1, nrow)]
    block = jnp.concatenate([points, vectors], axis=0)
    line = [block] + [lax.ppermute(block, AXES, permutation(sizes, "far", k)) for k in range(1, far)]
    cols = list(line)
    for k in range(1, pair):
        cols += [lax.ppermute(item, AXES, permutation(sizes, "pair", k)) for item in line]
    row_count, col_count = nrow * width, ncol * width
    parts = pl.pallas_call(
        functools.partial(kernel, nrow, ncol),
        out_shape=[jax.ShapeDtypeStruct((nvec, width), jnp.float32)] * nrow,
        scratch_shapes=[
            pltpu.VMEM((112, row_count), jnp.bfloat16),
            pltpu.VMEM((112, col_count), jnp.bfloat16),
            pltpu.VMEM((2 * nvec, col_count), jnp.bfloat16),
            pltpu.VMEM((2 * nvec, row_count), jnp.float32),
            pltpu.VMEM((nvec, row_count), jnp.float32),
        ],
        compiler_params=pltpu.CompilerParams(vmem_limit_bytes=32 * 1024 * 1024),
    )(lengthscales[:, None], *row_p, *cols)
    total = parts[0]
    for k in range(1, nrow):
        back = [(target, source) for source, target in permutation(sizes, "mid", k)]
        total = total + lax.ppermute(parts[k], AXES, back)
    return total


def solution(mesh):
    sizes = split_blocks(mesh.shape["blk"]) + (mesh.shape["rep"],)
    return jax.shard_map(
        functools.partial(per_device, sizes),
        mesh=mesh,
        in_specs=(P(None, AXES), P(None, AXES), P()),
        out_specs=P(None, AXES),
        check_vma=False,
    )
```

```python
import functools

import jax
import jax.numpy as jnp
from jax import lax
from jax.experimental import pallas as pl
from jax.experimental.pallas import tpu as pltpu
from jax.sharding import PartitionSpec as P

AXES = ("blk", "rep")


def split_blocks(blk):
    pair = 2 if blk % 2 == 0 else 1
    mid = max(d for d in range(1, blk // pair + 1) if (blk // pair) % d == 0 and d * d <= blk // pair)
    return blk // pair // mid, mid, pair


def partner(index, step, size):
    return index ^ step if size & (size - 1) == 0 else (index + step) % size


def permutation(sizes, axis, step):
    far, mid, pair, rep = sizes
    pairs = []
    for f in range(far):
        for m in range(mid):
            for p in range(pair):
                for q in range(rep):
                    sf, sm, sp, sq = f, m, p, q
                    if axis == "far":
                        sf = partner(f, step, far)
                    elif axis == "pair":
                        sp = partner(p, step, pair)
                    else:
                        sm, sq = divmod(partner(m * rep + q, step, mid * rep), rep)
                    source = ((sf * mid + sm) * pair + sp) * rep + sq
                    pairs.append((source, ((f * mid + m) * pair + p) * rep + q))
    return pairs


def three_parts(value):
    first = value.astype(jnp.bfloat16)
    rest = value - first.astype(jnp.float32)
    second = rest.astype(jnp.bfloat16)
    third = (rest - second.astype(jnp.float32)).astype(jnp.bfloat16)
    return first, second, third


def norm_rows(square, ones_first):
    first, second, third = (part.astype(jnp.float32) for part in three_parts(square))
    line = lax.broadcasted_iota(jnp.int32, (16, square.shape[1]), 0)
    at = line - 3 if ones_first else line
    rows = jnp.where(at == 0, first, jnp.where(at == 1, second, jnp.where(at == 2, third, 0.0)))
    ones = (line < 3) if ones_first else (line >= 3) & (line < 6)
    return jnp.where(ones, 1.0, rows).astype(jnp.bfloat16)


def column_stack(z):
    a, b, c = three_parts(z)
    square = jnp.sum(z * z, axis=0, keepdims=True)
    return jnp.concatenate([a, a, b, a, c, b, norm_rows(square, False)], axis=0)


def row_stack(z):
    a, b, c = three_parts(z * -2.0)
    square = jnp.sum(z * z, axis=0, keepdims=True)
    return jnp.concatenate([a, b, a, c, a, b, norm_rows(square, True)], axis=0)


def tile_of(total, most):
    size = most
    while size >= 128:
        if total % size == 0:
            return size
        size -= 128
    return total


def packed_pieces(count, width):
    rest = width % 128
    return 128 // rest if width > 128 and rest and 128 % rest == 0 and count % 8 == 0 else 0


def pack_kernel(points_ref, vectors_ref, out_ref):
    block = jnp.concatenate([points_ref[...], vectors_ref[...]], axis=0)
    count, width = block.shape
    fit = packed_pieces(count, width)
    if not fit:
        out_ref[...] = block
        return
    main = width // 128 * 128
    for at in range(0, main, 128):
        out_ref[at // 128 * count : (at // 128 + 1) * count, :] = block[:, at : at + 128]
    base = main // 128 * count
    pieces = [block[at : at + 8, main:] for at in range(0, count, 8)]
    for first in range(0, len(pieces), fit):
        line = pieces[first : first + fit]
        line += [jnp.zeros_like(line[0])] * (fit - len(line))
        out_ref[base + first // fit * 8 : base + first // fit * 8 + 8, :] = jnp.concatenate(line, axis=1)


def packed_shape(count, width):
    fit = packed_pieces(count, width)
    if not fit:
        return count, width
    return width // 128 * count + -(-(count // 8) // fit) * 8, 128


def line_kernel(count, width, *refs):
    block_refs, out_ref = refs[:-1], refs[-1]
    fit = packed_pieces(count, width)
    if not fit:
        out_ref[...] = jnp.concatenate([ref[...] for ref in block_refs], axis=1)
        return
    full, rest = width // 128, width % 128
    mains, rests = [], []
    for ref in block_refs:
        mains += [ref[k * count : (k + 1) * count, :] for k in range(full)]
        pieces = []
        for k in range(count // 8):
            at = full * count + k // fit * 8
            pieces.append(ref[at : at + 8, k % fit * rest : (k % fit + 1) * rest])
        rests.append(jnp.concatenate(pieces, axis=0))
    out_ref[...] = jnp.concatenate(mains + rests, axis=1)


def product_kernel(has_total, last, *refs):
    scale_ref, points_ref = refs[:2]
    line_refs = refs[2 + has_total : -4]
    out_ref, col_feat, vec_feat, row_feat = refs[-4:]
    feat, width = points_ref.shape
    nvec = line_refs[0].shape[0] - feat
    scale = jnp.sqrt(jnp.float32(5.0)) / scale_ref[...]
    row_feat[...] = row_stack(points_ref[...] * scale)
    begin = 0
    for ref in line_refs:
        there = pl.ds(begin, ref.shape[1])
        col_feat[:, there] = column_stack(ref[:feat, :] * scale)
        vec = ref[feat:, :]
        vec_high = vec.astype(jnp.bfloat16)
        vec_feat[:nvec, there] = vec_high
        vec_feat[nvec:, there] = (vec - vec_high.astype(jnp.float32)).astype(jnp.bfloat16)
        begin += ref.shape[1]
    tile = tile_of(begin, 384)

    def add(number, carry):
        both, low = carry
        there = pl.ds(pl.multiple_of(number * tile, tile), tile)
        square = lax.dot_general(
            row_feat[...],
            col_feat[:, there],
            (((0,), (0,)), ((), ())),
            preferred_element_type=jnp.float32,
        )
        square = jnp.maximum(square, 1e-30)
        svalue = square * lax.rsqrt(square)
        value = (1.0 + svalue + square * (1.0 / 3.0)) * jnp.exp(-svalue)
        high = value.astype(jnp.bfloat16)
        rest = (value - high.astype(jnp.float32)).astype(jnp.bfloat16)
        vec = vec_feat[:, there]
        across = (((1,), (1,)), ((), ()))
        both = both + lax.dot_general(high, vec, across, preferred_element_type=jnp.float32)
        low = low + lax.dot_general(rest, vec[:nvec], across, preferred_element_type=jnp.float32)
        return both, low

    count = begin // tile
    zeros = jnp.zeros((width, 2 * nvec), jnp.float32), jnp.zeros((width, nvec), jnp.float32)
    both, low = lax.fori_loop(0, count, add, zeros, unroll=count <= 8)
    total = both[:, :nvec] + both[:, nvec:] + low
    if has_total:
        total = total + refs[2][...]
    out_ref[...] = total.T if last else total


def product(scale, points, total, lines, last):
    nvec, width = lines[0].shape[0] - points.shape[0], points.shape[1]
    cols = sum(line.shape[1] for line in lines)
    shape = (nvec, width) if last else (width, nvec)
    before = [] if total is None else [total]
    return pl.pallas_call(
        functools.partial(product_kernel, len(before), last),
        out_shape=jax.ShapeDtypeStruct(shape, jnp.float32),
        scratch_shapes=[
            pltpu.VMEM((112, cols), jnp.bfloat16),
            pltpu.VMEM((2 * nvec, cols), jnp.bfloat16),
            pltpu.VMEM((112, width), jnp.bfloat16),
        ],
        compiler_params=pltpu.CompilerParams(vmem_limit_bytes=8 * 1024 * 1024 + 2048 * cols),
        cost_estimate=pl.CostEstimate(
            flops=2 * width * cols * 256, bytes_accessed=cols * 192, transcendentals=2 * width * cols
        ),
    )(scale, points, *before, *lines)


def per_device(sizes, points, vectors, lengthscales):
    far, mid, pair, rep = sizes
    width, count = points.shape[1], points.shape[0] + vectors.shape[0]
    block = pl.pallas_call(
        pack_kernel, out_shape=jax.ShapeDtypeStruct(packed_shape(count, width), jnp.float32)
    )(points, vectors)
    blocks = [block] + [lax.ppermute(block, AXES, permutation(sizes, "far", k)) for k in range(1, far)]
    line = pl.pallas_call(
        functools.partial(line_kernel, count, width),
        out_shape=jax.ShapeDtypeStruct((count, far * width), jnp.float32),
    )(*blocks)

    def to_pair(item):
        return [lax.ppermute(item, AXES, permutation(sizes, "pair", k)) for k in range(1, pair)]

    plane = [lax.ppermute(line, AXES, permutation(sizes, "mid", k)) for k in reversed(range(1, mid * rep))]
    scale = lengthscales[:, None]
    total = product(scale, points, None, [line] + to_pair(line), not plane)
    if plane:
        others = [other for item in plane for other in to_pair(item)]
        total = product(scale, points, total, plane, not others)
        if others:
            total = product(scale, points, total, others, True)
    return total


def solution(mesh):
    sizes = split_blocks(mesh.shape["blk"]) + (mesh.shape["rep"],)
    return jax.shard_map(
        functools.partial(per_device, sizes),
        mesh=mesh,
        in_specs=(P(None, AXES), P(None, AXES), P()),
        out_specs=P(None, AXES),
        check_vma=False,
    )
```

```python
import functools

import jax
import jax.numpy as jnp
from jax import lax
from jax.experimental import pallas as pl
from jax.experimental.pallas import tpu as pltpu
from jax.sharding import PartitionSpec as P

AXES = ("blk", "rep")


def split_blocks(blk):
    pair = 2 if blk % 2 == 0 else 1
    mid = max(d for d in range(1, blk // pair + 1) if (blk // pair) % d == 0 and d * d <= blk // pair)
    return blk // pair // mid, mid, pair


def partner(index, step, size):
    return index ^ step if size & (size - 1) == 0 else (index + step) % size


def permutation(sizes, axis, step):
    far, mid, pair, rep = sizes
    pairs = []
    for f in range(far):
        for m in range(mid):
            for p in range(pair):
                for q in range(rep):
                    sf, sm, sp, sq = f, m, p, q
                    if axis == "far":
                        sf = partner(f, step, far)
                    elif axis == "pair":
                        sp = partner(p, step, pair)
                    else:
                        sm, sq = divmod(partner(m * rep + q, step, mid * rep), rep)
                    source = ((sf * mid + sm) * pair + sp) * rep + sq
                    pairs.append((source, ((f * mid + m) * pair + p) * rep + q))
    return pairs


def three_parts(value):
    first = value.astype(jnp.bfloat16)
    rest = value - first.astype(jnp.float32)
    second = rest.astype(jnp.bfloat16)
    third = (rest - second.astype(jnp.float32)).astype(jnp.bfloat16)
    return first, second, third


def norm_rows(square, ones_first):
    first, second, third = (part.astype(jnp.float32) for part in three_parts(square))
    line = lax.broadcasted_iota(jnp.int32, (16, square.shape[1]), 0)
    at = line - 3 if ones_first else line
    rows = jnp.where(at == 0, first, jnp.where(at == 1, second, jnp.where(at == 2, third, 0.0)))
    ones = (line < 3) if ones_first else (line >= 3) & (line < 6)
    return jnp.where(ones, 1.0, rows).astype(jnp.bfloat16)


def column_stack(z):
    a, b, c = three_parts(z)
    square = jnp.sum(z * z, axis=0, keepdims=True)
    return jnp.concatenate([a, a, b, a, c, b, norm_rows(square, False)], axis=0)


def row_stack(z):
    a, b, c = three_parts(z * -2.0)
    square = jnp.sum(z * z, axis=0, keepdims=True)
    return jnp.concatenate([a, b, a, c, a, b, norm_rows(square, True)], axis=0)


def tile_of(total, most):
    size = most
    while size >= 128:
        if total % size == 0:
            return size
        size -= 128
    return total


def packed_pieces(count, width):
    rest = width % 128
    return 128 // rest if width > 128 and rest and 128 % rest == 0 and count % 8 == 0 else 0


def pack_kernel(points_ref, vectors_ref, out_ref):
    block = jnp.concatenate([points_ref[...], vectors_ref[...]], axis=0)
    count, width = block.shape
    fit = packed_pieces(count, width)
    if not fit:
        out_ref[...] = block
        return
    main = width // 128 * 128
    for at in range(0, main, 128):
        out_ref[at // 128 * count : (at // 128 + 1) * count, :] = block[:, at : at + 128]
    base = main // 128 * count
    pieces = [block[at : at + 8, main:] for at in range(0, count, 8)]
    for first in range(0, len(pieces), fit):
        line = pieces[first : first + fit]
        line += [jnp.zeros_like(line[0])] * (fit - len(line))
        out_ref[base + first // fit * 8 : base + first // fit * 8 + 8, :] = jnp.concatenate(line, axis=1)


def packed_shape(count, width):
    fit = packed_pieces(count, width)
    if not fit:
        return count, width
    return width // 128 * count + -(-(count // 8) // fit) * 8, 128


def line_kernel(count, width, *refs):
    block_refs, out_ref = refs[:-1], refs[-1]
    fit = packed_pieces(count, width)
    if not fit:
        out_ref[...] = jnp.concatenate([ref[...] for ref in block_refs], axis=1)
        return
    full, rest = width // 128, width % 128
    mains, rests = [], []
    for ref in block_refs:
        mains += [ref[k * count : (k + 1) * count, :] for k in range(full)]
        pieces = []
        for k in range(count // 8):
            at = full * count + k // fit * 8
            pieces.append(ref[at : at + 8, k % fit * rest : (k % fit + 1) * rest])
        rests.append(jnp.concatenate(pieces, axis=0))
    out_ref[...] = jnp.concatenate(mains + rests, axis=1)


def product_kernel(has_total, last, *refs):
    scale_ref, points_ref = refs[:2]
    line_refs = refs[2 + has_total : -4]
    out_ref, col_feat, vec_feat, row_feat = refs[-4:]
    feat, width = points_ref.shape
    nvec = line_refs[0].shape[0] - feat
    scale = jnp.sqrt(jnp.float32(5.0)) / scale_ref[...]
    row_feat[...] = row_stack(points_ref[...] * scale)
    begin = 0
    for ref in line_refs:
        there = pl.ds(begin, ref.shape[1])
        col_feat[:, there] = column_stack(ref[:feat, :] * scale)
        vec = ref[feat:, :]
        vec_high = vec.astype(jnp.bfloat16)
        vec_feat[:nvec, there] = vec_high
        vec_feat[nvec:, there] = (vec - vec_high.astype(jnp.float32)).astype(jnp.bfloat16)
        begin += ref.shape[1]
    tile = tile_of(begin, 384)

    def add(number, carry):
        both, low = carry
        there = pl.ds(pl.multiple_of(number * tile, tile), tile)
        square = lax.dot_general(
            row_feat[...],
            col_feat[:, there],
            (((0,), (0,)), ((), ())),
            preferred_element_type=jnp.float32,
        )
        square = jnp.maximum(square, 1e-30)
        svalue = square * lax.rsqrt(square)
        value = (1.0 + svalue + square * (1.0 / 3.0)) * jnp.exp(-svalue)
        high = value.astype(jnp.bfloat16)
        rest = (value - high.astype(jnp.float32)).astype(jnp.bfloat16)
        vec = vec_feat[:, there]
        across = (((1,), (1,)), ((), ()))
        both = both + lax.dot_general(high, vec, across, preferred_element_type=jnp.float32)
        low = low + lax.dot_general(rest, vec[:nvec], across, preferred_element_type=jnp.float32)
        return both, low

    count = begin // tile
    zeros = jnp.zeros((width, 2 * nvec), jnp.float32), jnp.zeros((width, nvec), jnp.float32)
    both, low = lax.fori_loop(0, count, add, zeros, unroll=count <= 8)
    total = both[:, :nvec] + both[:, nvec:] + low
    if has_total:
        total = total + refs[2][...]
    out_ref[...] = total.T if last else total


def product(scale, points, total, lines, last):
    nvec, width = lines[0].shape[0] - points.shape[0], points.shape[1]
    cols = sum(line.shape[1] for line in lines)
    shape = (nvec, width) if last else (width, nvec)
    before = [] if total is None else [total]
    return pl.pallas_call(
        functools.partial(product_kernel, len(before), last),
        out_shape=jax.ShapeDtypeStruct(shape, jnp.float32),
        scratch_shapes=[
            pltpu.VMEM((112, cols), jnp.bfloat16),
            pltpu.VMEM((2 * nvec, cols), jnp.bfloat16),
            pltpu.VMEM((112, width), jnp.bfloat16),
        ],
        compiler_params=pltpu.CompilerParams(vmem_limit_bytes=8 * 1024 * 1024 + 2048 * cols),
        cost_estimate=pl.CostEstimate(
            flops=2 * width * cols * 256, bytes_accessed=cols * 192, transcendentals=2 * width * cols
        ),
    )(scale, points, *before, *lines)


def per_device(sizes, points, vectors, lengthscales):
    far, mid, pair, rep = sizes
    width, count = points.shape[1], points.shape[0] + vectors.shape[0]
    block = pl.pallas_call(
        pack_kernel,
        out_shape=jax.ShapeDtypeStruct(packed_shape(count, width), jnp.float32),
        compiler_params=pltpu.CompilerParams(vmem_limit_bytes=2 * 1024 * 1024),
    )(points, vectors)
    blocks = [block] + [lax.ppermute(block, AXES, permutation(sizes, "far", k)) for k in reversed(range(1, far))]
    line = pl.pallas_call(
        functools.partial(line_kernel, count, width),
        out_shape=jax.ShapeDtypeStruct((count, far * width), jnp.float32),
        compiler_params=pltpu.CompilerParams(vmem_limit_bytes=2 * 1024 * 1024 + 16 * count * far * width),
    )(*blocks)

    def to_pair(item):
        return [lax.ppermute(item, AXES, permutation(sizes, "pair", k)) for k in range(1, pair)]

    plane = [lax.ppermute(line, AXES, permutation(sizes, "mid", k)) for k in reversed(range(1, mid * rep))]
    scale = lengthscales[:, None]
    total = product(scale, points, None, [line] + to_pair(line), not plane)
    if plane:
        total, *plane = lax.optimization_barrier((total, *plane))
        others = [other for item in plane for other in to_pair(item)]
        total = product(scale, points, total, plane, not others)
        if others:
            total = product(scale, points, total, others, True)
    return total


def solution(mesh):
    sizes = split_blocks(mesh.shape["blk"]) + (mesh.shape["rep"],)
    return jax.shard_map(
        functools.partial(per_device, sizes),
        mesh=mesh,
        in_specs=(P(None, AXES), P(None, AXES), P()),
        out_specs=P(None, AXES),
        check_vma=False,
    )
```

```python
import functools

import jax
import jax.numpy as jnp
from jax import lax
from jax.experimental import pallas as pl
from jax.experimental.pallas import tpu as pltpu
from jax.sharding import PartitionSpec as P

AXES = ("blk", "rep")
LANES = 128
STACK = 128
MIB = 1024 * 1024


def split_blocks(blk, rep):
    pair = 2 if blk % 2 == 0 else 1
    mid = max(d for d in range(1, blk // pair + 1) if (blk // pair) % d == 0 and d * d <= blk // pair)
    line = blk // pair // mid
    near = 2 if line % 2 == 0 else 1
    return line // near, near, mid, pair, rep


def partner(index, step, size):
    return index ^ step if size & (size - 1) == 0 else (index + step) % size


def permutation(sizes, axis, step):
    far, near, mid, pair, rep = sizes
    pairs = []
    for target in range(far * near * mid * pair * rep):
        rest, q = divmod(target, rep)
        rest, p = divmod(rest, pair)
        rest, m = divmod(rest, mid)
        f, n = divmod(rest, near)
        if axis == "far":
            f = partner(f, step, far)
        elif axis == "near":
            n = partner(n, step, near)
        elif axis == "pair":
            p = partner(p, step, pair)
        else:
            m, q = divmod(partner(m * rep + q, step, mid * rep), rep)
        pairs.append(((((f * near + n) * mid + m) * pair + p) * rep + q, target))
    return pairs


def three_parts(value):
    first = value.astype(jnp.bfloat16).astype(jnp.float32)
    second = (value - first).astype(jnp.bfloat16).astype(jnp.float32)
    return first, second, value - first - second


def norm_rows(square, ones_first, count):
    first, second, third = three_parts(square)
    line = lax.broadcasted_iota(jnp.int32, (count, square.shape[1]), 0)
    at = line - 3 if ones_first else line
    rows = jnp.where(at == 0, first, jnp.where(at == 1, second, jnp.where(at == 2, third, 0.0)))
    ones = (line < 3) if ones_first else (line >= 3) & (line < 6)
    return jnp.where(ones, 1.0, rows)


def column_stack(z):
    a, b, c = three_parts(z)
    square = jnp.sum(z * z, axis=0, keepdims=True)
    return jnp.concatenate([a, a, b, a, c, b, norm_rows(square, False, STACK - 6 * z.shape[0])], axis=0)


def row_stack(z):
    a, b, c = three_parts(z * -2.0)
    square = jnp.sum(z * z, axis=0, keepdims=True)
    return jnp.concatenate([a, b, a, c, a, b, norm_rows(square, True, STACK - 6 * z.shape[0])], axis=0)


def packed_pieces(count, width):
    rest = width % LANES
    return LANES // rest if width > LANES and rest and LANES % rest == 0 and count % 8 == 0 else 0


def packed_shape(count, width):
    fit = packed_pieces(count, width)
    if not fit:
        return count, width
    return width // LANES * count + -(-(count // 8) // fit) * 8, LANES


def pack_kernel(block_ref, out_ref):
    count, width = block_ref.shape
    block = block_ref[...]
    fit = packed_pieces(count, width)
    if not fit:
        out_ref[...] = block
        return
    main = width // LANES * LANES
    for at in range(0, main, LANES):
        out_ref[at // LANES * count : (at // LANES + 1) * count, :] = block[:, at : at + LANES]
    base = main // LANES * count
    pieces = [block[at : at + 8, main:] for at in range(0, count, 8)]
    for first in range(0, len(pieces), fit):
        line = pieces[first : first + fit]
        line += [jnp.zeros_like(line[0])] * (fit - len(line))
        out_ref[base + first // fit * 8 : base + first // fit * 8 + 8, :] = jnp.concatenate(line, axis=1)


def stack_kernel(*refs):
    begin = 0
    for ref in refs[:-1]:
        refs[-1][begin : begin + ref.shape[0], :] = ref[...]
        begin += ref.shape[0]


def unpacked(count, width, refs):
    fit = packed_pieces(count, width)
    high = packed_shape(count, width)[0]
    full, rest = width // LANES, width % LANES
    mains, rests = [], []
    for ref in refs:
        for base in range(0, ref.shape[0], high):
            if not fit:
                rests.append(ref[base : base + high, :])
                continue
            mains += [ref[base + k * count : base + (k + 1) * count, :] for k in range(full)]
            pieces = []
            for k in range(count // 8):
                at = base + full * count + k // fit * 8
                pieces.append(ref[at : at + 8, k % fit * rest : (k % fit + 1) * rest])
            rests.append(jnp.concatenate(pieces, axis=0))
    over = -sum(item.shape[1] for item in rests) % LANES
    if over:
        rests.append(jnp.zeros((count, over), jnp.float32))
    return jnp.concatenate(mains + rests, axis=1)


def columns_of(count, width, lines):
    blocks = sum(line.shape[0] for line in lines) // packed_shape(count, width)[0]
    return -(-blocks * width // LANES) * LANES


def tile_of(total, most):
    size = most
    while size > LANES:
        if total % size == 0:
            return size
        size -= LANES
    return size


def add_columns(width, scale, row_feat, line_refs, col_feat, high_feat, low_feat):
    feat = scale.shape[0]
    nvec = high_feat.shape[0] // 2
    block = unpacked(feat + nvec, width, line_refs)
    cols = block.shape[1]
    z = block[:feat] * jnp.concatenate([scale] * (cols // LANES), axis=1)
    col_feat[...] = column_stack(z).astype(jnp.bfloat16)
    vec = block[feat:]
    vec_high = vec.astype(jnp.bfloat16)
    high_feat[:nvec, :] = vec_high
    high_feat[nvec:, :] = (vec - vec_high.astype(jnp.float32)).astype(jnp.bfloat16)
    low_feat[:nvec, :] = vec_high
    low_feat[nvec:, :] = jnp.zeros_like(vec_high)
    tile = tile_of(cols, 256)

    def add(number, total):
        there = pl.ds(pl.multiple_of(number * tile, tile), tile)
        square = jnp.dot(row_feat, col_feat[:, there], preferred_element_type=jnp.float32)
        square = jnp.maximum(square, 1e-30)
        svalue = square * lax.rsqrt(square)
        value = (1.0 + svalue + square * (1.0 / 3.0)) * jnp.exp(-svalue)
        high = value.astype(jnp.bfloat16)
        low = (value - high.astype(jnp.float32)).astype(jnp.bfloat16)
        across = (((1,), (1,)), ((), ()))
        total = total + lax.dot_general(high, high_feat[:, there], across, preferred_element_type=jnp.float32)
        return total + lax.dot_general(low, low_feat[:, there], across, preferred_element_type=jnp.float32)

    count = cols // tile
    zeros = jnp.zeros((row_feat.shape[0], 2 * nvec), jnp.float32)
    return lax.fori_loop(0, count, add, zeros, unroll=count <= 8)


def first_kernel(nrow, *refs):
    scale_ref, row_refs, line_refs = refs[0], refs[1 : 1 + nrow], refs[1 + nrow : -6]
    total_ref, feat_ref, scale_out, col_feat, high_feat, low_feat = refs[-6:]
    feat, width = row_refs[0].shape
    scale = jnp.broadcast_to(jnp.sqrt(jnp.float32(5.0)) / scale_ref[...], (feat, LANES))
    scale_out[...] = scale
    for k, ref in enumerate(row_refs):
        z = ref[...] * scale[:, :1]
        feat_ref[k * width : (k + 1) * width, :] = row_stack(z).T.astype(jnp.bfloat16)
    total_ref[...] = add_columns(width, scale, feat_ref[...], line_refs, col_feat, high_feat, low_feat)


def next_kernel(width, nout, *refs):
    scale_ref, feat_ref, before_ref = refs[:3]
    line_refs, out_refs = refs[3 : -3 - nout], refs[-3 - nout : -3]
    total = before_ref[...] + add_columns(width, scale_ref[...], feat_ref[...], line_refs, *refs[-3:])
    if out_refs[0].shape == total.shape:
        out_refs[0][...] = total
        return
    nvec = total.shape[1] // 2
    for k, ref in enumerate(out_refs):
        part = total[k * width : (k + 1) * width].T
        ref[...] = part[:nvec] + part[nvec:]


def scratch(nvec, cols):
    return [
        pltpu.VMEM((STACK, cols), jnp.bfloat16),
        pltpu.VMEM((2 * nvec, cols), jnp.bfloat16),
        pltpu.VMEM((2 * nvec, cols), jnp.bfloat16),
    ]


def limits(rows, cols):
    return {
        "compiler_params": pltpu.CompilerParams(vmem_limit_bytes=4 * MIB + 4096 * rows + 2048 * cols),
        "cost_estimate": pl.CostEstimate(
            flops=2 * rows * cols * 256, bytes_accessed=cols * 192, transcendentals=2 * rows * cols
        ),
    }


def per_device(sizes, points, vectors, lengthscales):
    far, near, mid, pair, rep = sizes
    (feat, width), nvec = points.shape, vectors.shape[0]
    count, rows = feat + nvec, near * width
    packed = packed_shape(count, width)
    block = pl.pallas_call(
        pack_kernel,
        out_shape=jax.ShapeDtypeStruct(packed, jnp.float32),
        compiler_params=pltpu.CompilerParams(vmem_limit_bytes=2 * MIB),
    )(jnp.concatenate([points, vectors], axis=0))
    blocks = [lax.ppermute(block, AXES, permutation(sizes, "far", k)) for k in reversed(range(1, far))]
    later_points, block = lax.optimization_barrier((points, block))
    row_points = [points]
    row_points += [lax.ppermute(later_points, AXES, permutation(sizes, "near", k)) for k in range(1, near)]
    blocks, row_points = lax.optimization_barrier((blocks, row_points))
    line = pl.pallas_call(
        stack_kernel,
        out_shape=jax.ShapeDtypeStruct((far * packed[0], packed[1]), jnp.float32),
        compiler_params=pltpu.CompilerParams(vmem_limit_bytes=2 * MIB + 16 * far * packed[0] * packed[1]),
    )(block, *blocks)

    def to_pair(item):
        return [lax.ppermute(item, AXES, permutation(sizes, "pair", k)) for k in range(1, pair)]

    plane = [lax.ppermute(line, AXES, permutation(sizes, "mid", k)) for k in reversed(range(1, mid * rep))]
    lines = [line] + to_pair(line)
    cols = columns_of(count, width, lines)
    total, row_feat, scale = pl.pallas_call(
        functools.partial(first_kernel, near),
        out_shape=[
            jax.ShapeDtypeStruct((rows, 2 * nvec), jnp.float32),
            jax.ShapeDtypeStruct((rows, STACK), jnp.bfloat16),
            jax.ShapeDtypeStruct((feat, LANES), jnp.float32),
        ],
        scratch_shapes=scratch(nvec, cols),
        **limits(rows, cols),
    )(lengthscales[:, None], *row_points, *lines)

    def more(total, lines, out_shape):
        cols = columns_of(count, width, lines)
        return pl.pallas_call(
            functools.partial(next_kernel, width, len(out_shape)),
            out_shape=[jax.ShapeDtypeStruct(shape, jnp.float32) for shape in out_shape],
            scratch_shapes=scratch(nvec, cols),
            **limits(rows, cols),
        )(scale, row_feat, total, *lines)

    total, *plane = lax.optimization_barrier((total, *plane))
    others = [other for item in plane for other in to_pair(item)]
    (total,) = more(total, plane, [(rows, 2 * nvec)])
    parts = more(total, others, [(nvec, width)] * near)
    result = parts[0]
    for k in range(1, near):
        back = [(target, source) for source, target in permutation(sizes, "near", k)]
        result = result + lax.ppermute(parts[k], AXES, back)
    return result


def solution(mesh):
    sizes = split_blocks(mesh.shape["blk"], mesh.shape["rep"])
    return jax.shard_map(
        functools.partial(per_device, sizes),
        mesh=mesh,
        in_specs=(P(None, AXES), P(None, AXES), P()),
        out_specs=P(None, AXES),
        check_vma=False,
    )
```

```python
import functools

import jax
import jax.numpy as jnp
from jax import lax
from jax.experimental import pallas as pl
from jax.experimental.pallas import tpu as pltpu
from jax.sharding import PartitionSpec as P

AXES = ("blk", "rep")
LANES = 128
STACK = 128
MIB = 1024 * 1024


def split_blocks(blk, rep):
    pair = 2 if blk % 2 == 0 else 1
    line = blk // pair
    mid = max(d for d in range(1, line + 1) if line % d == 0 and d * d <= line)
    return line // mid, mid, pair, rep


def partner(index, step, size):
    return index ^ step if size & (size - 1) == 0 else (index + step) % size


def permutation(sizes, axis, step):
    far, mid, pair, rep = sizes
    pairs = []
    for target in range(far * mid * pair * rep):
        rest, q = divmod(target, rep)
        rest, p = divmod(rest, pair)
        f, m = divmod(rest, mid)
        if axis == "far":
            f = partner(f, step, far)
        elif axis == "pair":
            p = partner(p, step, pair)
        else:
            m, q = divmod(partner(m * rep + q, step, mid * rep), rep)
        pairs.append((((f * mid + m) * pair + p) * rep + q, target))
    return pairs


def three_parts(value):
    first = value.astype(jnp.bfloat16).astype(jnp.float32)
    second = (value - first).astype(jnp.bfloat16).astype(jnp.float32)
    return first, second, value - first - second


def norm_rows(square, ones_first, count):
    first, second, third = three_parts(square)
    line = lax.broadcasted_iota(jnp.int32, (count, square.shape[1]), 0)
    at = line - 3 if ones_first else line
    rows = jnp.where(at == 0, first, jnp.where(at == 1, second, jnp.where(at == 2, third, 0.0)))
    ones = (line < 3) if ones_first else (line >= 3) & (line < 6)
    return jnp.where(ones, 1.0, rows)


def column_stack(z):
    a, b, c = three_parts(z)
    square = jnp.sum(z * z, axis=0, keepdims=True)
    return jnp.concatenate([a, a, b, a, c, b, norm_rows(square, False, STACK - 6 * z.shape[0])], axis=0)


def row_stack(z):
    a, b, c = three_parts(z * -2.0)
    square = jnp.sum(z * z, axis=0, keepdims=True)
    return jnp.concatenate([a, b, a, c, a, b, norm_rows(square, True, STACK - 6 * z.shape[0])], axis=0)


def packed_pieces(count, width):
    rest = width % LANES
    return LANES // rest if width > LANES and rest and LANES % rest == 0 and count % 8 == 0 else 0


def packed_shape(count, width):
    fit = packed_pieces(count, width)
    if not fit:
        return count, width
    return width // LANES * count + -(-(count // 8) // fit) * 8, LANES


def pack_kernel(block_ref, out_ref):
    block = block_ref[...]
    count, width = block.shape
    fit = packed_pieces(count, width)
    if not fit:
        out_ref[...] = block
        return
    full = width // LANES
    for k in range(full):
        out_ref[k * count : (k + 1) * count, :] = block[:, k * LANES : (k + 1) * LANES]
    base = full * count
    pieces = [block[at : at + 8, full * LANES :] for at in range(0, count, 8)]
    for first in range(0, len(pieces), fit):
        line = pieces[first : first + fit]
        line += [jnp.zeros_like(line[0])] * (fit - len(line))
        out_ref[base + first // fit * 8 : base + first // fit * 8 + 8, :] = jnp.concatenate(line, axis=1)


def stack_kernel(*refs):
    begin = 0
    for ref in refs[:-1]:
        refs[-1][begin : begin + ref.shape[0], :] = ref[...]
        begin += ref.shape[0]


def unpacked(count, width, items):
    fit = packed_pieces(count, width)
    high = packed_shape(count, width)[0]
    full, rest = width // LANES, width % LANES
    mains, rests = [], []
    for ref in items:
        for base in range(0, ref.shape[0], high):
            if not fit:
                rests.append(ref[base : base + high, :])
                continue
            mains += [ref[base + k * count : base + (k + 1) * count, :] for k in range(full)]
            pieces = []
            for k in range(count // 8):
                at = base + full * count + k // fit * 8
                pieces.append(ref[at : at + 8, k % fit * rest : (k % fit + 1) * rest])
            rests.append(jnp.concatenate(pieces, axis=0))
    over = -sum(item.shape[1] for item in rests) % LANES
    if over:
        rests.append(jnp.zeros((count, over), jnp.float32))
    return jnp.concatenate(mains + rests, axis=1)


def columns_of(count, width, lines):
    blocks = sum(line.shape[0] for line in lines) // packed_shape(count, width)[0]
    return -(-blocks * width // LANES) * LANES


def tile_of(total, most):
    size = most
    while size > LANES:
        if total % size == 0:
            return size
        size -= LANES
    return size


def add_columns(width, scale, row_feat, lines, col_feat, high_feat, low_feat):
    feat = scale.shape[0]
    nvec = high_feat.shape[0] // 2
    block = unpacked(feat + nvec, width, lines)
    cols = block.shape[1]
    z = block[:feat] * jnp.concatenate([scale] * (cols // LANES), axis=1)
    col_feat[...] = column_stack(z).astype(jnp.bfloat16)
    vec = block[feat:]
    vec_high = vec.astype(jnp.bfloat16)
    high_feat[:nvec, :] = vec_high
    high_feat[nvec:, :] = (vec - vec_high.astype(jnp.float32)).astype(jnp.bfloat16)
    low_feat[:nvec, :] = vec_high
    low_feat[nvec:, :] = jnp.zeros_like(vec_high)
    tile = tile_of(cols, 256)

    def add(number, total):
        there = pl.ds(pl.multiple_of(number * tile, tile), tile)
        square = jnp.dot(row_feat, col_feat[:, there], preferred_element_type=jnp.float32)
        square = jnp.maximum(square, 1e-30)
        svalue = square * lax.rsqrt(square)
        value = (1.0 + svalue + square * (1.0 / 3.0)) * jnp.exp(-svalue)
        high = value.astype(jnp.bfloat16)
        low = (value - high.astype(jnp.float32)).astype(jnp.bfloat16)
        across = (((1,), (1,)), ((), ()))
        total = total + lax.dot_general(high, high_feat[:, there], across, preferred_element_type=jnp.float32)
        return total + lax.dot_general(low, low_feat[:, there], across, preferred_element_type=jnp.float32)

    count = cols // tile
    zeros = jnp.zeros((row_feat.shape[0], 2 * nvec), jnp.float32)
    return lax.fori_loop(0, count, add, zeros, unroll=count <= 16)


def first_kernel(nrow, scale_ref, *refs):
    row_refs, line_refs = refs[:nrow], refs[nrow:-6]
    total_ref, feat_ref, scale_out, *feats = refs[-6:]
    feat, width = row_refs[0].shape
    scale = jnp.broadcast_to(jnp.sqrt(jnp.float32(5.0)) / scale_ref[...], (feat, LANES))
    scale_out[...] = scale
    for k, ref in enumerate(row_refs):
        z = ref[...] * scale[:, :1]
        feat_ref[k * width : (k + 1) * width, :] = row_stack(z).T.astype(jnp.bfloat16)
    lines = [ref[...] for ref in line_refs]
    total_ref[...] = add_columns(width, scale, feat_ref[...], lines, *feats)


def last_kernel(nrow, scale_ref, feat_ref, before_ref, *refs):
    line_refs, out_refs, feats = refs[: -3 - nrow], refs[-3 - nrow : -3], refs[-3:]
    nvec, width = out_refs[0].shape
    lines = [ref[...] for ref in line_refs]
    total = before_ref[...] + add_columns(width, scale_ref[...], feat_ref[...], lines, *feats)
    for k, ref in enumerate(out_refs):
        part = total[k * width : (k + 1) * width].T
        ref[...] = part[:nvec] + part[nvec:]


def scratch(nvec, cols):
    return [
        pltpu.VMEM((STACK, cols), jnp.bfloat16),
        pltpu.VMEM((2 * nvec, cols), jnp.bfloat16),
        pltpu.VMEM((2 * nvec, cols), jnp.bfloat16),
    ]


def limits(rows, cols):
    return {
        "compiler_params": pltpu.CompilerParams(vmem_limit_bytes=4 * MIB + 4096 * rows + 2048 * cols),
        "cost_estimate": pl.CostEstimate(flops=0, bytes_accessed=0, transcendentals=0),
    }


def per_device(sizes, points, vectors, lengthscales):
    far, mid, pair, rep = sizes
    (feat, width), nvec = points.shape, vectors.shape[0]
    count, rows = feat + nvec, pair * width
    high, wide = packed_shape(count, width)

    def send(item, axis, step):
        return lax.ppermute(item, AXES, permutation(sizes, axis, step))

    def call(body, lines, out_shape, *operands):
        cols = columns_of(count, width, lines)
        return pl.pallas_call(
            body,
            out_shape=[jax.ShapeDtypeStruct(shape, dtype) for shape, dtype in out_shape],
            scratch_shapes=scratch(nvec, cols),
            **limits(rows, cols),
        )(*operands, *lines)

    block = pl.pallas_call(
        pack_kernel,
        out_shape=jax.ShapeDtypeStruct((high, wide), jnp.float32),
        compiler_params=pltpu.CompilerParams(vmem_limit_bytes=2 * MIB),
    )(jnp.concatenate([points, vectors], axis=0))
    later_points, block = lax.optimization_barrier((points, block))
    blocks = [send(block, "far", k) for k in reversed(range(1, far))]
    row_points = [send(later_points, "pair", k) for k in range(1, pair)]
    blocks, row_points = lax.optimization_barrier((blocks, row_points))
    line = pl.pallas_call(
        stack_kernel,
        out_shape=jax.ShapeDtypeStruct((far * high, wide), jnp.float32),
        compiler_params=pltpu.CompilerParams(vmem_limit_bytes=2 * MIB + 16 * far * high * wide),
    )(block, *blocks)
    plane = [send(line, "plane", k) for k in reversed(range(1, mid * rep))]
    total, row_feat, scale = call(
        functools.partial(first_kernel, pair),
        [line],
        [((rows, 2 * nvec), jnp.float32), ((rows, STACK), jnp.bfloat16), ((feat, LANES), jnp.float32)],
        lengthscales[:, None],
        points,
        *row_points,
    )
    total, plane = lax.optimization_barrier((total, plane))
    parts = call(
        functools.partial(last_kernel, pair),
        plane,
        [((nvec, width), jnp.float32)] * pair,
        scale,
        row_feat,
        total,
    )
    result = parts[0]
    for k in range(1, pair):
        back = [(target, source) for source, target in permutation(sizes, "pair", k)]
        result = result + lax.ppermute(parts[k], AXES, back)
    return result


def solution(mesh):
    sizes = split_blocks(mesh.shape["blk"], mesh.shape["rep"])
    return jax.shard_map(
        functools.partial(per_device, sizes),
        mesh=mesh,
        in_specs=(P(None, AXES), P(None, AXES), P()),
        out_specs=P(None, AXES),
        check_vma=False,
    )
```

```python
import functools

import jax
import jax.numpy as jnp
from jax import lax
from jax.experimental import pallas as pl
from jax.experimental.pallas import tpu as pltpu
from jax.sharding import PartitionSpec as P

AXES = ("blk", "rep")
LANES = 128
STACK = 128
MIB = 1024 * 1024


def split_blocks(blk, rep):
    pair = 2 if blk % 2 == 0 else 1
    line = blk // pair
    mid = max(d for d in range(1, line + 1) if line % d == 0 and d * d <= line)
    return line // mid, mid, pair, rep


def partner(index, step, size):
    return index ^ step if size & (size - 1) == 0 else (index + step) % size


def permutation(sizes, axis, step):
    far, mid, pair, rep = sizes
    pairs = []
    for target in range(far * mid * pair * rep):
        rest, q = divmod(target, rep)
        rest, p = divmod(rest, pair)
        f, m = divmod(rest, mid)
        if axis == "far":
            f = partner(f, step, far)
        elif axis == "pair":
            p = partner(p, step, pair)
        else:
            m, q = divmod(partner(m * rep + q, step, mid * rep), rep)
        pairs.append((((f * mid + m) * pair + p) * rep + q, target))
    return pairs


def three_parts(value):
    first = value.astype(jnp.bfloat16).astype(jnp.float32)
    second = (value - first).astype(jnp.bfloat16).astype(jnp.float32)
    return first, second, value - first - second


def norm_rows(square, ones_first, count):
    first, second, third = three_parts(square)
    line = lax.broadcasted_iota(jnp.int32, (count, square.shape[1]), 0)
    at = line - 3 if ones_first else line
    rows = jnp.where(at == 0, first, jnp.where(at == 1, second, jnp.where(at == 2, third, 0.0)))
    ones = (line < 3) if ones_first else (line >= 3) & (line < 6)
    return jnp.where(ones, 1.0, rows)


def column_stack(z):
    a, b, c = three_parts(z)
    square = jnp.sum(z * z, axis=0, keepdims=True)
    return jnp.concatenate([a, a, b, a, c, b, norm_rows(square, False, STACK - 6 * z.shape[0])], axis=0)


def row_stack(z):
    a, b, c = three_parts(z * -2.0)
    square = jnp.sum(z * z, axis=0, keepdims=True)
    return jnp.concatenate([a, b, a, c, a, b, norm_rows(square, True, STACK - 6 * z.shape[0])], axis=0)


def packed_pieces(count, width):
    rest = width % LANES
    return LANES // rest if width > LANES and rest and LANES % rest == 0 and count % 8 == 0 else 0


def packed_shape(count, width):
    fit = packed_pieces(count, width)
    if not fit:
        return count, width
    return width // LANES * count + -(-(count // 8) // fit) * 8, LANES


def pack_kernel(block_ref, out_ref):
    block = block_ref[...]
    count, width = block.shape
    fit = packed_pieces(count, width)
    if not fit:
        out_ref[...] = block
        return
    full = width // LANES
    for k in range(full):
        out_ref[k * count : (k + 1) * count, :] = block[:, k * LANES : (k + 1) * LANES]
    base = full * count
    pieces = [block[at : at + 8, full * LANES :] for at in range(0, count, 8)]
    for first in range(0, len(pieces), fit):
        line = pieces[first : first + fit]
        line += [jnp.zeros_like(line[0])] * (fit - len(line))
        out_ref[base + first // fit * 8 : base + first // fit * 8 + 8, :] = jnp.concatenate(line, axis=1)


def line_shape(count, width, blocks):
    return -(-blocks * width // LANES) * count, LANES


def line_kernel(count, width, *refs):
    block_refs, out_ref = refs[:-1], refs[-1]
    fit = packed_pieces(count, width)
    full, rest = width // LANES, width % LANES
    if not fit:
        joined = [ref[...] for ref in block_refs]
    else:
        joined, at = [], 0
        for ref in block_refs:
            for k in range(full):
                out_ref[at : at + count, :] = ref[k * count : (k + 1) * count, :]
                at += count
            pieces = []
            for k in range(count // 8):
                begin = full * count + k // fit * 8
                pieces.append(ref[begin : begin + 8, k % fit * rest : (k % fit + 1) * rest])
            joined.append(jnp.concatenate(pieces, axis=0))
    begin = 0 if not fit else len(block_refs) * full * count
    over = -sum(item.shape[1] for item in joined) % LANES
    if over:
        joined.append(jnp.zeros((count, over), jnp.float32))
    tails = jnp.concatenate(joined, axis=1)
    for k in range(tails.shape[1] // LANES):
        out_ref[begin + k * count : begin + (k + 1) * count, :] = tails[:, k * LANES : (k + 1) * LANES]


def tile_of(total, most):
    size = most
    while size > LANES:
        if total % size == 0:
            return size
        size -= LANES
    return size


def add_columns(scale, row_feat, lines, col_feat, high_feat, low_feat):
    feat = scale.shape[0]
    nvec = high_feat.shape[0] // 2
    count = feat + nvec
    pieces = [line[at : at + count] for line in lines for at in range(0, line.shape[0], count)]
    block = jnp.concatenate(pieces, axis=1)
    cols = block.shape[1]
    z = block[:feat] * jnp.concatenate([scale] * (cols // LANES), axis=1)
    col_feat[...] = column_stack(z).astype(jnp.bfloat16)
    vec = block[feat:]
    vec_high = vec.astype(jnp.bfloat16)
    high_feat[:nvec, :] = vec_high
    high_feat[nvec:, :] = (vec - vec_high.astype(jnp.float32)).astype(jnp.bfloat16)
    low_feat[:nvec, :] = vec_high
    low_feat[nvec:, :] = jnp.zeros_like(vec_high)
    tile = tile_of(cols, 256)

    def add(number, total):
        there = pl.ds(pl.multiple_of(number * tile, tile), tile)
        square = jnp.dot(row_feat, col_feat[:, there], preferred_element_type=jnp.float32)
        square = jnp.maximum(square, 1e-30)
        svalue = square * lax.rsqrt(square)
        value = (1.0 + svalue + square * (1.0 / 3.0)) * jnp.exp(-svalue)
        high = value.astype(jnp.bfloat16)
        low = (value - high.astype(jnp.float32)).astype(jnp.bfloat16)
        across = (((1,), (1,)), ((), ()))
        total = total + lax.dot_general(high, high_feat[:, there], across, preferred_element_type=jnp.float32)
        return total + lax.dot_general(low, low_feat[:, there], across, preferred_element_type=jnp.float32)

    count = cols // tile
    zeros = jnp.zeros((row_feat.shape[0], 2 * nvec), jnp.float32)
    return lax.fori_loop(0, count, add, zeros, unroll=count <= 16)


def first_kernel(nrow, scale_ref, *refs):
    row_refs, line_refs = refs[:nrow], refs[nrow:-6]
    total_ref, feat_ref, scale_out, *feats = refs[-6:]
    feat, width = row_refs[0].shape
    scale = jnp.broadcast_to(jnp.sqrt(jnp.float32(5.0)) / scale_ref[...], (feat, LANES))
    scale_out[...] = scale
    for k, ref in enumerate(row_refs):
        z = ref[...] * scale[:, :1]
        feat_ref[k * width : (k + 1) * width, :] = row_stack(z).T.astype(jnp.bfloat16)
    lines = [ref[...] for ref in line_refs]
    total_ref[...] = add_columns(scale, feat_ref[...], lines, *feats)


def next_kernel(nout, scale_ref, feat_ref, before_ref, *refs):
    line_refs, out_refs, feats = refs[: -3 - nout], refs[-3 - nout : -3], refs[-3:]
    nvec, width = out_refs[0].shape
    lines = [ref[...] for ref in line_refs]
    total = before_ref[...] + add_columns(scale_ref[...], feat_ref[...], lines, *feats)
    if out_refs[0].shape == total.shape:
        out_refs[0][...] = total
        return
    for k, ref in enumerate(out_refs):
        part = total[k * width : (k + 1) * width].T
        ref[...] = part[:nvec] + part[nvec:]


def scratch(nvec, cols):
    return [
        pltpu.VMEM((STACK, cols), jnp.bfloat16),
        pltpu.VMEM((2 * nvec, cols), jnp.bfloat16),
        pltpu.VMEM((2 * nvec, cols), jnp.bfloat16),
    ]


def limits(rows, cols):
    return {
        "compiler_params": pltpu.CompilerParams(vmem_limit_bytes=4 * MIB + 4096 * rows + 2048 * cols),
        "cost_estimate": pl.CostEstimate(flops=0, bytes_accessed=0, transcendentals=0),
    }


def per_device(sizes, points, vectors, lengthscales):
    far, mid, pair, rep = sizes
    (feat, width), nvec = points.shape, vectors.shape[0]
    count, rows = feat + nvec, pair * width
    high, wide = packed_shape(count, width)

    def send(item, axis, step):
        return lax.ppermute(item, AXES, permutation(sizes, axis, step))

    def call(body, lines, out_shape, *operands):
        cols = sum(line.shape[0] for line in lines) // count * LANES
        return pl.pallas_call(
            body,
            out_shape=[jax.ShapeDtypeStruct(shape, dtype) for shape, dtype in out_shape],
            scratch_shapes=scratch(nvec, cols),
            **limits(rows, cols),
        )(*operands, *lines)

    block = pl.pallas_call(
        pack_kernel,
        out_shape=jax.ShapeDtypeStruct((high, wide), jnp.float32),
        compiler_params=pltpu.CompilerParams(vmem_limit_bytes=2 * MIB),
    )(jnp.concatenate([points, vectors], axis=0))
    later_points, block = lax.optimization_barrier((points, block))
    blocks = [send(block, "far", k) for k in reversed(range(1, far))]
    row_points = [send(later_points, "pair", k) for k in range(1, pair)]
    blocks, row_points = lax.optimization_barrier((blocks, row_points))
    line = pl.pallas_call(
        functools.partial(line_kernel, count, width),
        out_shape=jax.ShapeDtypeStruct(line_shape(count, width, far), jnp.float32),
        compiler_params=pltpu.CompilerParams(vmem_limit_bytes=2 * MIB + 16 * far * high * wide),
    )(block, *blocks)
    plane = [send(line, "plane", k) for k in range(1, mid * rep)]
    total, row_feat, scale = call(
        functools.partial(first_kernel, pair),
        [line],
        [((rows, 2 * nvec), jnp.float32), ((rows, STACK), jnp.bfloat16), ((feat, LANES), jnp.float32)],
        lengthscales[:, None],
        points,
        *row_points,
    )
    total_shape = (rows, 2 * nvec)

    def more(total, lines, shapes):
        total, lines = lax.optimization_barrier((total, lines))
        out_shape = [(shape, jnp.float32) for shape in shapes]
        return call(functools.partial(next_kernel, len(shapes)), lines, out_shape, scale, row_feat, total)

    early, late = plane[:-1], plane[-1:]
    if early:
        (total,) = more(total, early, [total_shape])
    parts = more(total, late, [(nvec, width)] * pair)
    result = parts[0]
    for k in range(1, pair):
        back = [(target, source) for source, target in permutation(sizes, "pair", k)]
        result = result + lax.ppermute(parts[k], AXES, back)
    return result


def solution(mesh):
    sizes = split_blocks(mesh.shape["blk"], mesh.shape["rep"])
    return jax.shard_map(
        functools.partial(per_device, sizes),
        mesh=mesh,
        in_specs=(P(None, AXES), P(None, AXES), P()),
        out_specs=P(None, AXES),
        check_vma=False,
    )
```

```python
import functools

import jax
import jax.numpy as jnp
from jax import lax
from jax.experimental import pallas as pl
from jax.experimental.pallas import tpu as pltpu
from jax.sharding import PartitionSpec as P

AXES = ("blk", "rep")
LANES = 128
MIB = 1024 * 1024


def split_blocks(blk, rep):
    pair = 2 if blk % 2 == 0 else 1
    line = blk // pair
    mid = max(d for d in range(1, line + 1) if line % d == 0 and d * d <= line)
    return line // mid, mid, pair, rep


def partner(index, step, size):
    return index ^ step if size & (size - 1) == 0 else (index + step) % size


def permutation(sizes, axis, step):
    far, mid, pair, rep = sizes
    pairs = []
    for target in range(far * mid * pair * rep):
        rest, q = divmod(target, rep)
        rest, p = divmod(rest, pair)
        f, m = divmod(rest, mid)
        if axis == "far":
            f = partner(f, step, far)
        elif axis == "pair":
            p = partner(p, step, pair)
        else:
            m, q = divmod(partner(m * rep + q, step, mid * rep), rep)
        pairs.append((((f * mid + m) * pair + p) * rep + q, target))
    return pairs


def three_parts(value):
    first = value.astype(jnp.bfloat16).astype(jnp.float32)
    second = (value - first).astype(jnp.bfloat16).astype(jnp.float32)
    return first, second, value - first - second


def stack_rows(feat):
    return 6 * feat + 16


def norm_rows(square, ones_first):
    first, second, third = three_parts(square)
    line = lax.broadcasted_iota(jnp.int32, (16, square.shape[1]), 0)
    at = line - 3 if ones_first else line
    rows = jnp.where(at == 0, first, jnp.where(at == 1, second, jnp.where(at == 2, third, 0.0)))
    ones = (line < 3) if ones_first else (line >= 3) & (line < 6)
    return jnp.where(ones, 1.0, rows)


def column_stack(z):
    a, b, c = three_parts(z)
    square = jnp.sum(z * z, axis=0, keepdims=True)
    return jnp.concatenate([a, a, b, a, c, b, norm_rows(square, False)], axis=0)


def row_stack(z):
    a, b, c = three_parts(z * -2.0)
    square = jnp.sum(z * z, axis=0, keepdims=True)
    return jnp.concatenate([a, b, a, c, a, b, norm_rows(square, True)], axis=0)


def packed_pieces(count, width):
    rest = width % LANES
    return LANES // rest if width > LANES and rest and LANES % rest == 0 and count % 8 == 0 else 0


def packed_shape(count, width):
    fit = packed_pieces(count, width)
    if not fit:
        return count, width
    return width // LANES * count + -(-(count // 8) // fit) * 8, LANES


def pack_kernel(block_ref, out_ref):
    block = block_ref[...]
    count, width = block.shape
    fit = packed_pieces(count, width)
    if not fit:
        out_ref[...] = block
        return
    full = width // LANES
    for k in range(full):
        out_ref[k * count : (k + 1) * count, :] = block[:, k * LANES : (k + 1) * LANES]
    base = full * count
    pieces = [block[at : at + 8, full * LANES :] for at in range(0, count, 8)]
    for first in range(0, len(pieces), fit):
        line = pieces[first : first + fit]
        line += [jnp.zeros_like(line[0])] * (fit - len(line))
        out_ref[base + first // fit * 8 : base + first // fit * 8 + 8, :] = jnp.concatenate(line, axis=1)


def line_shape(count, width, blocks):
    return -(-blocks * width // LANES) * count, LANES


def line_kernel(count, width, *refs):
    block_refs, out_ref = refs[:-1], refs[-1]
    fit = packed_pieces(count, width)
    full, rest = width // LANES, width % LANES
    if not fit:
        joined = [ref[...] for ref in block_refs]
    else:
        joined, at = [], 0
        for ref in block_refs:
            for k in range(full):
                out_ref[at : at + count, :] = ref[k * count : (k + 1) * count, :]
                at += count
            pieces = []
            for k in range(count // 8):
                begin = full * count + k // fit * 8
                pieces.append(ref[begin : begin + 8, k % fit * rest : (k % fit + 1) * rest])
            joined.append(jnp.concatenate(pieces, axis=0))
    begin = 0 if not fit else len(block_refs) * full * count
    over = -sum(item.shape[1] for item in joined) % LANES
    if over:
        joined.append(jnp.zeros((count, over), jnp.float32))
    tails = jnp.concatenate(joined, axis=1)
    for k in range(tails.shape[1] // LANES):
        out_ref[begin + k * count : begin + (k + 1) * count, :] = tails[:, k * LANES : (k + 1) * LANES]


def add_columns(scale, row_feat, lines, col_feat, vec_feat):
    feat = scale.shape[0]
    nvec = vec_feat.shape[0] // 2
    count = feat + nvec
    pieces = [line[at : at + count] for line in lines for at in range(0, line.shape[0], count)]
    for k, piece in enumerate(pieces):
        there = pl.ds(k * LANES, LANES)
        col_feat[:, there] = column_stack(piece[:feat] * scale).astype(jnp.bfloat16)
        vec = piece[feat:]
        vec_high = vec.astype(jnp.bfloat16)
        at = 2 * k * LANES
        vec_feat[:nvec, at : at + LANES] = vec_high
        vec_feat[nvec:, at : at + LANES] = (vec - vec_high.astype(jnp.float32)).astype(jnp.bfloat16)
        vec_feat[:nvec, at + LANES : at + 2 * LANES] = vec_high
        vec_feat[nvec:, at + LANES : at + 2 * LANES] = jnp.zeros_like(vec_high)

    def add(number, total):
        there = pl.ds(pl.multiple_of(number * LANES, LANES), LANES)
        square = jnp.dot(row_feat, col_feat[:, there], preferred_element_type=jnp.float32)
        square = jnp.maximum(square, 1e-30)
        svalue = square * lax.rsqrt(square)
        value = (1.0 + svalue + square * (1.0 / 3.0)) * jnp.exp(-svalue)
        high = value.astype(jnp.bfloat16)
        low = (value - high.astype(jnp.float32)).astype(jnp.bfloat16)
        vec = vec_feat[:, pl.ds(pl.multiple_of(number * 2 * LANES, 2 * LANES), 2 * LANES)]
        across = (((1,), (1,)), ((), ()))
        both = jnp.concatenate([high, low], axis=1)
        return total + lax.dot_general(both, vec, across, preferred_element_type=jnp.float32)

    zeros = jnp.zeros((row_feat.shape[0], 2 * nvec), jnp.float32)
    return lax.fori_loop(0, len(pieces), add, zeros, unroll=len(pieces) <= 16)


def first_kernel(nrow, scale_ref, *refs):
    row_refs, line_refs = refs[:nrow], refs[nrow:-5]
    total_ref, feat_ref, scale_out, *feats = refs[-5:]
    feat, width = row_refs[0].shape
    scale = jnp.broadcast_to(jnp.sqrt(jnp.float32(5.0)) / scale_ref[...], (feat, LANES))
    scale_out[...] = scale
    for k, ref in enumerate(row_refs):
        z = ref[...] * scale[:, :1]
        feat_ref[k * width : (k + 1) * width, :] = row_stack(z).T.astype(jnp.bfloat16)
    lines = [ref[...] for ref in line_refs]
    total_ref[...] = add_columns(scale, feat_ref[...], lines, *feats)


def next_kernel(nout, scale_ref, feat_ref, before_ref, *refs):
    line_refs, out_refs, feats = refs[: -2 - nout], refs[-2 - nout : -2], refs[-2:]
    nvec, width = out_refs[0].shape
    lines = [ref[...] for ref in line_refs]
    total = before_ref[...] + add_columns(scale_ref[...], feat_ref[...], lines, *feats)
    if out_refs[0].shape == total.shape:
        out_refs[0][...] = total
        return
    for k, ref in enumerate(out_refs):
        part = total[k * width : (k + 1) * width].T
        ref[...] = part[:nvec] + part[nvec:]


def scratch(feat, nvec, cols):
    return [pltpu.VMEM((stack_rows(feat), cols), jnp.bfloat16), pltpu.VMEM((2 * nvec, 2 * cols), jnp.bfloat16)]


def limits(rows, cols):
    return {
        "compiler_params": pltpu.CompilerParams(vmem_limit_bytes=4 * MIB + 4096 * rows + 2048 * cols),
        "cost_estimate": pl.CostEstimate(flops=0, bytes_accessed=0, transcendentals=0),
    }


def per_device(sizes, points, vectors, lengthscales):
    far, mid, pair, rep = sizes
    (feat, width), nvec = points.shape, vectors.shape[0]
    count, rows = feat + nvec, pair * width
    high, wide = packed_shape(count, width)

    def send(item, axis, step):
        return lax.ppermute(item, AXES, permutation(sizes, axis, step))

    def call(body, lines, out_shape, *operands):
        cols = sum(line.shape[0] for line in lines) // count * LANES
        return pl.pallas_call(
            body,
            out_shape=[jax.ShapeDtypeStruct(shape, dtype) for shape, dtype in out_shape],
            scratch_shapes=scratch(feat, nvec, cols),
            **limits(rows, cols),
        )(*operands, *lines)

    block = pl.pallas_call(
        pack_kernel,
        out_shape=jax.ShapeDtypeStruct((high, wide), jnp.float32),
        compiler_params=pltpu.CompilerParams(vmem_limit_bytes=2 * MIB),
    )(jnp.concatenate([points, vectors], axis=0))
    later_points, block = lax.optimization_barrier((points, block))
    blocks = [send(block, "far", k) for k in [1, *reversed(range(2, far))][: far - 1]]
    row_points = [send(later_points, "pair", k) for k in range(1, pair)]
    blocks, row_points = lax.optimization_barrier((blocks, row_points))
    line = pl.pallas_call(
        functools.partial(line_kernel, count, width),
        out_shape=jax.ShapeDtypeStruct(line_shape(count, width, far), jnp.float32),
        compiler_params=pltpu.CompilerParams(vmem_limit_bytes=2 * MIB + 16 * far * high * wide),
    )(block, *blocks)
    plane = [send(line, "plane", k) for k in range(1, mid * rep)]
    total, row_feat, scale = call(
        functools.partial(first_kernel, pair),
        [line],
        [((rows, 2 * nvec), jnp.float32), ((rows, stack_rows(feat)), jnp.bfloat16), ((feat, LANES), jnp.float32)],
        lengthscales[:, None],
        points,
        *row_points,
    )
    total_shape = (rows, 2 * nvec)

    def more(total, lines, shapes):
        total, lines = lax.optimization_barrier((total, lines))
        out_shape = [(shape, jnp.float32) for shape in shapes]
        return call(functools.partial(next_kernel, len(shapes)), lines, out_shape, scale, row_feat, total)

    early, late = plane[:-1], plane[-1:]
    if early:
        (total,) = more(total, early, [total_shape])
    parts = more(total, late, [(nvec, width)] * pair)
    result = parts[0]
    for k in range(1, pair):
        back = [(target, source) for source, target in permutation(sizes, "pair", k)]
        result = result + lax.ppermute(parts[k], AXES, back)
    return result


def solution(mesh):
    sizes = split_blocks(mesh.shape["blk"], mesh.shape["rep"])
    return jax.shard_map(
        functools.partial(per_device, sizes),
        mesh=mesh,
        in_specs=(P(None, AXES), P(None, AXES), P()),
        out_specs=P(None, AXES),
        check_vma=False,
    )
```

```python
import functools

import jax
import jax.numpy as jnp
from jax import lax
from jax.experimental import pallas as pl
from jax.experimental.pallas import tpu as pltpu
from jax.sharding import PartitionSpec as P

AXES = ("blk", "rep")
LANES = 128
MIB = 1024 * 1024


def split_blocks(blk, rep):
    pair = 2 if blk % 2 == 0 else 1
    line = blk // pair
    mid = max(d for d in range(1, line + 1) if line % d == 0 and d * d <= line)
    return line // mid, mid, pair, rep


def partner(index, step, size):
    return index ^ step if size & (size - 1) == 0 else (index + step) % size


def permutation(sizes, axis, step):
    far, mid, pair, rep = sizes
    pairs = []
    for target in range(far * mid * pair * rep):
        rest, q = divmod(target, rep)
        rest, p = divmod(rest, pair)
        f, m = divmod(rest, mid)
        if axis == "far":
            f = partner(f, step, far)
        elif axis == "pair":
            p = partner(p, step, pair)
        else:
            m, q = divmod(partner(m * rep + q, step, mid * rep), rep)
        pairs.append((((f * mid + m) * pair + p) * rep + q, target))
    return pairs


def three_parts(value):
    first = value.astype(jnp.bfloat16).astype(jnp.float32)
    second = (value - first).astype(jnp.bfloat16).astype(jnp.float32)
    return first, second, value - first - second


def stack_rows(feat):
    return 6 * feat + 16


def norm_rows(square, ones_first):
    first, second, third = three_parts(square)
    line = lax.broadcasted_iota(jnp.int32, (16, square.shape[1]), 0)
    at = line - 3 if ones_first else line
    rows = jnp.where(at == 0, first, jnp.where(at == 1, second, jnp.where(at == 2, third, 0.0)))
    ones = (line < 3) if ones_first else (line >= 3) & (line < 6)
    return jnp.where(ones, 1.0, rows)


def column_stack(z):
    a, b, c = three_parts(z)
    square = jnp.sum(z * z, axis=0, keepdims=True)
    return jnp.concatenate([a, a, b, a, c, b, norm_rows(square, False)], axis=0)


def row_stack(z):
    a, b, c = three_parts(z * -2.0)
    square = jnp.sum(z * z, axis=0, keepdims=True)
    return jnp.concatenate([a, b, a, c, a, b, norm_rows(square, True)], axis=0)


def packed_pieces(count, width):
    rest = width % LANES
    return LANES // rest if width > LANES and rest and LANES % rest == 0 and count % 8 == 0 else 0


def packed_shape(count, width):
    fit = packed_pieces(count, width)
    if not fit:
        return count, width
    return width // LANES * count + -(-(count // 8) // fit) * 8, LANES


def pack_kernel(block_ref, out_ref):
    block = block_ref[...]
    count, width = block.shape
    fit = packed_pieces(count, width)
    if not fit:
        out_ref[...] = block
        return
    full = width // LANES
    for k in range(full):
        out_ref[k * count : (k + 1) * count, :] = block[:, k * LANES : (k + 1) * LANES]
    base = full * count
    pieces = [block[at : at + 8, full * LANES :] for at in range(0, count, 8)]
    for first in range(0, len(pieces), fit):
        line = pieces[first : first + fit]
        line += [jnp.zeros_like(line[0])] * (fit - len(line))
        out_ref[base + first // fit * 8 : base + first // fit * 8 + 8, :] = jnp.concatenate(line, axis=1)


def line_shape(count, width, blocks):
    return -(-blocks * width // LANES) * count, LANES


def line_kernel(count, width, blocks_ref, out_ref):
    high = packed_shape(count, width)[0]
    blocks = [blocks_ref[at : at + high, :] for at in range(0, blocks_ref.shape[0], high)]
    fit = packed_pieces(count, width)
    full, rest = width // LANES, width % LANES
    if not fit:
        joined = blocks
    else:
        joined, at = [], 0
        for block in blocks:
            for k in range(full):
                out_ref[at : at + count, :] = block[k * count : (k + 1) * count]
                at += count
            pieces = []
            for k in range(count // 8):
                begin = full * count + k // fit * 8
                pieces.append(block[begin : begin + 8, k % fit * rest : (k % fit + 1) * rest])
            joined.append(jnp.concatenate(pieces, axis=0))
    begin = 0 if not fit else len(blocks) * full * count
    over = -sum(item.shape[1] for item in joined) % LANES
    if over:
        joined.append(jnp.zeros((count, over), jnp.float32))
    tails = jnp.concatenate(joined, axis=1)
    for k in range(tails.shape[1] // LANES):
        out_ref[begin + k * count : begin + (k + 1) * count, :] = tails[:, k * LANES : (k + 1) * LANES]


def add_columns(scale, row_feat, lines, col_feat, vec_feat):
    feat = scale.shape[0]
    nvec = vec_feat.shape[0] // 2
    count = feat + nvec
    pieces = [line[at : at + count] for line in lines for at in range(0, line.shape[0], count)]
    for k, piece in enumerate(pieces):
        there = pl.ds(k * LANES, LANES)
        col_feat[:, there] = column_stack(piece[:feat] * scale).astype(jnp.bfloat16)
        vec = piece[feat:]
        vec_high = vec.astype(jnp.bfloat16)
        at = 2 * k * LANES
        vec_feat[:nvec, at : at + LANES] = vec_high
        vec_feat[nvec:, at : at + LANES] = (vec - vec_high.astype(jnp.float32)).astype(jnp.bfloat16)
        vec_feat[:nvec, at + LANES : at + 2 * LANES] = vec_high
        vec_feat[nvec:, at + LANES : at + 2 * LANES] = jnp.zeros_like(vec_high)

    def add(number, total):
        there = pl.ds(pl.multiple_of(number * LANES, LANES), LANES)
        square = jnp.dot(row_feat, col_feat[:, there], preferred_element_type=jnp.float32)
        square = jnp.maximum(square, 1e-30)
        svalue = square * lax.rsqrt(square)
        value = (1.0 + svalue + square * (1.0 / 3.0)) * jnp.exp(-svalue)
        high = value.astype(jnp.bfloat16)
        low = (value - high.astype(jnp.float32)).astype(jnp.bfloat16)
        vec = vec_feat[:, pl.ds(pl.multiple_of(number * 2 * LANES, 2 * LANES), 2 * LANES)]
        across = (((1,), (1,)), ((), ()))
        both = jnp.concatenate([high, low], axis=1)
        return total + lax.dot_general(both, vec, across, preferred_element_type=jnp.float32)

    zeros = jnp.zeros((row_feat.shape[0], 2 * nvec), jnp.float32)
    return lax.fori_loop(0, len(pieces), add, zeros, unroll=len(pieces) <= 16)


def first_kernel(nrow, scale_ref, *refs):
    row_refs, line_refs = refs[:nrow], refs[nrow:-5]
    total_ref, feat_ref, scale_out, *feats = refs[-5:]
    feat, width = row_refs[0].shape
    scale = jnp.broadcast_to(jnp.sqrt(jnp.float32(5.0)) / scale_ref[...], (feat, LANES))
    scale_out[...] = scale
    for k, ref in enumerate(row_refs):
        z = ref[...] * scale[:, :1]
        feat_ref[k * width : (k + 1) * width, :] = row_stack(z).T.astype(jnp.bfloat16)
    lines = [ref[...] for ref in line_refs]
    total_ref[...] = add_columns(scale, feat_ref[...], lines, *feats)


def next_kernel(nout, scale_ref, feat_ref, before_ref, *refs):
    line_refs, out_refs, feats = refs[: -2 - nout], refs[-2 - nout : -2], refs[-2:]
    nvec, width = out_refs[0].shape
    lines = [ref[...] for ref in line_refs]
    total = before_ref[...] + add_columns(scale_ref[...], feat_ref[...], lines, *feats)
    if out_refs[0].shape == total.shape:
        out_refs[0][...] = total
        return
    for k, ref in enumerate(out_refs):
        part = total[k * width : (k + 1) * width].T
        ref[...] = part[:nvec] + part[nvec:]


def scratch(feat, nvec, cols):
    return [pltpu.VMEM((stack_rows(feat), cols), jnp.bfloat16), pltpu.VMEM((2 * nvec, 2 * cols), jnp.bfloat16)]


def limits(rows, cols):
    return {
        "compiler_params": pltpu.CompilerParams(vmem_limit_bytes=4 * MIB + 4096 * rows + 2048 * cols),
        "cost_estimate": pl.CostEstimate(flops=0, bytes_accessed=0, transcendentals=0),
    }


def per_device(sizes, points, vectors, lengthscales):
    far, mid, pair, rep = sizes
    (feat, width), nvec = points.shape, vectors.shape[0]
    count, rows = feat + nvec, pair * width
    high, wide = packed_shape(count, width)

    def send(item, axis, step):
        return lax.ppermute(item, AXES, permutation(sizes, axis, step))

    def call(body, lines, out_shape, *operands):
        cols = sum(line.shape[0] for line in lines) // count * LANES
        return pl.pallas_call(
            body,
            out_shape=[jax.ShapeDtypeStruct(shape, dtype) for shape, dtype in out_shape],
            scratch_shapes=scratch(feat, nvec, cols),
            **limits(rows, cols),
        )(*operands, *lines)

    block = pl.pallas_call(
        pack_kernel,
        out_shape=jax.ShapeDtypeStruct((high, wide), jnp.float32),
        compiler_params=pltpu.CompilerParams(vmem_limit_bytes=2 * MIB),
    )(jnp.concatenate([points, vectors], axis=0))
    later_points, block = lax.optimization_barrier((points, block))
    groups = [[(f * mid + m) * pair + p for f in range(far)] for m in range(mid) for p in range(pair)]
    blocks = lax.all_gather(block, "blk", axis_index_groups=groups, axis=0, tiled=True)
    row_points = [send(later_points, "pair", k) for k in range(1, pair)]
    blocks, row_points = lax.optimization_barrier((blocks, row_points))
    line = pl.pallas_call(
        functools.partial(line_kernel, count, width),
        out_shape=jax.ShapeDtypeStruct(line_shape(count, width, far), jnp.float32),
        compiler_params=pltpu.CompilerParams(vmem_limit_bytes=2 * MIB + 16 * far * high * wide),
    )(blocks)
    plane = [send(line, "plane", k) for k in range(1, mid * rep)]
    total, row_feat, scale = call(
        functools.partial(first_kernel, pair),
        [line],
        [((rows, 2 * nvec), jnp.float32), ((rows, stack_rows(feat)), jnp.bfloat16), ((feat, LANES), jnp.float32)],
        lengthscales[:, None],
        points,
        *row_points,
    )
    total_shape = (rows, 2 * nvec)

    def more(total, lines, shapes):
        total, lines = lax.optimization_barrier((total, lines))
        out_shape = [(shape, jnp.float32) for shape in shapes]
        return call(functools.partial(next_kernel, len(shapes)), lines, out_shape, scale, row_feat, total)

    early, late = plane[:-1], plane[-1:]
    if early:
        (total,) = more(total, early, [total_shape])
    parts = more(total, late, [(nvec, width)] * pair)
    result = parts[0]
    for k in range(1, pair):
        back = [(target, source) for source, target in permutation(sizes, "pair", k)]
        result = result + lax.ppermute(parts[k], AXES, back)
    return result


def solution(mesh):
    sizes = split_blocks(mesh.shape["blk"], mesh.shape["rep"])
    return jax.shard_map(
        functools.partial(per_device, sizes),
        mesh=mesh,
        in_specs=(P(None, AXES), P(None, AXES), P()),
        out_specs=P(None, AXES),
        check_vma=False,
    )
```

```python
import functools

import jax
import jax.numpy as jnp
from jax import lax
from jax.experimental import pallas as pl
from jax.experimental.pallas import tpu as pltpu
from jax.sharding import PartitionSpec as P

AXES = ("blk", "rep")
LANES = 128
MIB = 1024 * 1024


def split_blocks(blk, rep):
    pair = 2 if blk % 2 == 0 else 1
    line = blk // pair
    mid = max(d for d in range(1, line + 1) if line % d == 0 and d * d <= line)
    return line // mid, mid, pair, rep


def partner(index, step, size):
    return index ^ step if size & (size - 1) == 0 else (index + step) % size


def permutation(sizes, axis, step):
    far, mid, pair, rep = sizes
    pairs = []
    for target in range(far * mid * pair * rep):
        rest, q = divmod(target, rep)
        rest, p = divmod(rest, pair)
        f, m = divmod(rest, mid)
        if axis == "far":
            f = partner(f, step, far)
        elif axis == "pair":
            p = partner(p, step, pair)
        else:
            m, q = divmod(partner(m * rep + q, step, mid * rep), rep)
        pairs.append((((f * mid + m) * pair + p) * rep + q, target))
    return pairs


def reverse(pairs):
    return [(target, source) for source, target in pairs]


def three_parts(value):
    first = value.astype(jnp.bfloat16).astype(jnp.float32)
    second = (value - first).astype(jnp.bfloat16).astype(jnp.float32)
    return first, second, value - first - second


def stack_rows(feat):
    return 6 * feat + 16


def norm_rows(square, ones_first):
    first, second, third = three_parts(square)
    line = lax.broadcasted_iota(jnp.int32, (16, square.shape[1]), 0)
    at = line - 3 if ones_first else line
    rows = jnp.where(at == 0, first, jnp.where(at == 1, second, jnp.where(at == 2, third, 0.0)))
    ones = (line < 3) if ones_first else (line >= 3) & (line < 6)
    return jnp.where(ones, 1.0, rows)


def column_stack(z):
    a, b, c = three_parts(z)
    square = jnp.sum(z * z, axis=0, keepdims=True)
    return jnp.concatenate([a, a, b, a, c, b, norm_rows(square, False)], axis=0)


def row_stack(z):
    a, b, c = three_parts(z * -2.0)
    square = jnp.sum(z * z, axis=0, keepdims=True)
    return jnp.concatenate([a, b, a, c, a, b, norm_rows(square, True)], axis=0)


def packed_pieces(count, width):
    rest = width % LANES
    return LANES // rest if width > LANES and rest and LANES % rest == 0 and count % 8 == 0 else 0


def packed_shape(count, width):
    fit = packed_pieces(count, width)
    if not fit:
        return count, width
    return width // LANES * count + -(-(count // 8) // fit) * 8, LANES


def pack_kernel(block_ref, out_ref):
    block = block_ref[...]
    count, width = block.shape
    fit = packed_pieces(count, width)
    if not fit:
        out_ref[...] = block
        return
    full = width // LANES
    for k in range(full):
        out_ref[k * count : (k + 1) * count, :] = block[:, k * LANES : (k + 1) * LANES]
    base = full * count
    pieces = [block[at : at + 8, full * LANES :] for at in range(0, count, 8)]
    for first in range(0, len(pieces), fit):
        line = pieces[first : first + fit]
        line += [jnp.zeros_like(line[0])] * (fit - len(line))
        out_ref[base + first // fit * 8 : base + first // fit * 8 + 8, :] = jnp.concatenate(line, axis=1)


def line_shape(count, width, blocks):
    return -(-blocks * width // LANES) * count, LANES


def line_kernel(count, width, *refs):
    block_refs, out_ref = refs[:-1], refs[-1]
    fit = packed_pieces(count, width)
    full, rest = width // LANES, width % LANES
    if not fit:
        joined = [ref[...] for ref in block_refs]
    else:
        joined, at = [], 0
        for ref in block_refs:
            for k in range(full):
                out_ref[at : at + count, :] = ref[k * count : (k + 1) * count, :]
                at += count
            pieces = []
            for k in range(count // 8):
                begin = full * count + k // fit * 8
                pieces.append(ref[begin : begin + 8, k % fit * rest : (k % fit + 1) * rest])
            joined.append(jnp.concatenate(pieces, axis=0))
    begin = 0 if not fit else len(block_refs) * full * count
    over = -sum(item.shape[1] for item in joined) % LANES
    if over:
        joined.append(jnp.zeros((count, over), jnp.float32))
    tails = jnp.concatenate(joined, axis=1)
    for k in range(tails.shape[1] // LANES):
        out_ref[begin + k * count : begin + (k + 1) * count, :] = tails[:, k * LANES : (k + 1) * LANES]


def add_columns(scale, row_feat, lines, col_feat, vec_feat):
    feat = scale.shape[0]
    nvec = vec_feat.shape[0] // 2
    count = feat + nvec
    pieces = [line[at : at + count] for line in lines for at in range(0, line.shape[0], count)]
    for k, piece in enumerate(pieces):
        there = pl.ds(k * LANES, LANES)
        col_feat[:, there] = column_stack(piece[:feat] * scale).astype(jnp.bfloat16)
        vec = piece[feat:]
        vec_high = vec.astype(jnp.bfloat16)
        at = 2 * k * LANES
        vec_feat[:nvec, at : at + LANES] = vec_high
        vec_feat[nvec:, at : at + LANES] = (vec - vec_high.astype(jnp.float32)).astype(jnp.bfloat16)
        vec_feat[:nvec, at + LANES : at + 2 * LANES] = vec_high
        vec_feat[nvec:, at + LANES : at + 2 * LANES] = jnp.zeros_like(vec_high)

    def add(number, total):
        there = pl.ds(pl.multiple_of(number * LANES, LANES), LANES)
        square = jnp.dot(row_feat, col_feat[:, there], preferred_element_type=jnp.float32)
        square = jnp.maximum(square, 1e-30)
        svalue = square * lax.rsqrt(square)
        value = (1.0 + svalue + square * (1.0 / 3.0)) * jnp.exp(-svalue)
        high = value.astype(jnp.bfloat16)
        low = (value - high.astype(jnp.float32)).astype(jnp.bfloat16)
        vec = vec_feat[:, pl.ds(pl.multiple_of(number * 2 * LANES, 2 * LANES), 2 * LANES)]
        across = (((1,), (1,)), ((), ()))
        both = jnp.concatenate([high, low], axis=1)
        return total + lax.dot_general(both, vec, across, preferred_element_type=jnp.float32)

    zeros = jnp.zeros((row_feat.shape[0], 2 * nvec), jnp.float32)
    return lax.fori_loop(0, len(pieces), add, zeros, unroll=len(pieces) <= 16)


def scale_of(scale_ref):
    return jnp.broadcast_to(jnp.sqrt(jnp.float32(5.0)) / scale_ref[...], (scale_ref.shape[0], LANES))


def row_features(points_refs, scale):
    points = [row_stack(ref[...] * scale[:, :1]).T.astype(jnp.bfloat16) for ref in points_refs]
    return jnp.concatenate(points, axis=0)


def halves_added(total):
    part = total.T
    nvec = part.shape[0] // 2
    return part[:nvec] + part[nvec:]


def back_kernel(scale_ref, *refs):
    rows_refs, line_ref, out_ref, feats = refs[:-4], refs[-4], refs[-3], refs[-2:]
    scale = scale_of(scale_ref)
    out_ref[...] = halves_added(add_columns(scale, row_features(rows_refs, scale), [line_ref[...]], *feats))


def first_kernel(scale_ref, *refs):
    rows_refs, line_ref, total_ref, feat_ref, scale_out = refs[:-6], *refs[-6:-2]
    scale = scale_of(scale_ref)
    scale_out[...] = scale
    feat_ref[...] = row_features(rows_refs, scale)
    total_ref[...] = add_columns(scale, feat_ref[...], [line_ref[...]], *refs[-2:])


def last_kernel(begin, scale_ref, feat_ref, before_ref, *refs):
    line_refs, out_ref, feats = refs[:-3], refs[-3], refs[-2:]
    here = slice(begin, begin + out_ref.shape[1])
    lines = [ref[...] for ref in line_refs]
    total = before_ref[here, :]
    if lines:
        total = total + add_columns(scale_ref[...], feat_ref[here, :], lines, *feats)
    out_ref[...] = halves_added(total)


def scratch(feat, nvec, cols):
    return [pltpu.VMEM((stack_rows(feat), cols), jnp.bfloat16), pltpu.VMEM((2 * nvec, 2 * cols), jnp.bfloat16)]


def limits(rows, cols):
    return {
        "compiler_params": pltpu.CompilerParams(vmem_limit_bytes=4 * MIB + 4096 * rows + 2048 * cols),
        "cost_estimate": pl.CostEstimate(flops=0, bytes_accessed=0, transcendentals=0),
    }


def per_device(sizes, points, vectors, lengthscales):
    far, mid, pair, rep = sizes
    (feat, width), nvec = points.shape, vectors.shape[0]
    count, rows = feat + nvec, pair * width
    high, wide = packed_shape(count, width)

    def send(item, axis, step):
        return lax.ppermute(item, AXES, permutation(sizes, axis, step))

    def call(body, lines, out_shape, *operands):
        cols = sum(line.shape[0] for line in lines) // count * LANES
        return pl.pallas_call(
            body,
            out_shape=[jax.ShapeDtypeStruct(shape, dtype) for shape, dtype in out_shape],
            scratch_shapes=scratch(feat, nvec, cols),
            **limits(rows, cols),
        )(*operands, *lines)

    block = pl.pallas_call(
        pack_kernel,
        out_shape=jax.ShapeDtypeStruct((high, wide), jnp.float32),
        compiler_params=pltpu.CompilerParams(vmem_limit_bytes=2 * MIB),
    )(jnp.concatenate([points, vectors], axis=0))
    later_points, block = lax.optimization_barrier((points, block))
    blocks = [send(block, "far", k) for k in [*range(2, far), 1][: far - 1]]
    steps = list(range(1, mid * rep))
    by_rows = steps[2:][-1:]
    far_points = [send(later_points, "plane", k) for k in by_rows]
    pair_points = [send(later_points, "pair", k) for k in range(1, pair)]
    blocks, far_points, pair_points = lax.optimization_barrier((blocks, far_points, pair_points))
    line = pl.pallas_call(
        functools.partial(line_kernel, count, width),
        out_shape=jax.ShapeDtypeStruct(line_shape(count, width, far), jnp.float32),
        compiler_params=pltpu.CompilerParams(vmem_limit_bytes=2 * MIB + 16 * far * high * wide),
    )(block, *blocks)

    plane = [send(line, "plane", k) for k in steps if k not in by_rows]
    scale = lengthscales[:, None]
    returned = []
    row_points = [points] + pair_points
    for k, mine in zip(by_rows, far_points):
        others = [send(mine, "pair", j) for j in range(1, pair)]
        (back,) = call(back_kernel, [line], [((nvec, rows), jnp.float32)], scale, mine, *others)
        returned.append(lax.ppermute(back, AXES, reverse(permutation(sizes, "plane", k))))
        row_points, back = lax.optimization_barrier((row_points, back))
    total, row_feat, scale = call(
        first_kernel,
        [line],
        [
            ((rows, 2 * nvec), jnp.float32),
            ((rows, stack_rows(feat)), jnp.bfloat16),
            ((feat, LANES), jnp.float32),
        ],
        scale,
        *row_points,
    )
    total, plane = lax.optimization_barrier((total, plane))

    def finish(k, total):
        body = functools.partial(last_kernel, k * width)
        (part,) = call(body, plane, [((nvec, width), jnp.float32)], scale, row_feat, total)
        return part

    parts = []
    for k in range(1, pair):
        part = finish(k, total)
        total, part, returned = lax.optimization_barrier((total, part, returned))
        parts.append(part)
    result = finish(0, total)
    for item in returned:
        result += item[:, :width]
    for k, part in enumerate(parts, 1):
        back = reverse(permutation(sizes, "pair", k))
        result += lax.ppermute(part, AXES, back)
        for item in returned:
            result += lax.ppermute(item, AXES, back)[:, k * width : (k + 1) * width]
    return result


def solution(mesh):
    sizes = split_blocks(mesh.shape["blk"], mesh.shape["rep"])
    return jax.shard_map(
        functools.partial(per_device, sizes),
        mesh=mesh,
        in_specs=(P(None, AXES), P(None, AXES), P()),
        out_specs=P(None, AXES),
        check_vma=False,
    )
```

```python
import functools

import jax
import jax.numpy as jnp
from jax import lax
from jax.experimental import pallas as pl
from jax.experimental.pallas import tpu as pltpu
from jax.sharding import PartitionSpec as P

AXES = ("blk", "rep")
LANES = 128
MIB = 1024 * 1024


def split_blocks(blk, rep):
    pair = 2 if blk % 2 == 0 else 1
    line = blk // pair
    mid = max(d for d in range(1, line + 1) if line % d == 0 and d * d <= line)
    return line // mid, mid, pair, rep


def partner(index, step, size):
    return index ^ step if size & (size - 1) == 0 else (index + step) % size


def permutation(sizes, axis, step):
    far, mid, pair, rep = sizes
    pairs = []
    for target in range(far * mid * pair * rep):
        rest, q = divmod(target, rep)
        rest, p = divmod(rest, pair)
        f, m = divmod(rest, mid)
        if axis == "far":
            f = partner(f, step, far)
        elif axis == "pair":
            p = partner(p, step, pair)
        else:
            m, q = divmod(partner(m * rep + q, step, mid * rep), rep)
        pairs.append((((f * mid + m) * pair + p) * rep + q, target))
    return pairs


def three_parts(value):
    first = value.astype(jnp.bfloat16).astype(jnp.float32)
    second = (value - first).astype(jnp.bfloat16).astype(jnp.float32)
    return first, second, value - first - second


def stack_rows(feat):
    return 6 * feat + 16


def norm_rows(square, ones_first):
    first, second, third = three_parts(square)
    line = lax.broadcasted_iota(jnp.int32, (16, square.shape[1]), 0)
    at = line - 3 if ones_first else line
    rows = jnp.where(at == 0, first, jnp.where(at == 1, second, jnp.where(at == 2, third, 0.0)))
    ones = (line < 3) if ones_first else (line >= 3) & (line < 6)
    return jnp.where(ones, 1.0, rows)


def column_stack(z):
    a, b, c = three_parts(z)
    square = jnp.sum(z * z, axis=0, keepdims=True)
    return jnp.concatenate([a, a, b, a, c, b, norm_rows(square, False)], axis=0)


def row_stack(z):
    a, b, c = three_parts(z * -2.0)
    square = jnp.sum(z * z, axis=0, keepdims=True)
    return jnp.concatenate([a, b, a, c, a, b, norm_rows(square, True)], axis=0)


def packed_pieces(count, width):
    rest = width % LANES
    return LANES // rest if width > LANES and rest and LANES % rest == 0 and count % 8 == 0 else 0


def packed_shape(count, width):
    fit = packed_pieces(count, width)
    if not fit:
        return count, width
    return width // LANES * count + -(-(count // 8) // fit) * 8, LANES


def pack_kernel(block_ref, out_ref):
    block = block_ref[...]
    count, width = block.shape
    fit = packed_pieces(count, width)
    if not fit:
        out_ref[...] = block
        return
    full = width // LANES
    for k in range(full):
        out_ref[k * count : (k + 1) * count, :] = block[:, k * LANES : (k + 1) * LANES]
    base = full * count
    pieces = [block[at : at + 8, full * LANES :] for at in range(0, count, 8)]
    for first in range(0, len(pieces), fit):
        line = pieces[first : first + fit]
        line += [jnp.zeros_like(line[0])] * (fit - len(line))
        out_ref[base + first // fit * 8 : base + first // fit * 8 + 8, :] = jnp.concatenate(line, axis=1)


def line_shape(count, width, blocks):
    return -(-blocks * width // LANES) * count, LANES


def line_kernel(count, width, *refs):
    block_refs, out_ref = refs[:-1], refs[-1]
    fit = packed_pieces(count, width)
    full, rest = width // LANES, width % LANES
    if not fit:
        joined = [ref[...] for ref in block_refs]
    else:
        joined, at = [], 0
        for ref in block_refs:
            for k in range(full):
                out_ref[at : at + count, :] = ref[k * count : (k + 1) * count, :]
                at += count
            pieces = []
            for k in range(count // 8):
                begin = full * count + k // fit * 8
                pieces.append(ref[begin : begin + 8, k % fit * rest : (k % fit + 1) * rest])
            joined.append(jnp.concatenate(pieces, axis=0))
    begin = 0 if not fit else len(block_refs) * full * count
    over = -sum(item.shape[1] for item in joined) % LANES
    if over:
        joined.append(jnp.zeros((count, over), jnp.float32))
    tails = jnp.concatenate(joined, axis=1)
    for k in range(tails.shape[1] // LANES):
        out_ref[begin + k * count : begin + (k + 1) * count, :] = tails[:, k * LANES : (k + 1) * LANES]


def add_columns(scale, row_feat, lines, col_feat, vec_feat):
    feat = scale.shape[0]
    nvec = vec_feat.shape[0] // 2
    count = feat + nvec
    pieces = [line[at : at + count] for line in lines for at in range(0, line.shape[0], count)]
    for k, piece in enumerate(pieces):
        there = pl.ds(k * LANES, LANES)
        col_feat[:, there] = column_stack(piece[:feat] * scale).astype(jnp.bfloat16)
        vec = piece[feat:]
        vec_high = vec.astype(jnp.bfloat16)
        at = 2 * k * LANES
        vec_feat[:nvec, at : at + LANES] = vec_high
        vec_feat[nvec:, at : at + LANES] = (vec - vec_high.astype(jnp.float32)).astype(jnp.bfloat16)
        vec_feat[:nvec, at + LANES : at + 2 * LANES] = vec_high
        vec_feat[nvec:, at + LANES : at + 2 * LANES] = jnp.zeros_like(vec_high)

    def add(number, total):
        there = pl.ds(pl.multiple_of(number * LANES, LANES), LANES)
        square = jnp.dot(row_feat, col_feat[:, there], preferred_element_type=jnp.float32)
        square = jnp.maximum(square, 1e-30)
        svalue = square * lax.rsqrt(square)
        value = (1.0 + svalue + square * (1.0 / 3.0)) * jnp.exp(-svalue)
        high = value.astype(jnp.bfloat16)
        low = (value - high.astype(jnp.float32)).astype(jnp.bfloat16)
        vec = vec_feat[:, pl.ds(pl.multiple_of(number * 2 * LANES, 2 * LANES), 2 * LANES)]
        across = (((1,), (1,)), ((), ()))
        both = jnp.concatenate([high, low], axis=1)
        return total + lax.dot_general(both, vec, across, preferred_element_type=jnp.float32)

    zeros = jnp.zeros((row_feat.shape[0], 2 * nvec), jnp.float32)
    return lax.fori_loop(0, len(pieces), add, zeros, unroll=len(pieces) <= 16)


def first_kernel(nrow, scale_ref, *refs):
    row_refs, line_refs = refs[:nrow], refs[nrow:-5]
    total_ref, feat_ref, scale_out, *feats = refs[-5:]
    feat, width = row_refs[0].shape
    scale = jnp.broadcast_to(jnp.sqrt(jnp.float32(5.0)) / scale_ref[...], (feat, LANES))
    scale_out[...] = scale
    for k, ref in enumerate(row_refs):
        z = ref[...] * scale[:, :1]
        feat_ref[k * width : (k + 1) * width, :] = row_stack(z).T.astype(jnp.bfloat16)
    lines = [ref[...] for ref in line_refs]
    total_ref[...] = add_columns(scale, feat_ref[...], lines, *feats)


def middle_kernel(scale_ref, feat_ref, before_ref, *refs):
    line_refs, total_ref, feats = refs[:-3], refs[-3], refs[-2:]
    lines = [ref[...] for ref in line_refs]
    total_ref[...] = before_ref[...] + add_columns(scale_ref[...], feat_ref[...], lines, *feats)


def last_kernel(begin, scale_ref, feat_ref, before_ref, *refs):
    line_refs, out_ref, feats = refs[:-3], refs[-3], refs[-2:]
    nvec, width = out_ref.shape
    here = slice(begin, begin + width)
    lines = [ref[...] for ref in line_refs]
    total = before_ref[here, :]
    if lines:
        total = total + add_columns(scale_ref[...], feat_ref[here, :], lines, *feats)
    part = total.T
    out_ref[...] = part[:nvec] + part[nvec:]


def scratch(feat, nvec, cols):
    return [pltpu.VMEM((stack_rows(feat), cols), jnp.bfloat16), pltpu.VMEM((2 * nvec, 2 * cols), jnp.bfloat16)]


def limits(rows, cols):
    return {
        "compiler_params": pltpu.CompilerParams(vmem_limit_bytes=4 * MIB + 4096 * rows + 2048 * cols),
        "cost_estimate": pl.CostEstimate(flops=0, bytes_accessed=0, transcendentals=0),
    }


def per_device(sizes, points, vectors, lengthscales):
    far, mid, pair, rep = sizes
    (feat, width), nvec = points.shape, vectors.shape[0]
    count, rows = feat + nvec, pair * width
    high, wide = packed_shape(count, width)

    def send(item, axis, step):
        return lax.ppermute(item, AXES, permutation(sizes, axis, step))

    def call(body, lines, out_shape, *operands):
        cols = sum(line.shape[0] for line in lines) // count * LANES
        return pl.pallas_call(
            body,
            out_shape=[jax.ShapeDtypeStruct(shape, dtype) for shape, dtype in out_shape],
            scratch_shapes=scratch(feat, nvec, cols),
            **limits(rows, cols),
        )(*operands, *lines)

    block = pl.pallas_call(
        pack_kernel,
        out_shape=jax.ShapeDtypeStruct((high, wide), jnp.float32),
        compiler_params=pltpu.CompilerParams(vmem_limit_bytes=2 * MIB),
    )(jnp.concatenate([points, vectors], axis=0))
    later_points, block = lax.optimization_barrier((points, block))
    blocks = [send(block, "far", k) for k in [*range(2, far), 1][: far - 1]]
    row_points = [send(later_points, "pair", k) for k in range(1, pair)]
    blocks, row_points = lax.optimization_barrier((blocks, row_points))
    line = pl.pallas_call(
        functools.partial(line_kernel, count, width),
        out_shape=jax.ShapeDtypeStruct(line_shape(count, width, far), jnp.float32),
        compiler_params=pltpu.CompilerParams(vmem_limit_bytes=2 * MIB + 16 * far * high * wide),
    )(block, *blocks)
    plane = [send(line, "plane", k) for k in reversed(range(1, mid * rep))]
    total, row_feat, scale = call(
        functools.partial(first_kernel, pair),
        [line],
        [((rows, 2 * nvec), jnp.float32), ((rows, stack_rows(feat)), jnp.bfloat16), ((feat, LANES), jnp.float32)],
        lengthscales[:, None],
        points,
        *row_points,
    )
    early, late = plane[:-2], plane[-2:]
    if early:
        total, early = lax.optimization_barrier((total, early))
        (total,) = call(middle_kernel, early, [((rows, 2 * nvec), jnp.float32)], scale, row_feat, total)
    total, late = lax.optimization_barrier((total, late))

    def finish(k, total):
        body = functools.partial(last_kernel, k * width)
        (part,) = call(body, late, [((nvec, width), jnp.float32)], scale, row_feat, total)
        return part

    parts = []
    for k in range(1, pair):
        part = finish(k, total)
        total, part = lax.optimization_barrier((total, part))
        parts.append(part)
    result = finish(0, total)
    for k, part in enumerate(parts, 1):
        back = [(target, source) for source, target in permutation(sizes, "pair", k)]
        result = result + lax.ppermute(part, AXES, back)
    return result


def solution(mesh):
    sizes = split_blocks(mesh.shape["blk"], mesh.shape["rep"])
    return jax.shard_map(
        functools.partial(per_device, sizes),
        mesh=mesh,
        in_specs=(P(None, AXES), P(None, AXES), P()),
        out_specs=P(None, AXES),
        check_vma=False,
    )
```

```python
import functools

import jax
import jax.numpy as jnp
from jax import lax
from jax.experimental import pallas as pl
from jax.experimental.pallas import tpu as pltpu
from jax.sharding import PartitionSpec as P

AXES = ("blk", "rep")
LANES = 128
MIB = 1024 * 1024


def split_blocks(blk, rep):
    pair = 2 if blk % 2 == 0 else 1
    line = blk // pair
    mid = max(d for d in range(1, line + 1) if line % d == 0 and d * d <= line)
    return line // mid, mid, pair, rep


def partner(index, step, size):
    return index ^ step if size & (size - 1) == 0 else (index + step) % size


def permutation(sizes, axis, step):
    far, mid, pair, rep = sizes
    pairs = []
    for target in range(far * mid * pair * rep):
        rest, q = divmod(target, rep)
        rest, p = divmod(rest, pair)
        f, m = divmod(rest, mid)
        if axis == "pair":
            p = partner(p, step, pair)
        else:
            p = pair - 1 - p
            if axis == "far":
                f = partner(f, step, far)
            else:
                m, q = divmod(partner(m * rep + q, step, mid * rep), rep)
        pairs.append((((f * mid + m) * pair + p) * rep + q, target))
    return pairs


def three_parts(value):
    first = value.astype(jnp.bfloat16).astype(jnp.float32)
    second = (value - first).astype(jnp.bfloat16).astype(jnp.float32)
    return first, second, value - first - second


def stack_rows(feat):
    return 6 * feat + 16


def norm_rows(square, ones_first):
    first, second, third = three_parts(square)
    line = lax.broadcasted_iota(jnp.int32, (16, square.shape[1]), 0)
    at = line - 3 if ones_first else line
    rows = jnp.where(at == 0, first, jnp.where(at == 1, second, jnp.where(at == 2, third, 0.0)))
    ones = (line < 3) if ones_first else (line >= 3) & (line < 6)
    return jnp.where(ones, 1.0, rows)


def column_stack(z):
    a, b, c = three_parts(z)
    square = jnp.sum(z * z, axis=0, keepdims=True)
    return jnp.concatenate([a, a, b, a, c, b, norm_rows(square, False)], axis=0)


def row_stack(z):
    a, b, c = three_parts(z * -2.0)
    square = jnp.sum(z * z, axis=0, keepdims=True)
    return jnp.concatenate([a, b, a, c, a, b, norm_rows(square, True)], axis=0)


def packed_pieces(count, width):
    rest = width % LANES
    return LANES // rest if width > LANES and rest and LANES % rest == 0 and count % 8 == 0 else 0


def packed_shape(count, width):
    fit = packed_pieces(count, width)
    if not fit:
        return count, width
    return width // LANES * count + -(-(count // 8) // fit) * 8, LANES


def pack_kernel(block_ref, out_ref):
    block = block_ref[...]
    count, width = block.shape
    fit = packed_pieces(count, width)
    if not fit:
        out_ref[...] = block
        return
    full = width // LANES
    for k in range(full):
        out_ref[k * count : (k + 1) * count, :] = block[:, k * LANES : (k + 1) * LANES]
    base = full * count
    pieces = [block[at : at + 8, full * LANES :] for at in range(0, count, 8)]
    for first in range(0, len(pieces), fit):
        line = pieces[first : first + fit]
        line += [jnp.zeros_like(line[0])] * (fit - len(line))
        out_ref[base + first // fit * 8 : base + first // fit * 8 + 8, :] = jnp.concatenate(line, axis=1)


def line_shape(count, width, blocks):
    return -(-blocks * width // LANES) * count, LANES


def line_kernel(count, width, *refs):
    block_refs, out_ref = refs[:-1], refs[-1]
    fit = packed_pieces(count, width)
    full, rest = width // LANES, width % LANES
    if not fit:
        joined = [ref[...] for ref in block_refs]
    else:
        joined, at = [], 0
        for ref in block_refs:
            for k in range(full):
                out_ref[at : at + count, :] = ref[k * count : (k + 1) * count, :]
                at += count
            pieces = []
            for k in range(count // 8):
                begin = full * count + k // fit * 8
                pieces.append(ref[begin : begin + 8, k % fit * rest : (k % fit + 1) * rest])
            joined.append(jnp.concatenate(pieces, axis=0))
    begin = 0 if not fit else len(block_refs) * full * count
    over = -sum(item.shape[1] for item in joined) % LANES
    if over:
        joined.append(jnp.zeros((count, over), jnp.float32))
    tails = jnp.concatenate(joined, axis=1)
    for k in range(tails.shape[1] // LANES):
        out_ref[begin + k * count : begin + (k + 1) * count, :] = tails[:, k * LANES : (k + 1) * LANES]


def add_columns(scale, row_feat, lines, col_feat, vec_feat):
    feat = scale.shape[0]
    nvec = vec_feat.shape[0] // 2
    count = feat + nvec
    pieces = [line[at : at + count] for line in lines for at in range(0, line.shape[0], count)]
    for k, piece in enumerate(pieces):
        there = pl.ds(k * LANES, LANES)
        col_feat[:, there] = column_stack(piece[:feat] * scale).astype(jnp.bfloat16)
        vec = piece[feat:]
        vec_high = vec.astype(jnp.bfloat16)
        at = 2 * k * LANES
        vec_feat[:nvec, at : at + LANES] = vec_high
        vec_feat[nvec:, at : at + LANES] = (vec - vec_high.astype(jnp.float32)).astype(jnp.bfloat16)
        vec_feat[:nvec, at + LANES : at + 2 * LANES] = vec_high
        vec_feat[nvec:, at + LANES : at + 2 * LANES] = jnp.zeros_like(vec_high)

    def add(number, total):
        there = pl.ds(pl.multiple_of(number * LANES, LANES), LANES)
        square = jnp.dot(row_feat, col_feat[:, there], preferred_element_type=jnp.float32)
        square = jnp.maximum(square, 1e-30)
        svalue = square * lax.rsqrt(square)
        value = (1.0 + svalue + square * (1.0 / 3.0)) * jnp.exp(-svalue)
        high = value.astype(jnp.bfloat16)
        low = (value - high.astype(jnp.float32)).astype(jnp.bfloat16)
        vec = vec_feat[:, pl.ds(pl.multiple_of(number * 2 * LANES, 2 * LANES), 2 * LANES)]
        across = (((1,), (1,)), ((), ()))
        both = jnp.concatenate([high, low], axis=1)
        return total + lax.dot_general(both, vec, across, preferred_element_type=jnp.float32)

    zeros = jnp.zeros((row_feat.shape[0], 2 * nvec), jnp.float32)
    return lax.fori_loop(0, len(pieces), add, zeros, unroll=len(pieces) <= 16)


def first_kernel(nrow, scale_ref, *refs):
    row_refs, line_refs = refs[:nrow], refs[nrow:-5]
    total_ref, feat_ref, scale_out, *feats = refs[-5:]
    feat, width = row_refs[0].shape
    scale = jnp.broadcast_to(jnp.sqrt(jnp.float32(5.0)) / scale_ref[...], (feat, LANES))
    scale_out[...] = scale
    for k, ref in enumerate(row_refs):
        z = ref[...] * scale[:, :1]
        feat_ref[k * width : (k + 1) * width, :] = row_stack(z).T.astype(jnp.bfloat16)
    lines = [ref[...] for ref in line_refs]
    total_ref[...] = add_columns(scale, feat_ref[...], lines, *feats)


def middle_kernel(scale_ref, feat_ref, before_ref, *refs):
    line_refs, total_ref, feats = refs[:-3], refs[-3], refs[-2:]
    lines = [ref[...] for ref in line_refs]
    total_ref[...] = before_ref[...] + add_columns(scale_ref[...], feat_ref[...], lines, *feats)


def last_kernel(begin, scale_ref, feat_ref, before_ref, *refs):
    line_refs, out_ref, feats = refs[:-3], refs[-3], refs[-2:]
    nvec, width = out_ref.shape
    here = slice(begin, begin + width)
    lines = [ref[...] for ref in line_refs]
    total = before_ref[here, :]
    if lines:
        total = total + add_columns(scale_ref[...], feat_ref[here, :], lines, *feats)
    part = total.T
    out_ref[...] = part[:nvec] + part[nvec:]


def scratch(feat, nvec, cols):
    return [pltpu.VMEM((stack_rows(feat), cols), jnp.bfloat16), pltpu.VMEM((2 * nvec, 2 * cols), jnp.bfloat16)]


def limits(rows, cols):
    return {
        "compiler_params": pltpu.CompilerParams(vmem_limit_bytes=4 * MIB + 4096 * rows + 2048 * cols),
        "cost_estimate": pl.CostEstimate(flops=0, bytes_accessed=0, transcendentals=0),
    }


def per_device(sizes, points, vectors, lengthscales):
    far, mid, pair, rep = sizes
    (feat, width), nvec = points.shape, vectors.shape[0]
    count, rows = feat + nvec, pair * width
    high, wide = packed_shape(count, width)

    def send(item, axis, step):
        return lax.ppermute(item, AXES, permutation(sizes, axis, step))

    def call(body, lines, out_shape, *operands):
        cols = sum(line.shape[0] for line in lines) // count * LANES
        return pl.pallas_call(
            body,
            out_shape=[jax.ShapeDtypeStruct(shape, dtype) for shape, dtype in out_shape],
            scratch_shapes=scratch(feat, nvec, cols),
            **limits(rows, cols),
        )(*operands, *lines)

    block = pl.pallas_call(
        pack_kernel,
        out_shape=jax.ShapeDtypeStruct((high, wide), jnp.float32),
        compiler_params=pltpu.CompilerParams(vmem_limit_bytes=2 * MIB),
    )(jnp.concatenate([points, vectors], axis=0))
    later_points, block = lax.optimization_barrier((points, block))
    blocks = [send(block, "far", k) for k in [*range(2, far), 1][: far - 1]]
    row_points = [send(later_points, "pair", k) for k in range(1, pair)]
    blocks, row_points = lax.optimization_barrier((blocks, row_points))
    line = pl.pallas_call(
        functools.partial(line_kernel, count, width),
        out_shape=jax.ShapeDtypeStruct(line_shape(count, width, far), jnp.float32),
        compiler_params=pltpu.CompilerParams(vmem_limit_bytes=2 * MIB + 16 * far * high * wide),
    )(block, *blocks)
    plane = [send(line, "plane", k) for k in reversed(range(1, mid * rep))]
    total, row_feat, scale = call(
        functools.partial(first_kernel, pair),
        [line],
        [((rows, 2 * nvec), jnp.float32), ((rows, stack_rows(feat)), jnp.bfloat16), ((feat, LANES), jnp.float32)],
        lengthscales[:, None],
        points,
        *row_points,
    )
    early, late = plane[:-2], plane[-2:]
    if early:
        total, early = lax.optimization_barrier((total, early))
        (total,) = call(middle_kernel, early, [((rows, 2 * nvec), jnp.float32)], scale, row_feat, total)
    total, late = lax.optimization_barrier((total, late))

    def finish(k, total):
        body = functools.partial(last_kernel, k * width)
        (part,) = call(body, late, [((nvec, width), jnp.float32)], scale, row_feat, total)
        return part

    parts = []
    for k in range(1, pair):
        part = finish(k, total)
        total, part = lax.optimization_barrier((total, part))
        parts.append(part)
    result = finish(0, total)
    for k, part in enumerate(parts, 1):
        back = [(target, source) for source, target in permutation(sizes, "pair", k)]
        result = result + lax.ppermute(part, AXES, back)
    return result


def solution(mesh):
    sizes = split_blocks(mesh.shape["blk"], mesh.shape["rep"])
    return jax.shard_map(
        functools.partial(per_device, sizes),
        mesh=mesh,
        in_specs=(P(None, AXES), P(None, AXES), P()),
        out_specs=P(None, AXES),
        check_vma=False,
    )
```

```python
import functools
import math

import jax
import jax.numpy as jnp
from jax import lax
from jax.experimental import pallas as pl
from jax.experimental.pallas import tpu as pltpu
from jax.sharding import PartitionSpec as P

AXES = ("blk", "rep")
LANES = 128
MIB = 1024 * 1024
LN2 = math.log(2.0)


def split_blocks(blk, rep):
    pair = 2 if blk % 2 == 0 else 1
    line = blk // pair
    mid = max(d for d in range(1, line + 1) if line % d == 0 and d * d <= line)
    return line // mid, mid, pair, rep


def partner(index, step, size):
    return index ^ step if size & (size - 1) == 0 else (index + step) % size


def permutation(sizes, axis, step):
    far, mid, pair, rep = sizes
    pairs = []
    for target in range(far * mid * pair * rep):
        rest, q = divmod(target, rep)
        rest, p = divmod(rest, pair)
        f, m = divmod(rest, mid)
        if axis == "far":
            f = partner(f, step, far)
        elif axis == "pair":
            p = partner(p, step, pair)
        else:
            m, q = divmod(partner(m * rep + q, step, mid * rep), rep)
        pairs.append((((f * mid + m) * pair + p) * rep + q, target))
    return pairs


def three_parts(value):
    first = value.astype(jnp.bfloat16).astype(jnp.float32)
    second = (value - first).astype(jnp.bfloat16).astype(jnp.float32)
    return first, second, value - first - second


def stack_rows(feat):
    return 6 * feat + 16


def norm_rows(square, ones_first):
    first, second, third = three_parts(square)
    line = lax.broadcasted_iota(jnp.int32, (16, square.shape[1]), 0)
    at = line - 3 if ones_first else line
    rows = jnp.where(at == 0, first, jnp.where(at == 1, second, jnp.where(at == 2, third, 0.0)))
    ones = (line < 3) if ones_first else (line >= 3) & (line < 6)
    return jnp.where(ones, 1.0, rows)


def column_stack(z):
    a, b, c = three_parts(z)
    square = jnp.sum(z * z, axis=0, keepdims=True)
    return jnp.concatenate([a, a, b, a, c, b, norm_rows(square, False)], axis=0)


def row_stack(z):
    a, b, c = three_parts(z * -2.0)
    square = jnp.sum(z * z, axis=0, keepdims=True)
    return jnp.concatenate([a, b, a, c, a, b, norm_rows(square, True)], axis=0)


def packed_pieces(count, width):
    rest = width % LANES
    return LANES // rest if width > LANES and rest and LANES % rest == 0 and count % 8 == 0 else 0


def packed_shape(count, width):
    fit = packed_pieces(count, width)
    if not fit:
        return count, width
    return width // LANES * count + -(-(count // 8) // fit) * 8, LANES


def pack_kernel(block_ref, out_ref):
    block = block_ref[...]
    count, width = block.shape
    fit = packed_pieces(count, width)
    if not fit:
        out_ref[...] = block
        return
    full = width // LANES
    for k in range(full):
        out_ref[k * count : (k + 1) * count, :] = block[:, k * LANES : (k + 1) * LANES]
    base = full * count
    pieces = [block[at : at + 8, full * LANES :] for at in range(0, count, 8)]
    for first in range(0, len(pieces), fit):
        line = pieces[first : first + fit]
        line += [jnp.zeros_like(line[0])] * (fit - len(line))
        out_ref[base + first // fit * 8 : base + first // fit * 8 + 8, :] = jnp.concatenate(line, axis=1)


def line_shape(count, width, blocks):
    return -(-blocks * width // LANES) * count, LANES


def line_kernel(count, width, *refs):
    block_refs, out_ref = refs[:-1], refs[-1]
    fit = packed_pieces(count, width)
    full, rest = width // LANES, width % LANES
    if not fit:
        joined = [ref[...] for ref in block_refs]
    else:
        joined, at = [], 0
        for ref in block_refs:
            for k in range(full):
                out_ref[at : at + count, :] = ref[k * count : (k + 1) * count, :]
                at += count
            pieces = []
            for k in range(count // 8):
                begin = full * count + k // fit * 8
                pieces.append(ref[begin : begin + 8, k % fit * rest : (k % fit + 1) * rest])
            joined.append(jnp.concatenate(pieces, axis=0))
    begin = 0 if not fit else len(block_refs) * full * count
    over = -sum(item.shape[1] for item in joined) % LANES
    if over:
        joined.append(jnp.zeros((count, over), jnp.float32))
    tails = jnp.concatenate(joined, axis=1)
    for k in range(tails.shape[1] // LANES):
        out_ref[begin + k * count : begin + (k + 1) * count, :] = tails[:, k * LANES : (k + 1) * LANES]


def piece_product(scale, row_feat, piece):
    feat = scale.shape[0]
    col_feat = column_stack(piece[:feat] * scale).astype(jnp.bfloat16)
    vec = piece[feat:]
    vec_high = vec.astype(jnp.bfloat16)
    vec_low = (vec - vec_high.astype(jnp.float32)).astype(jnp.bfloat16)
    for_high = jnp.concatenate([vec_high, vec_low], axis=0)
    for_low = jnp.concatenate([vec_high, jnp.zeros_like(vec_low)], axis=0)
    square = jnp.dot(row_feat, col_feat, preferred_element_type=jnp.float32)
    square = jnp.maximum(square, 1e-30)
    root = square * lax.rsqrt(square)
    value = (1.0 + LN2 * root + (LN2 * LN2 / 3.0) * square) * jnp.exp2(-root)
    high = value.astype(jnp.bfloat16)
    low = (value - high.astype(jnp.float32)).astype(jnp.bfloat16)
    both = jnp.concatenate([high, low], axis=1)
    vec = jnp.concatenate([for_high, for_low], axis=1)
    return lax.dot_general(both, vec, (((1,), (1,)), ((), ())), preferred_element_type=jnp.float32)


def add_columns(total, scale, row_feat, line_refs, count):
    pieces = [ref.shape[0] // count for ref in line_refs]
    for ref, number in zip(line_refs, pieces):
        if sum(pieces) <= 16:
            for k in range(number):
                total = total + piece_product(scale, row_feat, ref[k * count : (k + 1) * count, :])
        else:

            def add(k, total, ref=ref):
                piece = ref[pl.ds(pl.multiple_of(k * count, 8), count), :]
                return total + piece_product(scale, row_feat, piece)

            total = lax.fori_loop(0, number, add, total)
    return total


def first_kernel(nrow, count, scale_ref, *refs):
    row_refs, line_refs = refs[:nrow], refs[nrow:-3]
    total_ref, feat_ref, scale_out = refs[-3:]
    feat, width = row_refs[0].shape
    scale = jnp.broadcast_to(jnp.sqrt(jnp.float32(5.0)) / LN2 / scale_ref[...], (feat, LANES))
    scale_out[...] = scale
    for k, ref in enumerate(row_refs):
        z = ref[...] * scale[:, :1]
        feat_ref[k * width : (k + 1) * width, :] = row_stack(z).T.astype(jnp.bfloat16)
    zeros = jnp.zeros(total_ref.shape, jnp.float32)
    total_ref[...] = add_columns(zeros, scale, feat_ref[...], line_refs, count)


def middle_kernel(count, scale_ref, feat_ref, before_ref, *refs):
    refs[-1][...] = add_columns(before_ref[...], scale_ref[...], feat_ref[...], refs[:-1], count)


def last_kernel(count, begin, scale_ref, feat_ref, before_ref, *refs):
    nvec, width = refs[-1].shape
    here = slice(begin, begin + width)
    part = add_columns(before_ref[here, :], scale_ref[...], feat_ref[here, :], refs[:-1], count).T
    refs[-1][...] = part[:nvec] + part[nvec:]


def limits(rows, cols):
    return {
        "compiler_params": pltpu.CompilerParams(vmem_limit_bytes=4 * MIB + 4096 * rows + 2048 * cols),
        "cost_estimate": pl.CostEstimate(flops=0, bytes_accessed=0, transcendentals=0),
    }


def per_device(sizes, points, vectors, lengthscales):
    far, mid, pair, rep = sizes
    (feat, width), nvec = points.shape, vectors.shape[0]
    count, rows = feat + nvec, pair * width
    high, wide = packed_shape(count, width)

    def send(item, axis, step):
        return lax.ppermute(item, AXES, permutation(sizes, axis, step))

    def call(body, lines, out_shape, *operands):
        cols = sum(line.shape[0] for line in lines) // count * LANES
        return pl.pallas_call(
            body,
            out_shape=[jax.ShapeDtypeStruct(shape, dtype) for shape, dtype in out_shape],
            **limits(rows, cols),
        )(*operands, *lines)

    block = pl.pallas_call(
        pack_kernel,
        out_shape=jax.ShapeDtypeStruct((high, wide), jnp.float32),
        compiler_params=pltpu.CompilerParams(vmem_limit_bytes=2 * MIB),
    )(jnp.concatenate([points, vectors], axis=0))
    later_points, block = lax.optimization_barrier((points, block))
    blocks = [send(block, "far", k) for k in [*range(2, far), 1][: far - 1]]
    row_points = [send(later_points, "pair", k) for k in range(1, pair)]
    blocks, row_points = lax.optimization_barrier((blocks, row_points))
    line = pl.pallas_call(
        functools.partial(line_kernel, count, width),
        out_shape=jax.ShapeDtypeStruct(line_shape(count, width, far), jnp.float32),
        compiler_params=pltpu.CompilerParams(vmem_limit_bytes=2 * MIB + 16 * far * high * wide),
    )(block, *blocks)
    plane = [send(line, "plane", k) for k in reversed(range(1, mid * rep))]
    total, row_feat, scale = call(
        functools.partial(first_kernel, pair, count),
        [line],
        [((rows, 2 * nvec), jnp.float32), ((rows, stack_rows(feat)), jnp.bfloat16), ((feat, LANES), jnp.float32)],
        lengthscales[:, None],
        points,
        *row_points,
    )
    early, late = plane[:-2], plane[-2:]
    if early:
        total, early = lax.optimization_barrier((total, early))
        (total,) = call(functools.partial(middle_kernel, count), early, [((rows, 2 * nvec), jnp.float32)], scale, row_feat, total)
    total, late = lax.optimization_barrier((total, late))

    def finish(k, total):
        body = functools.partial(last_kernel, count, k * width)
        (part,) = call(body, late, [((nvec, width), jnp.float32)], scale, row_feat, total)
        return part

    parts = []
    for k in range(1, pair):
        part = finish(k, total)
        total, part = lax.optimization_barrier((total, part))
        parts.append(part)
    result = finish(0, total)
    for k, part in enumerate(parts, 1):
        back = [(target, source) for source, target in permutation(sizes, "pair", k)]
        result = result + lax.ppermute(part, AXES, back)
    return result


def solution(mesh):
    sizes = split_blocks(mesh.shape["blk"], mesh.shape["rep"])
    return jax.shard_map(
        functools.partial(per_device, sizes),
        mesh=mesh,
        in_specs=(P(None, AXES), P(None, AXES), P()),
        out_specs=P(None, AXES),
        check_vma=False,
    )
```

```python
import functools
import math

import jax
import jax.numpy as jnp
from jax import lax
from jax.experimental import pallas as pl
from jax.experimental.pallas import tpu as pltpu
from jax.sharding import PartitionSpec as P

AXES = ("blk", "rep")
LANES = 128
MIB = 1024 * 1024


def split_blocks(blk, rep):
    pair = 2 if blk % 2 == 0 else 1
    line = blk // pair
    mid = max(d for d in range(1, line + 1) if line % d == 0 and d * d <= line)
    return line // mid, mid, pair, rep


def partner(index, step, size):
    return index ^ step if size & (size - 1) == 0 else (index + step) % size


def permutation(sizes, axis, step):
    far, mid, pair, rep = sizes
    pairs = []
    for target in range(far * mid * pair * rep):
        rest, q = divmod(target, rep)
        rest, p = divmod(rest, pair)
        f, m = divmod(rest, mid)
        if axis == "far":
            f = partner(f, step, far)
        elif axis == "pair":
            p = partner(p, step, pair)
        else:
            m, q = divmod(partner(m * rep + q, step, mid * rep), rep)
        pairs.append((((f * mid + m) * pair + p) * rep + q, target))
    return pairs


def three_parts(value):
    first = value.astype(jnp.bfloat16).astype(jnp.float32)
    second = (value - first).astype(jnp.bfloat16).astype(jnp.float32)
    return first, second, value - first - second


def stack_rows(feat):
    return 6 * feat + 16


def norm_rows(values):
    line = lax.broadcasted_iota(jnp.int32, (16, values[0].shape[1]), 0)
    rows = jnp.zeros(line.shape, jnp.float32)
    for k, value in enumerate(values):
        rows = jnp.where(line == k, value, rows)
    return rows


def column_stack(z):
    a, b, c = three_parts(z)
    square = jnp.sum(z * z, axis=0, keepdims=True)
    return jnp.concatenate([a, a, b, a, c, b, norm_rows([*three_parts(square), 1.0, 1.0, 1.0, 1.0])], axis=0)


def row_stack(z, factor, constant):
    a, b, c = three_parts(z * (-2.0 * factor))
    square = three_parts(factor * jnp.sum(z * z, axis=0, keepdims=True))
    ones = jnp.full_like(square[0], factor)
    return jnp.concatenate([a, b, a, c, a, b, norm_rows([ones, ones, ones, *square, constant])], axis=0)


def packed_pieces(count, width):
    rest = width % LANES
    return LANES // rest if width > LANES and rest and LANES % rest == 0 and count % 8 == 0 else 0


def packed_shape(count, width):
    fit = packed_pieces(count, width)
    if not fit:
        return count, width
    return width // LANES * count + -(-(count // 8) // fit) * 8, LANES


def pack_kernel(block_ref, out_ref):
    block = block_ref[...]
    count, width = block.shape
    fit = packed_pieces(count, width)
    if not fit:
        out_ref[...] = block
        return
    full = width // LANES
    for k in range(full):
        out_ref[k * count : (k + 1) * count, :] = block[:, k * LANES : (k + 1) * LANES]
    base = full * count
    pieces = [block[at : at + 8, full * LANES :] for at in range(0, count, 8)]
    for first in range(0, len(pieces), fit):
        line = pieces[first : first + fit]
        line += [jnp.zeros_like(line[0])] * (fit - len(line))
        out_ref[base + first // fit * 8 : base + first // fit * 8 + 8, :] = jnp.concatenate(line, axis=1)


def line_shape(count, width, blocks):
    return -(-blocks * width // LANES) * count, LANES


def line_kernel(count, width, *refs):
    block_refs, out_ref = refs[:-1], refs[-1]
    fit = packed_pieces(count, width)
    full, rest = width // LANES, width % LANES
    if not fit:
        joined = [ref[...] for ref in block_refs]
    else:
        joined, at = [], 0
        for ref in block_refs:
            for k in range(full):
                out_ref[at : at + count, :] = ref[k * count : (k + 1) * count, :]
                at += count
            pieces = []
            for k in range(count // 8):
                begin = full * count + k // fit * 8
                pieces.append(ref[begin : begin + 8, k % fit * rest : (k % fit + 1) * rest])
            joined.append(jnp.concatenate(pieces, axis=0))
    begin = 0 if not fit else len(block_refs) * full * count
    over = -sum(item.shape[1] for item in joined) % LANES
    if over:
        joined.append(jnp.zeros((count, over), jnp.float32))
    tails = jnp.concatenate(joined, axis=1)
    for k in range(tails.shape[1] // LANES):
        out_ref[begin + k * count : begin + (k + 1) * count, :] = tails[:, k * LANES : (k + 1) * LANES]


def piece_values(scale, row_feat, piece):
    feat = scale.shape[0]
    rows = row_feat.shape[0] // 2
    col_feat = column_stack(piece[:feat] * scale).astype(jnp.bfloat16)
    vec = piece[feat:]
    vec_high = vec.astype(jnp.bfloat16)
    vec_low = (vec - vec_high.astype(jnp.float32)).astype(jnp.bfloat16)
    for_high = jnp.concatenate([vec_high, vec_low], axis=0)
    for_low = jnp.concatenate([vec_high, jnp.zeros_like(vec_low)], axis=0)
    both = jnp.dot(row_feat, col_feat, preferred_element_type=jnp.float32)
    square = jnp.maximum(both[:rows], 1e-30)
    root = square * lax.rsqrt(square)
    value = (both[rows:] + root) * jnp.exp2(root * (-1.0 / math.log(2.0)))
    high = value.astype(jnp.bfloat16)
    low = (value - high.astype(jnp.float32)).astype(jnp.bfloat16)
    return [high, low], [for_high, for_low]


def add_columns(total, scale, row_feat, line_refs, count):
    def products(pieces):
        values, vectors = [], []
        for piece in pieces:
            value, vector = piece_values(scale, row_feat, piece)
            values += value
            vectors += vector
        values, vectors = jnp.concatenate(values, axis=1), jnp.concatenate(vectors, axis=1)
        return lax.dot_general(values, vectors, (((1,), (1,)), ((), ())), preferred_element_type=jnp.float32)

    numbers = [ref.shape[0] // count for ref in line_refs]
    if sum(numbers) <= 16:
        pieces = [ref[k * count : (k + 1) * count, :] for ref, number in zip(line_refs, numbers) for k in range(number)]
        return total + products(pieces)
    for ref, number in zip(line_refs, numbers):

        def add(k, total, ref=ref):
            return total + products([ref[pl.ds(pl.multiple_of(k * count, 8), count), :]])

        total = lax.fori_loop(0, number, add, total)
    return total


def first_kernel(nrow, count, scale_ref, *refs):
    row_refs, line_refs = refs[:nrow], refs[nrow:-3]
    total_ref, feat_ref, scale_out = refs[-3:]
    feat, width = row_refs[0].shape
    scale = jnp.broadcast_to(jnp.sqrt(jnp.float32(5.0 / 3.0)) / scale_ref[...], (feat, LANES))
    scale_out[...] = scale
    for k, ref in enumerate(row_refs):
        z = ref[...] * scale[:, :1]
        begin = 2 * k * width
        feat_ref[begin : begin + width, :] = row_stack(z, 3.0, 0.0).T.astype(jnp.bfloat16)
        feat_ref[begin + width : begin + 2 * width, :] = row_stack(z, 1.0, 1.0).T.astype(jnp.bfloat16)
    for k in range(nrow):
        here = slice(k * width, (k + 1) * width)
        zeros = jnp.zeros((width, total_ref.shape[1]), jnp.float32)
        rows = feat_ref[2 * k * width : 2 * (k + 1) * width, :]
        total_ref[here, :] = add_columns(zeros, scale, rows, line_refs, count)


def middle_kernel(nrow, count, scale_ref, feat_ref, before_ref, *refs):
    width = before_ref.shape[0] // nrow
    for k in range(nrow):
        here = slice(k * width, (k + 1) * width)
        rows = feat_ref[2 * k * width : 2 * (k + 1) * width, :]
        refs[-1][here, :] = add_columns(before_ref[here, :], scale_ref[...], rows, refs[:-1], count)


def last_kernel(count, begin, scale_ref, feat_ref, before_ref, *refs):
    nvec, width = refs[-1].shape
    here = slice(begin, begin + width)
    rows = feat_ref[2 * begin : 2 * (begin + width), :]
    part = add_columns(before_ref[here, :], scale_ref[...], rows, refs[:-1], count).T
    refs[-1][...] = part[:nvec] + part[nvec:]


def limits(rows, cols):
    return {
        "compiler_params": pltpu.CompilerParams(vmem_limit_bytes=4 * MIB + 4096 * rows + 2048 * cols),
        "cost_estimate": pl.CostEstimate(flops=0, bytes_accessed=0, transcendentals=0),
    }


def per_device(sizes, points, vectors, lengthscales):
    far, mid, pair, rep = sizes
    (feat, width), nvec = points.shape, vectors.shape[0]
    count, rows = feat + nvec, pair * width
    high, wide = packed_shape(count, width)

    def send(item, axis, step):
        return lax.ppermute(item, AXES, permutation(sizes, axis, step))

    def call(body, lines, out_shape, *operands):
        cols = sum(line.shape[0] for line in lines) // count * LANES
        return pl.pallas_call(
            body,
            out_shape=[jax.ShapeDtypeStruct(shape, dtype) for shape, dtype in out_shape],
            **limits(rows, cols),
        )(*operands, *lines)

    block = pl.pallas_call(
        pack_kernel,
        out_shape=jax.ShapeDtypeStruct((high, wide), jnp.float32),
        compiler_params=pltpu.CompilerParams(vmem_limit_bytes=2 * MIB),
    )(jnp.concatenate([points, vectors], axis=0))
    later_points, block = lax.optimization_barrier((points, block))
    blocks = [send(block, "far", k) for k in [*range(2, far), 1][: far - 1]]
    row_points = [send(later_points, "pair", k) for k in range(1, pair)]
    blocks, row_points = lax.optimization_barrier((blocks, row_points))
    line = pl.pallas_call(
        functools.partial(line_kernel, count, width),
        out_shape=jax.ShapeDtypeStruct(line_shape(count, width, far), jnp.float32),
        compiler_params=pltpu.CompilerParams(vmem_limit_bytes=2 * MIB + 16 * far * high * wide),
    )(block, *blocks)
    plane = [send(line, "plane", k) for k in reversed(range(1, mid * rep))]
    total, row_feat, scale = call(
        functools.partial(first_kernel, pair, count),
        [line],
        [((rows, 2 * nvec), jnp.float32), ((2 * rows, stack_rows(feat)), jnp.bfloat16), ((feat, LANES), jnp.float32)],
        lengthscales[:, None],
        points,
        *row_points,
    )
    early, late = plane[:-2], plane[-2:]
    if early:
        total, early = lax.optimization_barrier((total, early))
        (total,) = call(functools.partial(middle_kernel, pair, count), early, [((rows, 2 * nvec), jnp.float32)], scale, row_feat, total)
    total, late = lax.optimization_barrier((total, late))

    def finish(k, total):
        body = functools.partial(last_kernel, count, k * width)
        (part,) = call(body, late, [((nvec, width), jnp.float32)], scale, row_feat, total)
        return part

    parts = []
    for k in range(1, pair):
        part = finish(k, total)
        total, part = lax.optimization_barrier((total, part))
        parts.append(part)
    result = finish(0, total)
    for k, part in enumerate(parts, 1):
        back = [(target, source) for source, target in permutation(sizes, "pair", k)]
        result = result + lax.ppermute(part, AXES, back)
    return result


def solution(mesh):
    sizes = split_blocks(mesh.shape["blk"], mesh.shape["rep"])
    return jax.shard_map(
        functools.partial(per_device, sizes),
        mesh=mesh,
        in_specs=(P(None, AXES), P(None, AXES), P()),
        out_specs=P(None, AXES),
        check_vma=False,
    )
```

```python
import functools
import math

import jax
import jax.numpy as jnp
from jax import lax
from jax.experimental import pallas as pl
from jax.experimental.pallas import tpu as pltpu
from jax.sharding import PartitionSpec as P

AXES = ("blk", "rep")
LANES = 128
MIB = 1024 * 1024


def split_blocks(blk, rep):
    pair = 2 if blk % 2 == 0 else 1
    line = blk // pair
    mid = max(d for d in range(1, line + 1) if line % d == 0 and d * d <= line)
    near = 2 if line // mid % 2 == 0 else 1
    return line // mid // near, near, mid, pair, rep


def partner(index, step, size):
    return index ^ step if size & (size - 1) == 0 else (index + step) % size


def permutation(sizes, far=0, near=0, plane=0, pair=0):
    fars, nears, mids, pairs, reps = sizes
    found = []
    for target in range(fars * nears * mids * pairs * reps):
        rest, q = divmod(target, reps)
        rest, p = divmod(rest, pairs)
        rest, m = divmod(rest, mids)
        f, n = divmod(rest, nears)
        m, q = divmod(partner(m * reps + q, plane, mids * reps), reps)
        f, n, p = partner(f, far, fars), partner(n, near, nears), partner(p, pair, pairs)
        found.append(((((f * nears + n) * mids + m) * pairs + p) * reps + q, target))
    return found


def three_parts(value):
    first = value.astype(jnp.bfloat16).astype(jnp.float32)
    second = (value - first).astype(jnp.bfloat16).astype(jnp.float32)
    return first, second, value - first - second


def stack_rows(feat):
    return 6 * feat + 16


def norm_rows(values):
    line = lax.broadcasted_iota(jnp.int32, (16, values[0].shape[1]), 0)
    rows = jnp.zeros(line.shape, jnp.float32)
    for k, value in enumerate(values):
        rows = jnp.where(line == k, value, rows)
    return rows


def column_stack(z):
    a, b, c = three_parts(z)
    square = jnp.sum(z * z, axis=0, keepdims=True)
    return jnp.concatenate([a, a, b, a, c, b, norm_rows([*three_parts(square), 1.0, 1.0, 1.0, 1.0])], axis=0)


def row_stack(z, factor, constant):
    a, b, c = three_parts(z * (-2.0 * factor))
    square = three_parts(factor * jnp.sum(z * z, axis=0, keepdims=True))
    ones = jnp.full_like(square[0], factor)
    return jnp.concatenate([a, b, a, c, a, b, norm_rows([ones, ones, ones, *square, constant])], axis=0)


def packed_pieces(count, width):
    rest = width % LANES
    return LANES // rest if width > LANES and rest and LANES % rest == 0 and count % 8 == 0 else 0


def packed_shape(count, width):
    fit = packed_pieces(count, width)
    if not fit:
        return count, width
    return width // LANES * count + -(-(count // 8) // fit) * 8, LANES


def pack_kernel(block_ref, out_ref):
    block = block_ref[...]
    count, width = block.shape
    fit = packed_pieces(count, width)
    if not fit:
        out_ref[...] = block
        return
    full = width // LANES
    for k in range(full):
        out_ref[k * count : (k + 1) * count, :] = block[:, k * LANES : (k + 1) * LANES]
    base = full * count
    pieces = [block[at : at + 8, full * LANES :] for at in range(0, count, 8)]
    for first in range(0, len(pieces), fit):
        line = pieces[first : first + fit]
        line += [jnp.zeros_like(line[0])] * (fit - len(line))
        out_ref[base + first // fit * 8 : base + first // fit * 8 + 8, :] = jnp.concatenate(line, axis=1)


def folds(count, width, blocks):
    tail = blocks * width % LANES
    return LANES // tail if tail and LANES % tail == 0 and count % (LANES // tail * 8) == 0 else 0


def line_shape(count, width, blocks):
    full, tail = divmod(blocks * width, LANES)
    fold = folds(count, width, blocks)
    return full * count + (count // fold if fold else count if tail else 0), LANES


def line_kernel(count, width, *refs):
    block_refs, out_ref = refs[:-1], refs[-1]
    fit = packed_pieces(count, width)
    full, rest = divmod(width, LANES)
    begin = 0
    if not fit:
        joined = [ref[...] for ref in block_refs]
    else:
        joined = []
        for ref in block_refs:
            for k in range(full):
                out_ref[begin : begin + count, :] = ref[k * count : (k + 1) * count, :]
                begin += count
            pieces = []
            for k in range(count // 8):
                at = full * count + k // fit * 8
                pieces.append(ref[at : at + 8, k % fit * rest : (k % fit + 1) * rest])
            joined.append(jnp.concatenate(pieces, axis=0))
    tails = jnp.concatenate(joined, axis=1)
    while tails.shape[1] >= LANES:
        out_ref[begin : begin + count, :] = tails[:, :LANES]
        begin += count
        tails = tails[:, LANES:]
    left = tails.shape[1]
    fold = folds(count, width, len(block_refs))
    if fold:
        high = count // fold
        parts = [tails[k * high : (k + 1) * high] for k in range(fold)]
        out_ref[begin : begin + high, :] = jnp.concatenate(parts, axis=1)
    elif left:
        zeros = jnp.zeros((count, LANES - left), jnp.float32)
        out_ref[begin : begin + count, :] = jnp.concatenate([tails, zeros], axis=1)


def joined_tails(count, line_refs):
    tails = []
    for ref in line_refs:
        high = ref.shape[0] % count
        if high:
            folded = ref[ref.shape[0] - high :, :]
            left = LANES * high // count
            parts = [folded[:, k * left : (k + 1) * left] for k in range(count // high)]
            tails.append(jnp.concatenate(parts, axis=0))
    if not tails:
        return []
    over = -sum(tail.shape[1] for tail in tails) % LANES
    if over:
        tails.append(jnp.zeros((count, over), jnp.float32))
    tails = jnp.concatenate(tails, axis=1)
    return [tails[:, at : at + LANES] for at in range(0, tails.shape[1], LANES)]


def piece_values(scale, row_feat, piece):
    feat = scale.shape[0]
    rows = row_feat.shape[0] // 2
    col_feat = column_stack(piece[:feat] * scale).astype(jnp.bfloat16)
    vec = piece[feat:]
    vec_high = vec.astype(jnp.bfloat16)
    vec_low = (vec - vec_high.astype(jnp.float32)).astype(jnp.bfloat16)
    for_high = jnp.concatenate([vec_high, vec_low], axis=0)
    for_low = jnp.concatenate([vec_high, jnp.zeros_like(vec_low)], axis=0)
    both = jnp.dot(row_feat, col_feat, preferred_element_type=jnp.float32)
    square = jnp.maximum(both[:rows], 1e-30)
    root = square * lax.rsqrt(square)
    value = (both[rows:] + root) * jnp.exp2(root * (-1.0 / math.log(2.0)))
    high = value.astype(jnp.bfloat16)
    low = (value - high.astype(jnp.float32)).astype(jnp.bfloat16)
    return [high, low], [for_high, for_low]


def add_columns(total, scale, row_feat, line_refs, count):
    def products(pieces):
        values, vectors = [], []
        for piece in pieces:
            value, vector = piece_values(scale, row_feat, piece)
            values += value
            vectors += vector
        values, vectors = jnp.concatenate(values, axis=1), jnp.concatenate(vectors, axis=1)
        return lax.dot_general(values, vectors, (((1,), (1,)), ((), ())), preferred_element_type=jnp.float32)

    numbers = [ref.shape[0] // count for ref in line_refs]
    if sum(numbers) <= 16:
        pieces = [ref[k * count : (k + 1) * count, :] for ref, number in zip(line_refs, numbers) for k in range(number)]
        return total + products(pieces + joined_tails(count, line_refs))
    for ref, number in zip(line_refs, numbers):

        def add(k, total, ref=ref):
            return total + products([ref[pl.ds(pl.multiple_of(k * count, 8), count), :]])

        total = lax.fori_loop(0, number, add, total)
    tails = joined_tails(count, line_refs)
    return total + products(tails) if tails else total


def points_of(ref, feat, width, count):
    if ref.shape == (feat, width):
        return ref[...]
    fit = packed_pieces(count, width)
    if not fit:
        return ref[:feat, :]
    full, rest = divmod(width, LANES)
    parts = [ref[k * count : k * count + feat, :] for k in range(full)]
    pieces = []
    for k in range(feat // 8):
        at = full * count + k // fit * 8
        pieces.append(ref[at : at + 8, k % fit * rest : (k % fit + 1) * rest])
    return jnp.concatenate(parts + [jnp.concatenate(pieces, axis=0)], axis=1)


def first_kernel(nrow, count, scale_ref, *refs):
    row_refs, line_refs = refs[:nrow], refs[nrow:-3]
    total_ref, feat_ref, scale_out = refs[-3:]
    feat, width = row_refs[0].shape
    scale = jnp.broadcast_to(jnp.sqrt(jnp.float32(5.0 / 3.0)) / scale_ref[...], (feat, LANES))
    scale_out[...] = scale
    for k, ref in enumerate(row_refs):
        z = points_of(ref, feat, width, count) * scale[:, :1]
        begin = 2 * k * width
        feat_ref[begin : begin + width, :] = row_stack(z, 3.0, 0.0).T.astype(jnp.bfloat16)
        feat_ref[begin + width : begin + 2 * width, :] = row_stack(z, 1.0, 1.0).T.astype(jnp.bfloat16)
    for k in range(nrow):
        here = slice(k * width, (k + 1) * width)
        zeros = jnp.zeros((width, total_ref.shape[1]), jnp.float32)
        rows = feat_ref[2 * k * width : 2 * (k + 1) * width, :]
        total_ref[here, :] = add_columns(zeros, scale, rows, line_refs, count)


def middle_kernel(nrow, count, scale_ref, feat_ref, before_ref, *refs):
    width = before_ref.shape[0] // nrow
    for k in range(nrow):
        here = slice(k * width, (k + 1) * width)
        rows = feat_ref[2 * k * width : 2 * (k + 1) * width, :]
        refs[-1][here, :] = add_columns(before_ref[here, :], scale_ref[...], rows, refs[:-1], count)


def last_kernel(count, begin, nout, scale_ref, feat_ref, before_ref, *refs):
    line_refs, out_refs = refs[:-nout], refs[-nout:]
    nvec, width = out_refs[0].shape
    for ref in out_refs:
        here = slice(begin, begin + width)
        rows = feat_ref[2 * begin : 2 * (begin + width), :]
        part = add_columns(before_ref[here, :], scale_ref[...], rows, line_refs, count).T
        ref[...] = part[:nvec] + part[nvec:]
        begin += width


def limits(rows, cols):
    return {
        "compiler_params": pltpu.CompilerParams(vmem_limit_bytes=4 * MIB + 4096 * rows + 2048 * cols),
        "cost_estimate": pl.CostEstimate(flops=0, bytes_accessed=0, transcendentals=0),
    }


def per_device(sizes, points, vectors, lengthscales):
    far, near, mid, pair, rep = sizes
    (feat, width), nvec = points.shape, vectors.shape[0]
    count, rows = feat + nvec, near * pair * width
    high, wide = packed_shape(count, width)

    def send(item, **steps):
        return lax.ppermute(item, AXES, permutation(sizes, **steps))

    def send_back(item, **steps):
        return lax.ppermute(item, AXES, [(target, source) for source, target in permutation(sizes, **steps)])

    def call(body, lines, out_shape, *operands):
        cols = sum(line.shape[0] for line in lines) // count * LANES
        return pl.pallas_call(
            body,
            out_shape=[jax.ShapeDtypeStruct(shape, dtype) for shape, dtype in out_shape],
            **limits(rows, cols),
        )(*operands, *lines)

    block = pl.pallas_call(
        pack_kernel,
        out_shape=jax.ShapeDtypeStruct((high, wide), jnp.float32),
        compiler_params=pltpu.CompilerParams(vmem_limit_bytes=2 * MIB),
    )(jnp.concatenate([points, vectors], axis=0))
    near_blocks = [send(block, near=k) for k in range(1, near)]
    blocks = [send(block, far=k) for k in range(1, far)]
    own_points = [send(points, pair=k) for k in range(1, pair)]
    near_blocks, blocks, own_points = lax.optimization_barrier((near_blocks, blocks, own_points))
    line = pl.pallas_call(
        functools.partial(line_kernel, count, width),
        out_shape=jax.ShapeDtypeStruct(line_shape(count, width, far), jnp.float32),
        compiler_params=pltpu.CompilerParams(vmem_limit_bytes=2 * MIB + 16 * far * high * wide),
    )(block, *blocks)
    plane = [send(line, plane=k) for k in reversed(range(1, mid * rep))]
    row_points = []
    row_points = [points] + own_points
    for item in near_blocks:
        row_points += [item] + [send(item, pair=k) for k in range(1, pair)]
    total_shape = (rows, 2 * nvec), jnp.float32
    total, row_feat, scale = call(
        functools.partial(first_kernel, near * pair, count),
        [line],
        [total_shape, ((2 * rows, stack_rows(feat)), jnp.bfloat16), ((feat, LANES), jnp.float32)],
        lengthscales[:, None],
        *row_points,
    )
    early, late = plane[:-2], plane[-2:]
    if early:
        total, early = lax.optimization_barrier((total, early))
        body = functools.partial(middle_kernel, near * pair, count)
        (total,) = call(body, early, [total_shape], scale, row_feat, total)
    total, late = lax.optimization_barrier((total, late))

    def finish(begin, number, total):
        body = functools.partial(last_kernel, count, begin * width, number)
        return call(body, late, [((nvec, width), jnp.float32)] * number, scale, row_feat, total)

    others = []
    if near * pair > 1:
        parts = finish(1, near * pair - 1, total)
        total, parts = lax.optimization_barrier((total, parts))
        for k, part in enumerate(parts, 1):
            others.append(send_back(part, near=k // pair, pair=k % pair))
    (result,) = finish(0, 1, total)
    for other in others:
        result = result + other
    return result


def solution(mesh):
    sizes = split_blocks(mesh.shape["blk"], mesh.shape["rep"])
    return jax.shard_map(
        functools.partial(per_device, sizes),
        mesh=mesh,
        in_specs=(P(None, AXES), P(None, AXES), P()),
        out_specs=P(None, AXES),
        check_vma=False,
    )
```

```python
import functools
import math

import jax
import jax.numpy as jnp
from jax import lax
from jax.experimental import pallas as pl
from jax.experimental.pallas import tpu as pltpu
from jax.sharding import PartitionSpec as P

AXES = ("blk", "rep")
LANES = 128
MIB = 1024 * 1024


def split_blocks(blk, rep):
    pair = 2 if blk % 2 == 0 else 1
    line = blk // pair
    mid = max(d for d in range(1, line + 1) if line % d == 0 and d * d <= line)
    return line // mid, mid, pair, rep


def partner(index, step, size):
    return index ^ step if size & (size - 1) == 0 else (index + step) % size


def permutation(sizes, axis, step):
    far, mid, pair, rep = sizes
    pairs = []
    for target in range(far * mid * pair * rep):
        rest, q = divmod(target, rep)
        rest, p = divmod(rest, pair)
        f, m = divmod(rest, mid)
        if axis == "far":
            f = partner(f, step, far)
        elif axis == "pair":
            p = partner(p, step, pair)
        else:
            m, q = divmod(partner(m * rep + q, step, mid * rep), rep)
        pairs.append((((f * mid + m) * pair + p) * rep + q, target))
    return pairs


def three_parts(value):
    first = value.astype(jnp.bfloat16).astype(jnp.float32)
    second = (value - first).astype(jnp.bfloat16).astype(jnp.float32)
    return first, second, value - first - second


def stack_rows(feat):
    return 6 * feat + 16


def norm_rows(values):
    line = lax.broadcasted_iota(jnp.int32, (16, values[0].shape[1]), 0)
    rows = jnp.zeros(line.shape, jnp.float32)
    for k, value in enumerate(values):
        rows = jnp.where(line == k, value, rows)
    return rows


def norm_parts(z, first):
    high = jnp.sum(first * first, axis=0, keepdims=True)
    low = jnp.sum((z - first) * (z + first), axis=0, keepdims=True)
    one = high.astype(jnp.bfloat16).astype(jnp.float32)
    left = (high - one) + low
    two = left.astype(jnp.bfloat16).astype(jnp.float32)
    return one, two, left - two


def column_stack(z):
    a, b, c = three_parts(z)
    norms = norm_rows([*norm_parts(z, a), 1.0, 1.0, 1.0, 3.0, 3.0, 3.0, 1.0])
    return jnp.concatenate([a, norms, a, b, a, c, b], axis=0)


def row_stack(z, tripled):
    norms = norm_parts(z, three_parts(z)[0])
    ones, zeros = jnp.ones_like(norms[0]), jnp.zeros_like(norms[0])
    a, b, c = three_parts(z * (-6.0 if tripled else -2.0))
    if tripled:
        norms = norm_rows([3.0 * ones] * 3 + [zeros] * 3 + [*norms])
    else:
        norms = norm_rows([ones] * 3 + [*norms] + [zeros] * 3 + [ones])
    return jnp.concatenate([a, norms, b, a, c, a, b], axis=0)


def packed_pieces(count, width):
    rest = width % LANES
    return LANES // rest if width > LANES and rest and LANES % rest == 0 and count % 8 == 0 else 0


def packed_shape(count, width):
    fit = packed_pieces(count, width)
    if not fit:
        return count, width
    return width // LANES * count + -(-(count // 8) // fit) * 8, LANES


def pack_kernel(block_ref, out_ref):
    block = block_ref[...]
    count, width = block.shape
    fit = packed_pieces(count, width)
    if not fit:
        out_ref[...] = block
        return
    full = width // LANES
    for k in range(full):
        out_ref[k * count : (k + 1) * count, :] = block[:, k * LANES : (k + 1) * LANES]
    base = full * count
    pieces = [block[at : at + 8, full * LANES :] for at in range(0, count, 8)]
    for first in range(0, len(pieces), fit):
        line = pieces[first : first + fit]
        line += [jnp.zeros_like(line[0])] * (fit - len(line))
        out_ref[base + first // fit * 8 : base + first // fit * 8 + 8, :] = jnp.concatenate(line, axis=1)


def line_shape(count, width, blocks):
    return -(-blocks * width // LANES) * count, LANES


def line_kernel(count, width, *refs):
    block_refs, out_ref = refs[:-1], refs[-1]
    fit = packed_pieces(count, width)
    full, rest = width // LANES, width % LANES
    if not fit:
        joined = [ref[...] for ref in block_refs]
    else:
        joined, at = [], 0
        for ref in block_refs:
            for k in range(full):
                out_ref[at : at + count, :] = ref[k * count : (k + 1) * count, :]
                at += count
            pieces = []
            for k in range(count // 8):
                begin = full * count + k // fit * 8
                pieces.append(ref[begin : begin + 8, k % fit * rest : (k % fit + 1) * rest])
            joined.append(jnp.concatenate(pieces, axis=0))
    begin = 0 if not fit else len(block_refs) * full * count
    over = -sum(item.shape[1] for item in joined) % LANES
    if over:
        joined.append(jnp.zeros((count, over), jnp.float32))
    tails = jnp.concatenate(joined, axis=1)
    for k in range(tails.shape[1] // LANES):
        out_ref[begin + k * count : begin + (k + 1) * count, :] = tails[:, k * LANES : (k + 1) * LANES]


def piece_values(scale, row_feat, piece):
    feat = scale.shape[0]
    rows = row_feat.shape[0] // 2
    col_feat = column_stack(piece[:feat] * scale).astype(jnp.bfloat16)
    vec = piece[feat:]
    vec_high = vec.astype(jnp.bfloat16)
    vec_low = (vec - vec_high.astype(jnp.float32)).astype(jnp.bfloat16)
    for_high = jnp.concatenate([vec_high, vec_low], axis=0)
    for_low = jnp.concatenate([vec_high, jnp.zeros_like(vec_low)], axis=0)
    both = jnp.dot(row_feat, col_feat, preferred_element_type=jnp.float32)
    square = jnp.maximum(both[:rows], 1e-30)
    root = square * lax.rsqrt(square)
    value = (jnp.maximum(both[rows:], 1.0) + root) * jnp.exp2(root * (-1.0 / math.log(2.0)))
    high = value.astype(jnp.bfloat16)
    low = (value - high.astype(jnp.float32)).astype(jnp.bfloat16)
    return [high, low], [for_high, for_low]


def add_columns(total, scale, row_feat, line_refs, count):
    def products(pieces):
        values, vectors = [], []
        for piece in pieces:
            value, vector = piece_values(scale, row_feat, piece)
            values += value
            vectors += vector
        values, vectors = jnp.concatenate(values, axis=1), jnp.concatenate(vectors, axis=1)
        return lax.dot_general(values, vectors, (((1,), (1,)), ((), ())), preferred_element_type=jnp.float32)

    numbers = [ref.shape[0] // count for ref in line_refs]
    if sum(numbers) <= 16:
        pieces = [ref[k * count : (k + 1) * count, :] for ref, number in zip(line_refs, numbers) for k in range(number)]
        return total + products(pieces)
    for ref, number in zip(line_refs, numbers):

        def add(k, total, ref=ref):
            return total + products([ref[pl.ds(pl.multiple_of(k * count, 8), count), :]])

        total = lax.fori_loop(0, number, add, total)
    return total


def first_kernel(nrow, count, scale_ref, *refs):
    row_refs, line_refs = refs[:nrow], refs[nrow:-3]
    total_ref, feat_ref, scale_out = refs[-3:]
    feat, width = row_refs[0].shape
    scale = jnp.broadcast_to(jnp.sqrt(jnp.float32(5.0 / 3.0)) / scale_ref[...], (feat, LANES))
    scale_out[...] = scale
    for k, ref in enumerate(row_refs):
        z = ref[...] * scale[:, :1]
        begin = 2 * k * width
        feat_ref[begin : begin + width, :] = row_stack(z, True).T.astype(jnp.bfloat16)
        feat_ref[begin + width : begin + 2 * width, :] = row_stack(z, False).T.astype(jnp.bfloat16)
    for k in range(nrow):
        here = slice(k * width, (k + 1) * width)
        zeros = jnp.zeros((width, total_ref.shape[1]), jnp.float32)
        rows = feat_ref[2 * k * width : 2 * (k + 1) * width, :]
        total_ref[here, :] = add_columns(zeros, scale, rows, line_refs, count)


def middle_kernel(nrow, count, scale_ref, feat_ref, before_ref, *refs):
    width = before_ref.shape[0] // nrow
    for k in range(nrow):
        here = slice(k * width, (k + 1) * width)
        rows = feat_ref[2 * k * width : 2 * (k + 1) * width, :]
        refs[-1][here, :] = add_columns(before_ref[here, :], scale_ref[...], rows, refs[:-1], count)


def last_kernel(count, begin, scale_ref, feat_ref, before_ref, *refs):
    nvec, width = refs[-1].shape
    here = slice(begin, begin + width)
    rows = feat_ref[2 * begin : 2 * (begin + width), :]
    part = add_columns(before_ref[here, :], scale_ref[...], rows, refs[:-1], count).T
    refs[-1][...] = part[:nvec] + part[nvec:]


def limits(rows, cols):
    return {
        "compiler_params": pltpu.CompilerParams(vmem_limit_bytes=4 * MIB + 4096 * rows + 2048 * cols),
        "cost_estimate": pl.CostEstimate(flops=0, bytes_accessed=0, transcendentals=0),
    }


def per_device(sizes, points, vectors, lengthscales):
    far, mid, pair, rep = sizes
    (feat, width), nvec = points.shape, vectors.shape[0]
    count, rows = feat + nvec, pair * width
    high, wide = packed_shape(count, width)

    def send(item, axis, step):
        return lax.ppermute(item, AXES, permutation(sizes, axis, step))

    def call(body, lines, out_shape, *operands):
        cols = sum(line.shape[0] for line in lines) // count * LANES
        return pl.pallas_call(
            body,
            out_shape=[jax.ShapeDtypeStruct(shape, dtype) for shape, dtype in out_shape],
            **limits(rows, cols),
        )(*operands, *lines)

    block = pl.pallas_call(
        pack_kernel,
        out_shape=jax.ShapeDtypeStruct((high, wide), jnp.float32),
        compiler_params=pltpu.CompilerParams(vmem_limit_bytes=2 * MIB),
    )(jnp.concatenate([points, vectors], axis=0))
    later_points, block = lax.optimization_barrier((points, block))
    blocks = [send(block, "far", k) for k in [*range(2, far), 1][: far - 1]]
    row_points = [send(later_points, "pair", k) for k in range(1, pair)]
    blocks, row_points = lax.optimization_barrier((blocks, row_points))
    line = pl.pallas_call(
        functools.partial(line_kernel, count, width),
        out_shape=jax.ShapeDtypeStruct(line_shape(count, width, far), jnp.float32),
        compiler_params=pltpu.CompilerParams(vmem_limit_bytes=2 * MIB + 16 * far * high * wide),
    )(block, *blocks)
    plane = [send(line, "plane", k) for k in reversed(range(1, mid * rep))]
    total, row_feat, scale = call(
        functools.partial(first_kernel, pair, count),
        [line],
        [((rows, 2 * nvec), jnp.float32), ((2 * rows, stack_rows(feat)), jnp.bfloat16), ((feat, LANES), jnp.float32)],
        lengthscales[:, None],
        points,
        *row_points,
    )
    early, late = plane[:-2], plane[-2:]
    if early:
        total, early = lax.optimization_barrier((total, early))
        (total,) = call(functools.partial(middle_kernel, pair, count), early, [((rows, 2 * nvec), jnp.float32)], scale, row_feat, total)
    total, late = lax.optimization_barrier((total, late))

    def finish(k, total):
        body = functools.partial(last_kernel, count, k * width)
        (part,) = call(body, late, [((nvec, width), jnp.float32)], scale, row_feat, total)
        return part

    parts = []
    for k in range(1, pair):
        part = finish(k, total)
        total, part = lax.optimization_barrier((total, part))
        parts.append(part)
    result = finish(0, total)
    for k, part in enumerate(parts, 1):
        back = [(target, source) for source, target in permutation(sizes, "pair", k)]
        result = result + lax.ppermute(part, AXES, back)
    return result


def solution(mesh):
    sizes = split_blocks(mesh.shape["blk"], mesh.shape["rep"])
    return jax.shard_map(
        functools.partial(per_device, sizes),
        mesh=mesh,
        in_specs=(P(None, AXES), P(None, AXES), P()),
        out_specs=P(None, AXES),
        check_vma=False,
    )
```

```python
import functools
import math

import jax
import jax.numpy as jnp
from jax import lax
from jax.experimental import pallas as pl
from jax.experimental.pallas import tpu as pltpu
from jax.sharding import PartitionSpec as P

AXES = ("blk", "rep")
LANES = 128
MIB = 1024 * 1024


def split_blocks(blk, rep):
    pair = 2 if blk % 2 == 0 else 1
    line = blk // pair
    mid = max(d for d in range(1, line + 1) if line % d == 0 and d * d <= line)
    return line // mid, mid, pair, rep


def partner(index, step, size):
    return index ^ step if size & (size - 1) == 0 else (index + step) % size


def permutation(sizes, axis, step):
    far, mid, pair, rep = sizes
    pairs = []
    for target in range(far * mid * pair * rep):
        rest, q = divmod(target, rep)
        rest, p = divmod(rest, pair)
        f, m = divmod(rest, mid)
        if axis == "far":
            f = partner(f, step, far)
        elif axis == "pair":
            p = partner(p, step, pair)
        else:
            m, q = divmod(partner(m * rep + q, step, mid * rep), rep)
        pairs.append((((f * mid + m) * pair + p) * rep + q, target))
    return pairs


def three_parts(value):
    first = value.astype(jnp.bfloat16).astype(jnp.float32)
    second = (value - first).astype(jnp.bfloat16).astype(jnp.float32)
    return first, second, value - first - second


def stack_rows(feat):
    return 6 * feat + 16


def norm_rows(values):
    width = next(value.shape[1] for value in values if not isinstance(value, float))
    halves = []
    for half in (values[:8], values[8:]):
        line = lax.broadcasted_iota(jnp.int32, (8, width), 0)
        rows = jnp.zeros((8, width), jnp.float32)
        for arrays in (False, True):
            for k, value in enumerate(half):
                if isinstance(value, float) != arrays:
                    rows = jnp.where(line == k, value, rows)
        halves.append(rows)
    return jnp.concatenate(halves, axis=0)


def norm_parts(z, first):
    high = jnp.sum(first * first, axis=0, keepdims=True)
    low = jnp.sum((z - first) * (z + first), axis=0, keepdims=True)
    one = high.astype(jnp.bfloat16).astype(jnp.float32)
    left = (high - one) + low
    two = left.astype(jnp.bfloat16).astype(jnp.float32)
    return one, two, left - two


def column_stack(z):
    a, b, c = three_parts(z)
    norms = norm_rows([*norm_parts(z, a), 1.0, 1.0, 1.0, 3.0, 3.0, 3.0, 1.0])
    return jnp.concatenate([a, norms, a, b, a, c, b], axis=0)


def row_stack(z, tripled):
    norms = norm_parts(z, three_parts(z)[0])
    a, b, c = three_parts(z * (-6.0 if tripled else -2.0))
    if tripled:
        norms = norm_rows([3.0] * 3 + [0.0] * 3 + [*norms])
    else:
        norms = norm_rows([1.0] * 3 + [*norms] + [0.0] * 3 + [1.0])
    return jnp.concatenate([a, norms, b, a, c, a, b], axis=0)


def packed_pieces(count, width):
    rest = width % LANES
    return LANES // rest if width > LANES and rest and LANES % rest == 0 and count % 8 == 0 else 0


def packed_shape(count, width):
    fit = packed_pieces(count, width)
    if not fit:
        return count, width
    return width // LANES * count + -(-(count // 8) // fit) * 8, LANES


def pack_kernel(block_ref, out_ref):
    block = block_ref[...]
    count, width = block.shape
    fit = packed_pieces(count, width)
    if not fit:
        out_ref[...] = block
        return
    full = width // LANES
    for k in range(full):
        out_ref[k * count : (k + 1) * count, :] = block[:, k * LANES : (k + 1) * LANES]
    base = full * count
    pieces = [block[at : at + 8, full * LANES :] for at in range(0, count, 8)]
    for first in range(0, len(pieces), fit):
        line = pieces[first : first + fit]
        line += [jnp.zeros_like(line[0])] * (fit - len(line))
        out_ref[base + first // fit * 8 : base + first // fit * 8 + 8, :] = jnp.concatenate(line, axis=1)


def line_shape(count, width, blocks):
    return -(-blocks * width // LANES) * count, LANES


def line_kernel(count, width, *refs):
    block_refs, out_ref = refs[:-1], refs[-1]
    fit = packed_pieces(count, width)
    full, rest = width // LANES, width % LANES
    if not fit:
        joined = [ref[...] for ref in block_refs]
    else:
        joined, at = [], 0
        for ref in block_refs:
            for k in range(full):
                out_ref[at : at + count, :] = ref[k * count : (k + 1) * count, :]
                at += count
            pieces = []
            for k in range(count // 8):
                begin = full * count + k // fit * 8
                pieces.append(ref[begin : begin + 8, k % fit * rest : (k % fit + 1) * rest])
            joined.append(jnp.concatenate(pieces, axis=0))
    begin = 0 if not fit else len(block_refs) * full * count
    over = -sum(item.shape[1] for item in joined) % LANES
    if over:
        joined.append(jnp.zeros((count, over), jnp.float32))
    tails = jnp.concatenate(joined, axis=1)
    for k in range(tails.shape[1] // LANES):
        out_ref[begin + k * count : begin + (k + 1) * count, :] = tails[:, k * LANES : (k + 1) * LANES]


def piece_values(scale, row_feat, piece):
    feat = scale.shape[0]
    rows = row_feat.shape[0] // 2
    col_feat = column_stack(piece[:feat] * scale).astype(jnp.bfloat16)
    vec = piece[feat:]
    vec_high = vec.astype(jnp.bfloat16)
    vec_low = (vec - vec_high.astype(jnp.float32)).astype(jnp.bfloat16)
    vec_parts = jnp.concatenate([vec_high, vec_low], axis=0)
    both = jnp.dot(row_feat, col_feat, preferred_element_type=jnp.float32)
    square = jnp.maximum(both[:rows], 1e-30)
    root = square * lax.rsqrt(square)
    value = (jnp.maximum(both[rows:], 1.0) + root) * jnp.exp2(root * (-1.0 / math.log(2.0)))
    high = value.astype(jnp.bfloat16)
    low = (value - high.astype(jnp.float32)).astype(jnp.bfloat16)
    return [high, low], [vec_parts, vec_parts]


def add_columns(total, scale, row_feat, line_refs, count):
    def products(pieces):
        values, vectors = [], []
        for piece in pieces:
            value, vector = piece_values(scale, row_feat, piece)
            values += value
            vectors += vector
        values, vectors = jnp.concatenate(values, axis=1), jnp.concatenate(vectors, axis=1)
        return lax.dot_general(values, vectors, (((1,), (1,)), ((), ())), preferred_element_type=jnp.float32)

    numbers = [ref.shape[0] // count for ref in line_refs]
    if sum(numbers) <= 16:
        pieces = [ref[k * count : (k + 1) * count, :] for ref, number in zip(line_refs, numbers) for k in range(number)]
        return total + products(pieces)
    for ref, number in zip(line_refs, numbers):

        def add(k, total, ref=ref):
            return total + products([ref[pl.ds(pl.multiple_of(k * count, 8), count), :]])

        total = lax.fori_loop(0, number, add, total)
    return total


def first_kernel(nrow, count, scale_ref, *refs):
    row_refs, line_refs = refs[:nrow], refs[nrow:-3]
    total_ref, feat_ref, scale_out = refs[-3:]
    feat, width = row_refs[0].shape
    scale = jnp.broadcast_to(jnp.sqrt(jnp.float32(5.0 / 3.0)) / scale_ref[...], (feat, LANES))
    scale_out[...] = scale
    for k, ref in enumerate(row_refs):
        z = ref[...] * scale[:, :1]
        begin = 2 * k * width
        feat_ref[begin : begin + width, :] = row_stack(z, True).T.astype(jnp.bfloat16)
        feat_ref[begin + width : begin + 2 * width, :] = row_stack(z, False).T.astype(jnp.bfloat16)
    for k in range(nrow):
        here = slice(k * width, (k + 1) * width)
        zeros = jnp.zeros((width, total_ref.shape[1]), jnp.float32)
        rows = feat_ref[2 * k * width : 2 * (k + 1) * width, :]
        total_ref[here, :] = add_columns(zeros, scale, rows, line_refs, count)


def middle_kernel(nrow, count, scale_ref, feat_ref, before_ref, *refs):
    width = before_ref.shape[0] // nrow
    for k in range(nrow):
        here = slice(k * width, (k + 1) * width)
        rows = feat_ref[2 * k * width : 2 * (k + 1) * width, :]
        refs[-1][here, :] = add_columns(before_ref[here, :], scale_ref[...], rows, refs[:-1], count)


def last_kernel(count, begin, scale_ref, feat_ref, before_ref, *refs):
    nvec, width = refs[-1].shape
    here = slice(begin, begin + width)
    rows = feat_ref[2 * begin : 2 * (begin + width), :]
    part = add_columns(before_ref[here, :], scale_ref[...], rows, refs[:-1], count).T
    refs[-1][...] = part[:nvec] + part[nvec:]


def limits(rows, cols):
    return {
        "compiler_params": pltpu.CompilerParams(vmem_limit_bytes=4 * MIB + 4096 * rows + 2048 * cols),
        "cost_estimate": pl.CostEstimate(flops=0, bytes_accessed=0, transcendentals=0),
    }


def per_device(sizes, points, vectors, lengthscales):
    far, mid, pair, rep = sizes
    (feat, width), nvec = points.shape, vectors.shape[0]
    count, rows = feat + nvec, pair * width
    high, wide = packed_shape(count, width)

    def send(item, axis, step):
        return lax.ppermute(item, AXES, permutation(sizes, axis, step))

    def call(body, lines, out_shape, *operands):
        cols = sum(line.shape[0] for line in lines) // count * LANES
        return pl.pallas_call(
            body,
            out_shape=[jax.ShapeDtypeStruct(shape, dtype) for shape, dtype in out_shape],
            **limits(rows, cols),
        )(*operands, *lines)

    block = pl.pallas_call(
        pack_kernel,
        out_shape=jax.ShapeDtypeStruct((high, wide), jnp.float32),
        compiler_params=pltpu.CompilerParams(vmem_limit_bytes=2 * MIB),
    )(jnp.concatenate([points, vectors], axis=0))
    later_points, block = lax.optimization_barrier((points, block))
    blocks = [send(block, "far", k) for k in [*range(2, far), 1][: far - 1]]
    row_points = [send(later_points, "pair", k) for k in range(1, pair)]
    blocks, row_points = lax.optimization_barrier((blocks, row_points))
    line = pl.pallas_call(
        functools.partial(line_kernel, count, width),
        out_shape=jax.ShapeDtypeStruct(line_shape(count, width, far), jnp.float32),
        compiler_params=pltpu.CompilerParams(vmem_limit_bytes=2 * MIB + 16 * far * high * wide),
    )(block, *blocks)
    plane = [send(line, "plane", k) for k in reversed(range(1, mid * rep))]
    total, row_feat, scale = call(
        functools.partial(first_kernel, pair, count),
        [line],
        [((rows, 2 * nvec), jnp.float32), ((2 * rows, stack_rows(feat)), jnp.bfloat16), ((feat, LANES), jnp.float32)],
        lengthscales[:, None],
        points,
        *row_points,
    )
    early, late = plane[:-2], plane[-2:]
    if early:
        total, early = lax.optimization_barrier((total, early))
        (total,) = call(functools.partial(middle_kernel, pair, count), early, [((rows, 2 * nvec), jnp.float32)], scale, row_feat, total)
    total, late = lax.optimization_barrier((total, late))

    def finish(k, total):
        body = functools.partial(last_kernel, count, k * width)
        (part,) = call(body, late, [((nvec, width), jnp.float32)], scale, row_feat, total)
        return part

    parts = []
    for k in range(1, pair):
        part = finish(k, total)
        total, part = lax.optimization_barrier((total, part))
        parts.append(part)
    result = finish(0, total)
    for k, part in enumerate(parts, 1):
        back = [(target, source) for source, target in permutation(sizes, "pair", k)]
        result = result + lax.ppermute(part, AXES, back)
    return result


def solution(mesh):
    sizes = split_blocks(mesh.shape["blk"], mesh.shape["rep"])
    return jax.shard_map(
        functools.partial(per_device, sizes),
        mesh=mesh,
        in_specs=(P(None, AXES), P(None, AXES), P()),
        out_specs=P(None, AXES),
        check_vma=False,
    )
```

```python
import functools
import math

import jax
import jax.numpy as jnp
from jax import lax
from jax.experimental import pallas as pl
from jax.experimental.pallas import tpu as pltpu
from jax.sharding import PartitionSpec as P

AXES = ("blk", "rep")
LANES = 128
MIB = 1024 * 1024


def split_blocks(blk, rep):
    pair = 2 if blk % 2 == 0 else 1
    line = blk // pair
    mid = max(d for d in range(1, line + 1) if line % d == 0 and d * d <= line)
    return line // mid, mid, pair, rep


def partner(index, step, size):
    return index ^ step if size & (size - 1) == 0 else (index + step) % size


def permutation(sizes, axis, step):
    far, mid, pair, rep = sizes
    pairs = []
    for target in range(far * mid * pair * rep):
        rest, q = divmod(target, rep)
        rest, p = divmod(rest, pair)
        f, m = divmod(rest, mid)
        if axis == "far":
            f = partner(f, step, far)
        elif axis == "pair":
            p = partner(p, step, pair)
        else:
            m, q = divmod(partner(m * rep + q, step, mid * rep), rep)
        pairs.append((((f * mid + m) * pair + p) * rep + q, target))
    return pairs


def three_parts(value):
    first = value.astype(jnp.bfloat16).astype(jnp.float32)
    second = (value - first).astype(jnp.bfloat16).astype(jnp.float32)
    return first, second, value - first - second


def stack_rows(feat):
    return 6 * feat + 16


def norm_rows(values):
    width = next(value.shape[1] for value in values if not isinstance(value, float))
    halves = []
    for half in (values[:8], values[8:]):
        line = lax.broadcasted_iota(jnp.int32, (8, width), 0)
        rows = jnp.zeros((8, width), jnp.float32)
        for arrays in (False, True):
            for k, value in enumerate(half):
                if isinstance(value, float) != arrays:
                    rows = jnp.where(line == k, value, rows)
        halves.append(rows)
    return jnp.concatenate(halves, axis=0)


def norm_parts(z, first):
    high = jnp.sum(first * first, axis=0, keepdims=True)
    low = jnp.sum((z - first) * (z + first), axis=0, keepdims=True)
    one = high.astype(jnp.bfloat16).astype(jnp.float32)
    left = (high - one) + low
    two = left.astype(jnp.bfloat16).astype(jnp.float32)
    return one, two, left - two


def column_stack(z):
    a, b, c = three_parts(z)
    norms = norm_rows([*norm_parts(z, a), 1.0, 1.0, 1.0, 3.0, 3.0, 3.0, 1.0])
    return jnp.concatenate([a, norms, a, b, a, c, b], axis=0)


def row_stack(z, tripled):
    norms = norm_parts(z, three_parts(z)[0])
    a, b, c = three_parts(z * (-6.0 if tripled else -2.0))
    if tripled:
        norms = norm_rows([3.0] * 3 + [0.0] * 3 + [*norms])
    else:
        norms = norm_rows([1.0] * 3 + [*norms] + [0.0] * 3 + [1.0])
    return jnp.concatenate([a, norms, b, a, c, a, b], axis=0)


def packed_pieces(count, width):
    rest = width % LANES
    return LANES // rest if width > LANES and rest and LANES % rest == 0 and count % 8 == 0 else 0


def packed_shape(count, width):
    fit = packed_pieces(count, width)
    if not fit:
        return count, width
    return width // LANES * count + -(-(count // 8) // fit) * 8, LANES


def pack_kernel(block_ref, out_ref):
    block = block_ref[...]
    count, width = block.shape
    fit = packed_pieces(count, width)
    if not fit:
        out_ref[...] = block
        return
    full = width // LANES
    for k in range(full):
        out_ref[k * count : (k + 1) * count, :] = block[:, k * LANES : (k + 1) * LANES]
    base = full * count
    pieces = [block[at : at + 8, full * LANES :] for at in range(0, count, 8)]
    for first in range(0, len(pieces), fit):
        line = pieces[first : first + fit]
        line += [jnp.zeros_like(line[0])] * (fit - len(line))
        out_ref[base + first // fit * 8 : base + first // fit * 8 + 8, :] = jnp.concatenate(line, axis=1)


def line_shape(count, width, blocks):
    return -(-blocks * width // LANES) * count, LANES


def line_kernel(count, width, *refs):
    block_refs, out_ref = refs[:-1], refs[-1]
    fit = packed_pieces(count, width)
    full, rest = width // LANES, width % LANES
    if not fit:
        joined = [ref[...] for ref in block_refs]
    else:
        joined, at = [], 0
        for ref in block_refs:
            for k in range(full):
                out_ref[at : at + count, :] = ref[k * count : (k + 1) * count, :]
                at += count
            pieces = []
            for k in range(count // 8):
                begin = full * count + k // fit * 8
                pieces.append(ref[begin : begin + 8, k % fit * rest : (k % fit + 1) * rest])
            joined.append(jnp.concatenate(pieces, axis=0))
    begin = 0 if not fit else len(block_refs) * full * count
    over = -sum(item.shape[1] for item in joined) % LANES
    if over:
        joined.append(jnp.zeros((count, over), jnp.float32))
    tails = jnp.concatenate(joined, axis=1)
    for k in range(tails.shape[1] // LANES):
        out_ref[begin + k * count : begin + (k + 1) * count, :] = tails[:, k * LANES : (k + 1) * LANES]


def piece_values(scale, row_feat, piece):
    feat = scale.shape[0]
    rows = row_feat.shape[0] // 2
    col_feat = column_stack(piece[:feat] * scale).astype(jnp.bfloat16)
    vec = piece[feat:]
    vec_high = vec.astype(jnp.bfloat16)
    vec_low = (vec - vec_high.astype(jnp.float32)).astype(jnp.bfloat16)
    vec_parts = jnp.concatenate([vec_high, vec_low], axis=0)
    both = jnp.dot(row_feat, col_feat, preferred_element_type=jnp.float32)
    square = jnp.maximum(both[:rows], 1e-30)
    root = square * lax.rsqrt(square)
    value = (jnp.maximum(both[rows:], 1.0) + root) * jnp.exp2(root * (-1.0 / math.log(2.0)))
    high = value.astype(jnp.bfloat16)
    low = (value - high.astype(jnp.float32)).astype(jnp.bfloat16)
    return [high, low], [vec_parts, vec_parts]


def add_columns(total, scale, row_feat, line_refs, count):
    def products(pieces):
        values, vectors = [], []
        for piece in pieces:
            value, vector = piece_values(scale, row_feat, piece)
            values += value
            vectors += vector
        values, vectors = jnp.concatenate(values, axis=1), jnp.concatenate(vectors, axis=1)
        return lax.dot_general(vectors, values, (((1,), (1,)), ((), ())), preferred_element_type=jnp.float32)

    numbers = [ref.shape[0] // count for ref in line_refs]
    if sum(numbers) <= 16:
        pieces = [ref[k * count : (k + 1) * count, :] for ref, number in zip(line_refs, numbers) for k in range(number)]
        return total + products(pieces)
    for ref, number in zip(line_refs, numbers):

        def add(k, total, ref=ref):
            return total + products([ref[pl.ds(pl.multiple_of(k * count, 8), count), :]])

        total = lax.fori_loop(0, number, add, total)
    return total


def first_kernel(nrow, count, scale_ref, *refs):
    row_refs, line_refs = refs[:nrow], refs[nrow : -2 - nrow]
    total_refs, feat_ref, scale_out = refs[-2 - nrow : -2], refs[-2], refs[-1]
    feat, width = row_refs[0].shape
    scale = jnp.broadcast_to(jnp.sqrt(jnp.float32(5.0 / 3.0)) / scale_ref[...], (feat, LANES))
    scale_out[...] = scale
    for k, ref in enumerate(row_refs):
        z = ref[...] * scale[:, :1]
        begin = 2 * k * width
        feat_ref[begin : begin + width, :] = row_stack(z, True).T.astype(jnp.bfloat16)
        feat_ref[begin + width : begin + 2 * width, :] = row_stack(z, False).T.astype(jnp.bfloat16)
    for k, ref in enumerate(total_refs):
        rows = feat_ref[2 * k * width : 2 * (k + 1) * width, :]
        ref[...] = add_columns(jnp.zeros(ref.shape, jnp.float32), scale, rows, line_refs, count)


def middle_kernel(nrow, count, scale_ref, feat_ref, *refs):
    before_refs, line_refs, total_refs = refs[:nrow], refs[nrow:-nrow], refs[-nrow:]
    width = total_refs[0].shape[1]
    for k, (before, after) in enumerate(zip(before_refs, total_refs)):
        rows = feat_ref[2 * k * width : 2 * (k + 1) * width, :]
        after[...] = add_columns(before[...], scale_ref[...], rows, line_refs, count)


def last_kernel(count, number, scale_ref, feat_ref, before_ref, *refs):
    nvec, width = refs[-1].shape
    rows = feat_ref[2 * number * width : 2 * (number + 1) * width, :]
    part = add_columns(before_ref[...], scale_ref[...], rows, refs[:-1], count)
    refs[-1][...] = part[:nvec] + part[nvec:]


def limits(rows, cols):
    return {
        "compiler_params": pltpu.CompilerParams(vmem_limit_bytes=4 * MIB + 4096 * rows + 2048 * cols),
        "cost_estimate": pl.CostEstimate(flops=0, bytes_accessed=0, transcendentals=0),
    }


def per_device(sizes, points, vectors, lengthscales):
    far, mid, pair, rep = sizes
    (feat, width), nvec = points.shape, vectors.shape[0]
    count, rows = feat + nvec, pair * width
    high, wide = packed_shape(count, width)

    def send(item, axis, step):
        return lax.ppermute(item, AXES, permutation(sizes, axis, step))

    def call(body, lines, out_shape, *operands):
        cols = sum(line.shape[0] for line in lines) // count * LANES
        return pl.pallas_call(
            body,
            out_shape=[jax.ShapeDtypeStruct(shape, dtype) for shape, dtype in out_shape],
            **limits(rows, cols),
        )(*operands, *lines)

    block = pl.pallas_call(
        pack_kernel,
        out_shape=jax.ShapeDtypeStruct((high, wide), jnp.float32),
        compiler_params=pltpu.CompilerParams(vmem_limit_bytes=2 * MIB),
    )(jnp.concatenate([points, vectors], axis=0))
    later_points, block = lax.optimization_barrier((points, block))
    blocks = [send(block, "far", k) for k in [*range(2, far), 1][: far - 1]]
    row_points = [send(later_points, "pair", k) for k in range(1, pair)]
    blocks, row_points = lax.optimization_barrier((blocks, row_points))
    line = pl.pallas_call(
        functools.partial(line_kernel, count, width),
        out_shape=jax.ShapeDtypeStruct(line_shape(count, width, far), jnp.float32),
        compiler_params=pltpu.CompilerParams(vmem_limit_bytes=2 * MIB + 16 * far * high * wide),
    )(block, *blocks)
    plane = [send(line, "plane", k) for k in reversed(range(1, mid * rep))]
    totals = [((2 * nvec, width), jnp.float32)] * pair
    *total, row_feat, scale = call(
        functools.partial(first_kernel, pair, count),
        [line],
        totals + [((2 * rows, stack_rows(feat)), jnp.bfloat16), ((feat, LANES), jnp.float32)],
        lengthscales[:, None],
        points,
        *row_points,
    )
    early, late = plane[:-2], plane[-2:]
    if early:
        total, early = lax.optimization_barrier((total, early))
        total = call(functools.partial(middle_kernel, pair, count), early, totals, scale, row_feat, *total)
    total, late = lax.optimization_barrier((total, late))

    def finish(k, total):
        body = functools.partial(last_kernel, count, k)
        (part,) = call(body, late, [((nvec, width), jnp.float32)], scale, row_feat, total[k])
        return part

    parts = []
    for k in range(1, pair):
        part = finish(k, total)
        total, part = lax.optimization_barrier((total, part))
        parts.append(part)
    result = finish(0, total)
    for k, part in enumerate(parts, 1):
        back = [(target, source) for source, target in permutation(sizes, "pair", k)]
        result = result + lax.ppermute(part, AXES, back)
    return result


def solution(mesh):
    sizes = split_blocks(mesh.shape["blk"], mesh.shape["rep"])
    return jax.shard_map(
        functools.partial(per_device, sizes),
        mesh=mesh,
        in_specs=(P(None, AXES), P(None, AXES), P()),
        out_specs=P(None, AXES),
        check_vma=False,
    )
```

```python
import functools
import math

import jax
import jax.numpy as jnp
from jax import lax
from jax.experimental import pallas as pl
from jax.experimental.pallas import tpu as pltpu
from jax.sharding import PartitionSpec as P

AXES = ("blk", "rep")
LANES = 128
MIB = 1024 * 1024


def split_blocks(blk, rep):
    pair = 2 if blk % 2 == 0 else 1
    line = blk // pair
    mid = max(d for d in range(1, line + 1) if line % d == 0 and d * d <= line)
    return line // mid, mid, pair, rep


def partner(index, step, size):
    return index ^ step if size & (size - 1) == 0 else (index + step) % size


def permutation(sizes, axis, step):
    far, mid, pair, rep = sizes
    pairs = []
    for target in range(far * mid * pair * rep):
        rest, q = divmod(target, rep)
        rest, p = divmod(rest, pair)
        f, m = divmod(rest, mid)
        if axis == "far":
            f = partner(f, step, far)
        elif axis == "pair":
            p = partner(p, step, pair)
        else:
            m, q = divmod(partner(m * rep + q, step, mid * rep), rep)
        pairs.append((((f * mid + m) * pair + p) * rep + q, target))
    return pairs


def three_parts(value):
    first = value.astype(jnp.bfloat16).astype(jnp.float32)
    second = (value - first).astype(jnp.bfloat16).astype(jnp.float32)
    return first, second, value - first - second


def stack_rows(feat):
    return 6 * feat + 16


def norm_rows(values):
    width = next(value.shape[1] for value in values if not isinstance(value, float))
    halves = []
    for half in (values[:8], values[8:]):
        line = lax.broadcasted_iota(jnp.int32, (8, width), 0)
        rows = jnp.zeros((8, width), jnp.float32)
        for arrays in (False, True):
            for k, value in enumerate(half):
                if isinstance(value, float) != arrays:
                    rows = jnp.where(line == k, value, rows)
        halves.append(rows)
    return jnp.concatenate(halves, axis=0)


def norm_parts(z, first):
    high = jnp.sum(first * first, axis=0, keepdims=True)
    low = jnp.sum((z - first) * (z + first), axis=0, keepdims=True)
    one = high.astype(jnp.bfloat16).astype(jnp.float32)
    left = (high - one) + low
    two = left.astype(jnp.bfloat16).astype(jnp.float32)
    return one, two, left - two


def column_stack(z):
    a, b, c = three_parts(z)
    norms = norm_rows([*norm_parts(z, a), 1.0, 1.0, 1.0, 3.0, 3.0, 3.0, 1.0])
    return jnp.concatenate([a, norms, a, b, a, c, b], axis=0)


def row_stack(z, tripled):
    norms = norm_parts(z, three_parts(z)[0])
    a, b, c = three_parts(z * (-6.0 if tripled else -2.0))
    if tripled:
        norms = norm_rows([3.0] * 3 + [0.0] * 3 + [*norms])
    else:
        norms = norm_rows([1.0] * 3 + [*norms] + [0.0] * 3 + [1.0])
    return jnp.concatenate([a, norms, b, a, c, a, b], axis=0)


def packed_pieces(count, width):
    rest = width % LANES
    return LANES // rest if width > LANES and rest and LANES % rest == 0 and count % 8 == 0 else 0


def packed_shape(count, width):
    fit = packed_pieces(count, width)
    if not fit:
        return count, width
    return width // LANES * count + -(-(count // 8) // fit) * 8, LANES


def pack_kernel(block_ref, out_ref):
    block = block_ref[...]
    count, width = block.shape
    fit = packed_pieces(count, width)
    if not fit:
        out_ref[...] = block
        return
    full = width // LANES
    for k in range(full):
        out_ref[k * count : (k + 1) * count, :] = block[:, k * LANES : (k + 1) * LANES]
    base = full * count
    pieces = [block[at : at + 8, full * LANES :] for at in range(0, count, 8)]
    for first in range(0, len(pieces), fit):
        line = pieces[first : first + fit]
        line += [jnp.zeros_like(line[0])] * (fit - len(line))
        out_ref[base + first // fit * 8 : base + first // fit * 8 + 8, :] = jnp.concatenate(line, axis=1)


def line_shape(count, width, blocks):
    return -(-blocks * width // LANES) * count, LANES


def line_kernel(count, width, *refs):
    block_refs, out_ref = refs[:-1], refs[-1]
    fit = packed_pieces(count, width)
    full, rest = width // LANES, width % LANES
    if not fit:
        joined = [ref[...] for ref in block_refs]
    else:
        joined, at = [], 0
        for ref in block_refs:
            for k in range(full):
                out_ref[at : at + count, :] = ref[k * count : (k + 1) * count, :]
                at += count
            pieces = []
            for k in range(count // 8):
                begin = full * count + k // fit * 8
                pieces.append(ref[begin : begin + 8, k % fit * rest : (k % fit + 1) * rest])
            joined.append(jnp.concatenate(pieces, axis=0))
    begin = 0 if not fit else len(block_refs) * full * count
    over = -sum(item.shape[1] for item in joined) % LANES
    if over:
        joined.append(jnp.zeros((count, over), jnp.float32))
    tails = jnp.concatenate(joined, axis=1)
    for k in range(tails.shape[1] // LANES):
        out_ref[begin + k * count : begin + (k + 1) * count, :] = tails[:, k * LANES : (k + 1) * LANES]


def piece_values(scale, row_feat, piece):
    feat = scale.shape[0]
    rows = row_feat.shape[0] // 2
    col_feat = column_stack(piece[:feat] * scale).astype(jnp.bfloat16)
    vec = piece[feat:]
    vec_high = vec.astype(jnp.bfloat16)
    vec_low = (vec - vec_high.astype(jnp.float32)).astype(jnp.bfloat16)
    vec_parts = jnp.concatenate([vec_high, vec_low], axis=0)
    both = jnp.dot(row_feat, col_feat, preferred_element_type=jnp.float32)
    square = jnp.maximum(both[:rows], 1e-30)
    root = square * lax.rsqrt(square)
    value = (jnp.maximum(both[rows:], 1.0) + root) * jnp.exp2(root * (-1.0 / math.log(2.0)))
    high = value.astype(jnp.bfloat16)
    low = (value - high.astype(jnp.float32)).astype(jnp.bfloat16)
    return [high, low], [vec_parts, vec_parts]


def add_columns(total, scale, row_feat, line_refs, count):
    def products(pieces):
        values, vectors = [], []
        for piece in pieces:
            value, vector = piece_values(scale, row_feat, piece)
            values += value
            vectors += vector
        values, vectors = jnp.concatenate(values, axis=1), jnp.concatenate(vectors, axis=1)
        return lax.dot_general(vectors, values, (((1,), (1,)), ((), ())), preferred_element_type=jnp.float32)

    numbers = [ref.shape[0] // count for ref in line_refs]
    if sum(numbers) <= 16:
        pieces = [ref[k * count : (k + 1) * count, :] for ref, number in zip(line_refs, numbers) for k in range(number)]
        return total + products(pieces)
    for ref, number in zip(line_refs, numbers):

        def add(k, total, ref=ref):
            return total + products([ref[pl.ds(pl.multiple_of(k * count, 8), count), :]])

        total = lax.fori_loop(0, number, add, total)
    return total


def first_kernel(nrow, count, scale_ref, *refs):
    row_refs, line_refs = refs[:nrow], refs[nrow : -2 - nrow]
    total_refs, feat_ref, scale_out = refs[-2 - nrow : -2], refs[-2], refs[-1]
    feat, width = row_refs[0].shape
    scale = jnp.broadcast_to(jnp.sqrt(jnp.float32(5.0 / 3.0)) / scale_ref[...], (feat, LANES))
    scale_out[...] = scale
    for k, ref in enumerate(row_refs):
        z = ref[...] * scale[:, :1]
        begin = 2 * k * width
        feat_ref[begin : begin + width, :] = row_stack(z, True).T.astype(jnp.bfloat16)
        feat_ref[begin + width : begin + 2 * width, :] = row_stack(z, False).T.astype(jnp.bfloat16)
    for k, ref in enumerate(total_refs):
        rows = feat_ref[2 * k * width : 2 * (k + 1) * width, :]
        ref[...] = add_columns(jnp.zeros(ref.shape, jnp.float32), scale, rows, line_refs, count)


def middle_kernel(nrow, count, scale_ref, feat_ref, *refs):
    before_refs, line_refs, total_refs = refs[:nrow], refs[nrow:-nrow], refs[-nrow:]
    width = total_refs[0].shape[1]
    for k, (before, after) in enumerate(zip(before_refs, total_refs)):
        rows = feat_ref[2 * k * width : 2 * (k + 1) * width, :]
        after[...] = add_columns(before[...], scale_ref[...], rows, line_refs, count)


def last_kernel(count, number, scale_ref, feat_ref, before_ref, *refs):
    nvec, width = refs[-1].shape
    rows = feat_ref[2 * number * width : 2 * (number + 1) * width, :]
    part = add_columns(before_ref[...], scale_ref[...], rows, refs[:-1], count)
    refs[-1][...] = part[:nvec] + part[nvec:]


def limits(rows, cols):
    return {
        "compiler_params": pltpu.CompilerParams(vmem_limit_bytes=4 * MIB + 4096 * rows + 2048 * cols),
        "cost_estimate": pl.CostEstimate(flops=0, bytes_accessed=0, transcendentals=0),
    }


def per_device(sizes, points, vectors, lengthscales):
    far, mid, pair, rep = sizes
    (feat, width), nvec = points.shape, vectors.shape[0]
    count, rows = feat + nvec, pair * width
    high, wide = packed_shape(count, width)

    def send(item, axis, step):
        return lax.ppermute(item, AXES, permutation(sizes, axis, step))

    def call(body, lines, out_shape, *operands):
        cols = sum(line.shape[0] for line in lines) // count * LANES
        return pl.pallas_call(
            body,
            out_shape=[jax.ShapeDtypeStruct(shape, dtype) for shape, dtype in out_shape],
            **limits(rows, cols),
        )(*operands, *lines)

    block = pl.pallas_call(
        pack_kernel,
        out_shape=jax.ShapeDtypeStruct((high, wide), jnp.float32),
        compiler_params=pltpu.CompilerParams(vmem_limit_bytes=2 * MIB),
    )(jnp.concatenate([points, vectors], axis=0))
    later_points, block = lax.optimization_barrier((points, block))
    blocks = [send(block, "far", k) for k in [*range(far - 1, 2, -1), 1, 2][: far - 1]]
    row_points = [send(later_points, "pair", k) for k in range(1, pair)]
    blocks, row_points = lax.optimization_barrier((blocks, row_points))
    line = pl.pallas_call(
        functools.partial(line_kernel, count, width),
        out_shape=jax.ShapeDtypeStruct(line_shape(count, width, far), jnp.float32),
        compiler_params=pltpu.CompilerParams(vmem_limit_bytes=2 * MIB + 16 * far * high * wide),
    )(block, *blocks)
    plane = [send(line, "plane", k) for k in reversed(range(1, mid * rep))]
    totals = [((2 * nvec, width), jnp.float32)] * pair
    *total, row_feat, scale = call(
        functools.partial(first_kernel, pair, count),
        [line],
        totals + [((2 * rows, stack_rows(feat)), jnp.bfloat16), ((feat, LANES), jnp.float32)],
        lengthscales[:, None],
        points,
        *row_points,
    )
    early, late = plane[:-2], plane[-2:]
    if early:
        total, early = lax.optimization_barrier((total, early))
        total = call(functools.partial(middle_kernel, pair, count), early, totals, scale, row_feat, *total)
    total, late = lax.optimization_barrier((total, late))

    def finish(k, total):
        body = functools.partial(last_kernel, count, k)
        (part,) = call(body, late, [((nvec, width), jnp.float32)], scale, row_feat, total[k])
        return part

    parts = []
    for k in range(1, pair):
        part = finish(k, total)
        total, part = lax.optimization_barrier((total, part))
        parts.append(part)
    result = finish(0, total)
    for k, part in enumerate(parts, 1):
        back = [(target, source) for source, target in permutation(sizes, "pair", k)]
        result = result + lax.ppermute(part, AXES, back)
    return result


def solution(mesh):
    sizes = split_blocks(mesh.shape["blk"], mesh.shape["rep"])
    return jax.shard_map(
        functools.partial(per_device, sizes),
        mesh=mesh,
        in_specs=(P(None, AXES), P(None, AXES), P()),
        out_specs=P(None, AXES),
        check_vma=False,
    )
```

```python
import functools
import math

import jax
import jax.numpy as jnp
from jax import lax
from jax.experimental import pallas as pl
from jax.experimental.pallas import tpu as pltpu
from jax.sharding import PartitionSpec as P

AXES = ("blk", "rep")
LANES = 128
MIB = 1024 * 1024


def split_blocks(blk, rep):
    pair = 2 if blk % 2 == 0 else 1
    line = blk // pair
    mid = max(d for d in range(1, line + 1) if line % d == 0 and d * d <= line)
    return line // mid, mid, pair, rep


def partner(index, step, size):
    return index ^ step if size & (size - 1) == 0 else (index + step) % size


def permutation(sizes, axis, step):
    far, mid, pair, rep = sizes
    pairs = []
    for target in range(far * mid * pair * rep):
        rest, q = divmod(target, rep)
        rest, p = divmod(rest, pair)
        f, m = divmod(rest, mid)
        if axis == "far":
            f = partner(f, step, far)
        elif axis == "pair":
            p = partner(p, step, pair)
        else:
            m, q = divmod(partner(m * rep + q, step, mid * rep), rep)
        pairs.append((((f * mid + m) * pair + p) * rep + q, target))
    return pairs


def three_parts(value):
    first = value.astype(jnp.bfloat16).astype(jnp.float32)
    second = (value - first).astype(jnp.bfloat16).astype(jnp.float32)
    return first, second, value - first - second


def stack_rows(feat):
    return 6 * feat + 16


def norm_rows(values):
    width = next(value.shape[1] for value in values if not isinstance(value, float))
    halves = []
    for half in (values[:8], values[8:]):
        line = lax.broadcasted_iota(jnp.int32, (8, width), 0)
        rows = jnp.zeros((8, width), jnp.float32)
        for arrays in (False, True):
            for k, value in enumerate(half):
                if isinstance(value, float) != arrays:
                    rows = jnp.where(line == k, value, rows)
        halves.append(rows)
    return jnp.concatenate(halves, axis=0)


def norm_parts(z, first):
    high = jnp.sum(first * first, axis=0, keepdims=True)
    low = jnp.sum((z - first) * (z + first), axis=0, keepdims=True)
    one = high.astype(jnp.bfloat16).astype(jnp.float32)
    left = (high - one) + low
    two = left.astype(jnp.bfloat16).astype(jnp.float32)
    return one, two, left - two


def column_stack(z):
    a, b, c = three_parts(z)
    norms = norm_rows([*norm_parts(z, a), 1.0, 1.0, 1.0, 3.0, 3.0, 3.0, 1.0])
    return jnp.concatenate([a, norms, a, b, a, c, b], axis=0)


def row_stack(z, tripled):
    norms = norm_parts(z, three_parts(z)[0])
    a, b, c = three_parts(z * (-6.0 if tripled else -2.0))
    if tripled:
        norms = norm_rows([3.0] * 3 + [0.0] * 3 + [*norms])
    else:
        norms = norm_rows([1.0] * 3 + [*norms] + [0.0] * 3 + [1.0])
    return jnp.concatenate([a, norms, b, a, c, a, b], axis=0)


def packed_pieces(count, width):
    rest = width % LANES
    return LANES // rest if width > LANES and rest and LANES % rest == 0 and count % 8 == 0 else 0


def packed_shape(count, width):
    fit = packed_pieces(count, width)
    if not fit:
        return count, width
    return width // LANES * count + -(-(count // 8) // fit) * 8, LANES


def pack_kernel(block_ref, out_ref):
    block = block_ref[...]
    count, width = block.shape
    fit = packed_pieces(count, width)
    if not fit:
        out_ref[...] = block
        return
    full = width // LANES
    for k in range(full):
        out_ref[k * count : (k + 1) * count, :] = block[:, k * LANES : (k + 1) * LANES]
    base = full * count
    pieces = [block[at : at + 8, full * LANES :] for at in range(0, count, 8)]
    for first in range(0, len(pieces), fit):
        line = pieces[first : first + fit]
        line += [jnp.zeros_like(line[0])] * (fit - len(line))
        out_ref[base + first // fit * 8 : base + first // fit * 8 + 8, :] = jnp.concatenate(line, axis=1)


def line_shape(count, width, blocks):
    return -(-blocks * width // LANES) * count, LANES


def line_kernel(count, width, *refs):
    block_refs, out_ref = refs[:-1], refs[-1]
    fit = packed_pieces(count, width)
    full, rest = width // LANES, width % LANES
    if not fit:
        joined = [ref[...] for ref in block_refs]
    else:
        joined, at = [], 0
        for ref in block_refs:
            for k in range(full):
                out_ref[at : at + count, :] = ref[k * count : (k + 1) * count, :]
                at += count
            pieces = []
            for k in range(count // 8):
                begin = full * count + k // fit * 8
                pieces.append(ref[begin : begin + 8, k % fit * rest : (k % fit + 1) * rest])
            joined.append(jnp.concatenate(pieces, axis=0))
    begin = 0 if not fit else len(block_refs) * full * count
    over = -sum(item.shape[1] for item in joined) % LANES
    if over:
        joined.append(jnp.zeros((count, over), jnp.float32))
    tails = jnp.concatenate(joined, axis=1)
    for k in range(tails.shape[1] // LANES):
        out_ref[begin + k * count : begin + (k + 1) * count, :] = tails[:, k * LANES : (k + 1) * LANES]


def piece_values(scale, row_feat, piece):
    feat = scale.shape[0]
    rows = row_feat.shape[0] // 2
    col_feat = column_stack(piece[:feat] * scale).astype(jnp.bfloat16)
    vec = piece[feat:]
    vec_high = vec.astype(jnp.bfloat16)
    vec_low = (vec - vec_high.astype(jnp.float32)).astype(jnp.bfloat16)
    vec_parts = jnp.concatenate([vec_high, vec_low], axis=0)
    both = jnp.dot(row_feat, col_feat, preferred_element_type=jnp.float32)
    square = jnp.maximum(both[:rows], 1e-30)
    root = square * lax.rsqrt(square)
    value = (jnp.maximum(both[rows:], 1.0) + root) * jnp.exp2(root * (-1.0 / math.log(2.0)))
    high = value.astype(jnp.bfloat16)
    low = (value - high.astype(jnp.float32)).astype(jnp.bfloat16)
    return [high, low], [vec_parts, vec_parts]


def add_columns(total, scale, row_feat, line_refs, count):
    def products(pieces):
        values, vectors = [], []
        for piece in pieces:
            value, vector = piece_values(scale, row_feat, piece)
            values += value
            vectors += vector
        values, vectors = jnp.concatenate(values, axis=1), jnp.concatenate(vectors, axis=1)
        return lax.dot_general(vectors, values, (((1,), (1,)), ((), ())), preferred_element_type=jnp.float32)

    numbers = [ref.shape[0] // count for ref in line_refs]
    if sum(numbers) <= 16:
        pieces = [ref[k * count : (k + 1) * count, :] for ref, number in zip(line_refs, numbers) for k in range(number)]
        return total + products(pieces)
    for ref, number in zip(line_refs, numbers):

        def add(k, total, ref=ref):
            return total + products([ref[pl.ds(pl.multiple_of(k * count, 8), count), :]])

        total = lax.fori_loop(0, number, add, total)
    return total


def first_kernel(nrow, count, scale_ref, *refs):
    row_refs, line_refs = refs[:nrow], refs[nrow : -2 - nrow]
    total_refs, feat_ref, scale_out = refs[-2 - nrow : -2], refs[-2], refs[-1]
    feat, width = row_refs[0].shape
    scale = jnp.broadcast_to(jnp.sqrt(jnp.float32(5.0 / 3.0)) / scale_ref[...], (feat, LANES))
    scale_out[...] = scale
    for k, ref in enumerate(row_refs):
        z = ref[...] * scale[:, :1]
        begin = 2 * k * width
        feat_ref[begin : begin + width, :] = row_stack(z, True).T.astype(jnp.bfloat16)
        feat_ref[begin + width : begin + 2 * width, :] = row_stack(z, False).T.astype(jnp.bfloat16)
    for k, ref in enumerate(total_refs):
        rows = feat_ref[2 * k * width : 2 * (k + 1) * width, :]
        ref[...] = add_columns(jnp.zeros(ref.shape, jnp.float32), scale, rows, line_refs, count)


def middle_kernel(nrow, count, scale_ref, feat_ref, *refs):
    before_refs, line_refs, total_refs = refs[: nrow - 1], refs[nrow - 1 : 1 - nrow], refs[1 - nrow :]
    width = total_refs[0].shape[1]
    for k, (before, after) in enumerate(zip(before_refs, total_refs), 1):
        rows = feat_ref[2 * k * width : 2 * (k + 1) * width, :]
        after[...] = add_columns(before[...], scale_ref[...], rows, line_refs, count)


def last_kernel(count, number, scale_ref, feat_ref, before_ref, *refs):
    nvec, width = refs[-1].shape
    rows = feat_ref[2 * number * width : 2 * (number + 1) * width, :]
    part = add_columns(before_ref[...], scale_ref[...], rows, refs[:-1], count)
    refs[-1][...] = part[:nvec] + part[nvec:]


def limits(rows, cols):
    return {
        "compiler_params": pltpu.CompilerParams(vmem_limit_bytes=4 * MIB + 4096 * rows + 2048 * cols),
        "cost_estimate": pl.CostEstimate(flops=0, bytes_accessed=0, transcendentals=0),
    }


def per_device(sizes, points, vectors, lengthscales):
    far, mid, pair, rep = sizes
    (feat, width), nvec = points.shape, vectors.shape[0]
    count, rows = feat + nvec, pair * width
    high, wide = packed_shape(count, width)

    def send(item, axis, step):
        return lax.ppermute(item, AXES, permutation(sizes, axis, step))

    def call(body, lines, out_shape, *operands):
        cols = sum(line.shape[0] for line in lines) // count * LANES
        return pl.pallas_call(
            body,
            out_shape=[jax.ShapeDtypeStruct(shape, dtype) for shape, dtype in out_shape],
            **limits(rows, cols),
        )(*operands, *lines)

    block = pl.pallas_call(
        pack_kernel,
        out_shape=jax.ShapeDtypeStruct((high, wide), jnp.float32),
        compiler_params=pltpu.CompilerParams(vmem_limit_bytes=2 * MIB),
    )(jnp.concatenate([points, vectors], axis=0))
    later_points, block = lax.optimization_barrier((points, block))
    blocks = [send(block, "far", k) for k in [*range(2, far), 1][: far - 1]]
    row_points = [send(later_points, "pair", k) for k in range(1, pair)]
    blocks, row_points = lax.optimization_barrier((blocks, row_points))
    line = pl.pallas_call(
        functools.partial(line_kernel, count, width),
        out_shape=jax.ShapeDtypeStruct(line_shape(count, width, far), jnp.float32),
        compiler_params=pltpu.CompilerParams(vmem_limit_bytes=2 * MIB + 16 * far * high * wide),
    )(block, *blocks)
    plane = [send(line, "plane", k) for k in reversed(range(1, mid * rep))]
    totals = [((2 * nvec, width), jnp.float32)] * pair
    *total, row_feat, scale = call(
        functools.partial(first_kernel, pair, count),
        [line],
        totals + [((2 * rows, stack_rows(feat)), jnp.bfloat16), ((feat, LANES), jnp.float32)],
        lengthscales[:, None],
        points,
        *row_points,
    )
    early, late = plane[:-2], plane[-2:]
    if early and pair > 1:
        total, early = lax.optimization_barrier((total, early))
        body = functools.partial(middle_kernel, pair, count)
        total[1:] = call(body, early, totals[1:], scale, row_feat, *total[1:])
    total, late = lax.optimization_barrier((total, late))

    def finish(k, total):
        lines = late if k else early + late
        body = functools.partial(last_kernel, count, k)
        (part,) = call(body, lines, [((nvec, width), jnp.float32)], scale, row_feat, total[k])
        return part

    parts = []
    for k in range(1, pair):
        part = finish(k, total)
        total, part = lax.optimization_barrier((total, part))
        parts.append(part)
    result = finish(0, total)
    for k, part in enumerate(parts, 1):
        back = [(target, source) for source, target in permutation(sizes, "pair", k)]
        result = result + lax.ppermute(part, AXES, back)
    return result


def solution(mesh):
    sizes = split_blocks(mesh.shape["blk"], mesh.shape["rep"])
    return jax.shard_map(
        functools.partial(per_device, sizes),
        mesh=mesh,
        in_specs=(P(None, AXES), P(None, AXES), P()),
        out_specs=P(None, AXES),
        check_vma=False,
    )
```

```python
import functools
import math

import jax
import jax.numpy as jnp
from jax import lax
from jax.experimental import pallas as pl
from jax.experimental.pallas import tpu as pltpu
from jax.sharding import PartitionSpec as P

AXES = ("blk", "rep")
LANES = 128
MIB = 1024 * 1024


def split_blocks(blk, rep):
    pair = 2 if blk % 2 == 0 else 1
    line = blk // pair
    mid = max(d for d in range(1, line + 1) if line % d == 0 and d * d <= line)
    return line // mid, mid, pair, rep


def partner(index, step, size):
    return index ^ step if size & (size - 1) == 0 else (index + step) % size


def permutation(sizes, axis, step):
    far, mid, pair, rep = sizes
    pairs = []
    for target in range(far * mid * pair * rep):
        rest, q = divmod(target, rep)
        rest, p = divmod(rest, pair)
        f, m = divmod(rest, mid)
        if axis == "far":
            f = partner(f, step, far)
        elif axis == "pair":
            p = partner(p, step, pair)
        else:
            m, q = divmod(partner(m * rep + q, step, mid * rep), rep)
        pairs.append((((f * mid + m) * pair + p) * rep + q, target))
    return pairs


def three_parts(value):
    first = value.astype(jnp.bfloat16).astype(jnp.float32)
    second = (value - first).astype(jnp.bfloat16).astype(jnp.float32)
    return first, second, value - first - second


def stack_rows(feat):
    return 6 * feat + 16


def norm_rows(values):
    width = next(value.shape[1] for value in values if not isinstance(value, float))
    halves = []
    for half in (values[:8], values[8:]):
        line = lax.broadcasted_iota(jnp.int32, (8, width), 0)
        rows = jnp.zeros((8, width), jnp.float32)
        for arrays in (False, True):
            for k, value in enumerate(half):
                if isinstance(value, float) != arrays:
                    rows = jnp.where(line == k, value, rows)
        halves.append(rows)
    return jnp.concatenate(halves, axis=0)


def norm_parts(z, first):
    high = jnp.sum(first * first, axis=0, keepdims=True)
    low = jnp.sum((z - first) * (z + first), axis=0, keepdims=True)
    one = high.astype(jnp.bfloat16).astype(jnp.float32)
    left = (high - one) + low
    two = left.astype(jnp.bfloat16).astype(jnp.float32)
    return one, two, left - two


def column_stack(z):
    a, b, c = three_parts(z)
    norms = norm_rows([*norm_parts(z, a), 1.0, 1.0, 1.0, 3.0, 3.0, 3.0, 1.0])
    return jnp.concatenate([a, norms, a, b, a, c, b], axis=0)


def row_stack(z, tripled):
    norms = norm_parts(z, three_parts(z)[0])
    a, b, c = three_parts(z * (-6.0 if tripled else -2.0))
    if tripled:
        norms = norm_rows([3.0] * 3 + [0.0] * 3 + [*norms])
    else:
        norms = norm_rows([1.0] * 3 + [*norms] + [0.0] * 3 + [1.0])
    return jnp.concatenate([a, norms, b, a, c, a, b], axis=0)


def packed_pieces(count, width):
    rest = width % LANES
    return LANES // rest if width > LANES and rest and LANES % rest == 0 and count % 8 == 0 else 0


def packed_shape(count, width):
    fit = packed_pieces(count, width)
    if not fit:
        return count, width
    return width // LANES * count + -(-(count // 8) // fit) * 8, LANES


def pack_kernel(block_ref, out_ref):
    block = block_ref[...]
    count, width = block.shape
    fit = packed_pieces(count, width)
    if not fit:
        out_ref[...] = block
        return
    full = width // LANES
    for k in range(full):
        out_ref[k * count : (k + 1) * count, :] = block[:, k * LANES : (k + 1) * LANES]
    base = full * count
    pieces = [block[at : at + 8, full * LANES :] for at in range(0, count, 8)]
    for first in range(0, len(pieces), fit):
        line = pieces[first : first + fit]
        line += [jnp.zeros_like(line[0])] * (fit - len(line))
        out_ref[base + first // fit * 8 : base + first // fit * 8 + 8, :] = jnp.concatenate(line, axis=1)


def line_shape(count, width, blocks):
    return -(-blocks * width // LANES) * count, LANES


def line_kernel(count, width, *refs):
    block_refs, out_ref = refs[:-1], refs[-1]
    fit = packed_pieces(count, width)
    full, rest = width // LANES, width % LANES
    if not fit:
        joined = [ref[...] for ref in block_refs]
    else:
        joined, at = [], 0
        for ref in block_refs:
            for k in range(full):
                out_ref[at : at + count, :] = ref[k * count : (k + 1) * count, :]
                at += count
            pieces = []
            for k in range(count // 8):
                begin = full * count + k // fit * 8
                pieces.append(ref[begin : begin + 8, k % fit * rest : (k % fit + 1) * rest])
            joined.append(jnp.concatenate(pieces, axis=0))
    begin = 0 if not fit else len(block_refs) * full * count
    over = -sum(item.shape[1] for item in joined) % LANES
    if over:
        joined.append(jnp.zeros((count, over), jnp.float32))
    tails = jnp.concatenate(joined, axis=1)
    for k in range(tails.shape[1] // LANES):
        out_ref[begin + k * count : begin + (k + 1) * count, :] = tails[:, k * LANES : (k + 1) * LANES]


def piece_values(scale, row_feat, piece):
    feat = scale.shape[0]
    rows = row_feat.shape[0] // 2
    col_feat = column_stack(piece[:feat] * scale).astype(jnp.bfloat16)
    vec = piece[feat:]
    vec_high = vec.astype(jnp.bfloat16)
    vec_low = (vec - vec_high.astype(jnp.float32)).astype(jnp.bfloat16)
    vec_parts = jnp.concatenate([vec_high, vec_low], axis=0)
    both = jnp.dot(row_feat, col_feat, preferred_element_type=jnp.float32)
    square = jnp.maximum(both[:rows], 1e-30)
    root = square * lax.rsqrt(square)
    value = (jnp.maximum(both[rows:], 1.0) + root) * jnp.exp2(root * (-1.0 / math.log(2.0)))
    high = value.astype(jnp.bfloat16)
    low = (value - high.astype(jnp.float32)).astype(jnp.bfloat16)
    return [high, low], [vec_parts, vec_parts]


def add_columns(total, scale, row_feat, line_refs, count):
    def products(pieces):
        values, vectors = [], []
        for piece in pieces:
            value, vector = piece_values(scale, row_feat, piece)
            values += value
            vectors += vector
        values, vectors = jnp.concatenate(values, axis=1), jnp.concatenate(vectors, axis=1)
        return lax.dot_general(vectors, values, (((1,), (1,)), ((), ())), preferred_element_type=jnp.float32)

    numbers = [ref.shape[0] // count for ref in line_refs]
    if sum(numbers) <= 16:
        pieces = [ref[k * count : (k + 1) * count, :] for ref, number in zip(line_refs, numbers) for k in range(number)]
        return total + products(pieces)
    for ref, number in zip(line_refs, numbers):

        def add(k, total, ref=ref):
            return total + products([ref[pl.ds(pl.multiple_of(k * count, 8), count), :]])

        total = lax.fori_loop(0, number, add, total)
    return total


def first_kernel(nrow, count, scale_ref, *refs):
    row_refs, line_refs = refs[:nrow], refs[nrow : -2 - nrow]
    total_refs, feat_ref, scale_out = refs[-2 - nrow : -2], refs[-2], refs[-1]
    feat, width = row_refs[0].shape
    scale = jnp.broadcast_to(jnp.sqrt(jnp.float32(5.0 / 3.0)) / scale_ref[...], (feat, LANES))
    scale_out[...] = scale
    for k, ref in enumerate(row_refs):
        z = ref[...] * scale[:, :1]
        begin = 2 * k * width
        feat_ref[begin : begin + width, :] = row_stack(z, True).T.astype(jnp.bfloat16)
        feat_ref[begin + width : begin + 2 * width, :] = row_stack(z, False).T.astype(jnp.bfloat16)
    for k, ref in enumerate(total_refs):
        rows = feat_ref[2 * k * width : 2 * (k + 1) * width, :]
        ref[...] = add_columns(jnp.zeros(ref.shape, jnp.float32), scale, rows, line_refs, count)


def middle_kernel(nrow, count, scale_ref, feat_ref, *refs):
    before_refs, line_refs, total_refs = refs[: nrow - 1], refs[nrow - 1 : 1 - nrow], refs[1 - nrow :]
    width = total_refs[0].shape[1]
    for k, (before, after) in enumerate(zip(before_refs, total_refs), 1):
        rows = feat_ref[2 * k * width : 2 * (k + 1) * width, :]
        after[...] = add_columns(before[...], scale_ref[...], rows, line_refs, count)


def last_kernel(count, number, scale_ref, feat_ref, before_ref, *refs):
    nvec, width = refs[-1].shape
    rows = feat_ref[2 * number * width : 2 * (number + 1) * width, :]
    part = add_columns(before_ref[...], scale_ref[...], rows, refs[:-1], count)
    refs[-1][...] = part[:nvec] + part[nvec:]


def limits(rows, cols):
    return {
        "compiler_params": pltpu.CompilerParams(vmem_limit_bytes=4 * MIB + 4096 * rows + 2048 * cols),
        "cost_estimate": pl.CostEstimate(flops=0, bytes_accessed=0, transcendentals=0),
    }


def per_device(sizes, points, vectors, lengthscales):
    far, mid, pair, rep = sizes
    (feat, width), nvec = points.shape, vectors.shape[0]
    count, rows = feat + nvec, pair * width
    high, wide = packed_shape(count, width)

    def send(item, axis, step):
        return lax.ppermute(item, AXES, permutation(sizes, axis, step))

    def call(body, lines, out_shape, *operands):
        cols = sum(line.shape[0] for line in lines) // count * LANES
        return pl.pallas_call(
            body,
            out_shape=[jax.ShapeDtypeStruct(shape, dtype) for shape, dtype in out_shape],
            **limits(rows, cols),
        )(*operands, *lines)

    block = pl.pallas_call(
        pack_kernel,
        out_shape=jax.ShapeDtypeStruct((high, wide), jnp.float32),
        compiler_params=pltpu.CompilerParams(vmem_limit_bytes=2 * MIB),
    )(jnp.concatenate([points, vectors], axis=0))
    later_points, block = lax.optimization_barrier((points, block))
    blocks = [send(block, "far", k) for k in [*range(2, far), 1][: far - 1]]
    row_points = [send(later_points, "pair", k) for k in range(1, pair)]
    blocks, row_points = lax.optimization_barrier((blocks, row_points))
    line = pl.pallas_call(
        functools.partial(line_kernel, count, width),
        out_shape=jax.ShapeDtypeStruct(line_shape(count, width, far), jnp.float32),
        compiler_params=pltpu.CompilerParams(vmem_limit_bytes=2 * MIB + 16 * far * high * wide),
    )(block, *blocks)
    steps = list(range(1, mid * rep))
    plane = [send(line, "plane", k) for k in steps[1:] + steps[:1]]
    totals = [((2 * nvec, width), jnp.float32)] * pair
    *total, row_feat, scale = call(
        functools.partial(first_kernel, pair, count),
        [line],
        totals + [((2 * rows, stack_rows(feat)), jnp.bfloat16), ((feat, LANES), jnp.float32)],
        lengthscales[:, None],
        points,
        *row_points,
    )
    early, late = plane[:-2], plane[-2:]
    if early and pair > 1:
        total, early = lax.optimization_barrier((total, early))
        body = functools.partial(middle_kernel, pair, count)
        total[1:] = call(body, early, totals[1:], scale, row_feat, *total[1:])
    total, late = lax.optimization_barrier((total, late))

    def finish(k, total):
        lines = late if k else early + late
        body = functools.partial(last_kernel, count, k)
        (part,) = call(body, lines, [((nvec, width), jnp.float32)], scale, row_feat, total[k])
        return part

    parts = []
    for k in range(1, pair):
        part = finish(k, total)
        total, part = lax.optimization_barrier((total, part))
        parts.append(part)
    result = finish(0, total)
    for k, part in enumerate(parts, 1):
        back = [(target, source) for source, target in permutation(sizes, "pair", k)]
        result = result + lax.ppermute(part, AXES, back)
    return result


def solution(mesh):
    sizes = split_blocks(mesh.shape["blk"], mesh.shape["rep"])
    return jax.shard_map(
        functools.partial(per_device, sizes),
        mesh=mesh,
        in_specs=(P(None, AXES), P(None, AXES), P()),
        out_specs=P(None, AXES),
        check_vma=False,
    )
```

```python
import functools
import math

import jax
import jax.numpy as jnp
from jax import lax
from jax.experimental import pallas as pl
from jax.experimental.pallas import tpu as pltpu
from jax.sharding import PartitionSpec as P

AXES = ("blk", "rep")
LANES = 128
MIB = 1024 * 1024


def split_blocks(blk, rep):
    pair = 2 if blk % 2 == 0 else 1
    line = blk // pair
    mid = max(d for d in range(1, line + 1) if line % d == 0 and d * d <= line)
    return line // mid, mid, pair, rep


def partner(index, step, size):
    return index ^ step if size & (size - 1) == 0 else (index + step) % size


def permutation(sizes, axis, step):
    far, mid, pair, rep = sizes
    pairs = []
    for target in range(far * mid * pair * rep):
        rest, q = divmod(target, rep)
        rest, p = divmod(rest, pair)
        f, m = divmod(rest, mid)
        if axis == "far":
            f = partner(f, step, far)
        elif axis == "pair":
            p = partner(p, step, pair)
        else:
            m, q = divmod(partner(m * rep + q, step, mid * rep), rep)
        pairs.append((((f * mid + m) * pair + p) * rep + q, target))
    return pairs


def three_parts(value):
    first = value.astype(jnp.bfloat16).astype(jnp.float32)
    second = (value - first).astype(jnp.bfloat16).astype(jnp.float32)
    return first, second, value - first - second


def stack_rows(feat):
    return 6 * feat + 16


def norm_rows(values):
    width = next(value.shape[1] for value in values if not isinstance(value, float))
    halves = []
    for half in (values[:8], values[8:]):
        line = lax.broadcasted_iota(jnp.int32, (8, width), 0)
        rows = jnp.zeros((8, width), jnp.float32)
        for arrays in (False, True):
            for k, value in enumerate(half):
                if isinstance(value, float) != arrays:
                    rows = jnp.where(line == k, value, rows)
        halves.append(rows)
    return jnp.concatenate(halves, axis=0)


def norm_parts(z, first):
    high = jnp.sum(first * first, axis=0, keepdims=True)
    low = jnp.sum((z - first) * (z + first), axis=0, keepdims=True)
    one = high.astype(jnp.bfloat16).astype(jnp.float32)
    left = (high - one) + low
    two = left.astype(jnp.bfloat16).astype(jnp.float32)
    return one, two, left - two


def column_stack(z):
    a, b, c = three_parts(z)
    norms = norm_rows([*norm_parts(z, a), 1.0, 1.0, 1.0, 3.0, 3.0, 3.0, 1.0])
    return jnp.concatenate([a, norms, a, b, a, c, b], axis=0)


def row_stack(z, tripled):
    norms = norm_parts(z, three_parts(z)[0])
    a, b, c = three_parts(z * (-6.0 if tripled else -2.0))
    if tripled:
        norms = norm_rows([3.0] * 3 + [0.0] * 3 + [*norms])
    else:
        norms = norm_rows([1.0] * 3 + [*norms] + [0.0] * 3 + [1.0])
    return jnp.concatenate([a, norms, b, a, c, a, b], axis=0)


def packed_pieces(count, width):
    rest = width % LANES
    return LANES // rest if width > LANES and rest and LANES % rest == 0 and count % 8 == 0 else 0


def packed_shape(count, width):
    fit = packed_pieces(count, width)
    if not fit:
        return count, width
    return width // LANES * count + -(-(count // 8) // fit) * 8, LANES


def pack_kernel(block_ref, out_ref):
    block = block_ref[...]
    count, width = block.shape
    fit = packed_pieces(count, width)
    if not fit:
        out_ref[...] = block
        return
    full = width // LANES
    for k in range(full):
        out_ref[k * count : (k + 1) * count, :] = block[:, k * LANES : (k + 1) * LANES]
    base = full * count
    pieces = [block[at : at + 8, full * LANES :] for at in range(0, count, 8)]
    for first in range(0, len(pieces), fit):
        line = pieces[first : first + fit]
        line += [jnp.zeros_like(line[0])] * (fit - len(line))
        out_ref[base + first // fit * 8 : base + first // fit * 8 + 8, :] = jnp.concatenate(line, axis=1)


def line_shape(count, width, blocks):
    return -(-blocks * width // LANES) * count, LANES


def line_kernel(count, width, *refs):
    block_refs, out_ref = refs[:-1], refs[-1]
    fit = packed_pieces(count, width)
    full, rest = width // LANES, width % LANES
    if not fit:
        joined = [ref[...] for ref in block_refs]
    else:
        joined, at = [], 0
        for ref in block_refs:
            for k in range(full):
                out_ref[at : at + count, :] = ref[k * count : (k + 1) * count, :]
                at += count
            pieces = []
            for k in range(count // 8):
                begin = full * count + k // fit * 8
                pieces.append(ref[begin : begin + 8, k % fit * rest : (k % fit + 1) * rest])
            joined.append(jnp.concatenate(pieces, axis=0))
    begin = 0 if not fit else len(block_refs) * full * count
    over = -sum(item.shape[1] for item in joined) % LANES
    if over:
        joined.append(jnp.zeros((count, over), jnp.float32))
    tails = jnp.concatenate(joined, axis=1)
    for k in range(tails.shape[1] // LANES):
        out_ref[begin + k * count : begin + (k + 1) * count, :] = tails[:, k * LANES : (k + 1) * LANES]


def piece_values(scale, row_feat, piece):
    feat = scale.shape[0]
    rows = row_feat.shape[0] // 2
    col_feat = column_stack(piece[:feat] * scale).astype(jnp.bfloat16)
    vec = piece[feat:]
    vec_high = vec.astype(jnp.bfloat16)
    vec_low = (vec - vec_high.astype(jnp.float32)).astype(jnp.bfloat16)
    vec_parts = jnp.concatenate([vec_high, vec_low], axis=0)
    both = jnp.dot(row_feat, col_feat, preferred_element_type=jnp.float32)
    square = jnp.maximum(both[:rows], 1e-30)
    root = square * lax.rsqrt(square)
    value = (jnp.maximum(both[rows:], 1.0) + root) * jnp.exp2(root * (-1.0 / math.log(2.0)))
    high = value.astype(jnp.bfloat16)
    low = (value - high.astype(jnp.float32)).astype(jnp.bfloat16)
    return [high, low], [vec_parts, vec_parts]


def add_columns(total, scale, row_feat, line_refs, count):
    def products(pieces):
        values, vectors = [], []
        for piece in pieces:
            value, vector = piece_values(scale, row_feat, piece)
            values += value
            vectors += vector
        values, vectors = jnp.concatenate(values, axis=1), jnp.concatenate(vectors, axis=1)
        return lax.dot_general(vectors, values, (((1,), (1,)), ((), ())), preferred_element_type=jnp.float32)

    numbers = [ref.shape[0] // count for ref in line_refs]
    if sum(numbers) <= 16:
        pieces = [ref[k * count : (k + 1) * count, :] for ref, number in zip(line_refs, numbers) for k in range(number)]
        return total + products(pieces)
    for ref, number in zip(line_refs, numbers):

        def add(k, total, ref=ref):
            return total + products([ref[pl.ds(pl.multiple_of(k * count, 8), count), :]])

        total = lax.fori_loop(0, number, add, total)
    return total


def first_kernel(nrow, count, scale_ref, *refs):
    row_refs, line_refs = refs[:nrow], refs[nrow : -2 - nrow]
    total_refs, feat_ref, scale_out = refs[-2 - nrow : -2], refs[-2], refs[-1]
    feat, width = row_refs[0].shape
    scale = jnp.broadcast_to(jnp.sqrt(jnp.float32(5.0 / 3.0)) / scale_ref[...], (feat, LANES))
    scale_out[...] = scale
    for k, ref in enumerate(row_refs):
        z = ref[...] * scale[:, :1]
        begin = 2 * k * width
        feat_ref[begin : begin + width, :] = row_stack(z, True).T.astype(jnp.bfloat16)
        feat_ref[begin + width : begin + 2 * width, :] = row_stack(z, False).T.astype(jnp.bfloat16)
    for k, ref in enumerate(total_refs):
        rows = feat_ref[2 * k * width : 2 * (k + 1) * width, :]
        ref[...] = add_columns(jnp.zeros(ref.shape, jnp.float32), scale, rows, line_refs, count)


def middle_kernel(numbers, count, scale_ref, feat_ref, *refs):
    many = len(numbers)
    before_refs, line_refs, total_refs = refs[:many], refs[many:-many], refs[-many:]
    width = total_refs[0].shape[1]
    for k, before, after in zip(numbers, before_refs, total_refs):
        rows = feat_ref[2 * k * width : 2 * (k + 1) * width, :]
        after[...] = add_columns(before[...], scale_ref[...], rows, line_refs, count)


def last_kernel(count, number, scale_ref, feat_ref, before_ref, *refs):
    nvec, width = refs[-1].shape
    rows = feat_ref[2 * number * width : 2 * (number + 1) * width, :]
    part = add_columns(before_ref[...], scale_ref[...], rows, refs[:-1], count)
    refs[-1][...] = part[:nvec] + part[nvec:]


def limits(rows, cols):
    return {
        "compiler_params": pltpu.CompilerParams(vmem_limit_bytes=4 * MIB + 4096 * rows + 2048 * cols),
        "cost_estimate": pl.CostEstimate(flops=0, bytes_accessed=0, transcendentals=0),
    }


def per_device(sizes, points, vectors, lengthscales):
    far, mid, pair, rep = sizes
    (feat, width), nvec = points.shape, vectors.shape[0]
    count, rows = feat + nvec, pair * width
    high, wide = packed_shape(count, width)

    def send(item, axis, step):
        return lax.ppermute(item, AXES, permutation(sizes, axis, step))

    def call(body, lines, out_shape, *operands):
        cols = sum(line.shape[0] for line in lines) // count * LANES
        return pl.pallas_call(
            body,
            out_shape=[jax.ShapeDtypeStruct(shape, dtype) for shape, dtype in out_shape],
            **limits(rows, cols),
        )(*operands, *lines)

    block = pl.pallas_call(
        pack_kernel,
        out_shape=jax.ShapeDtypeStruct((high, wide), jnp.float32),
        compiler_params=pltpu.CompilerParams(vmem_limit_bytes=2 * MIB),
    )(jnp.concatenate([points, vectors], axis=0))
    later_points, block = lax.optimization_barrier((points, block))
    blocks = [send(block, "far", k) for k in [*range(2, far), 1][: far - 1]]
    row_points = [send(later_points, "pair", k) for k in range(1, pair)]
    blocks, row_points = lax.optimization_barrier((blocks, row_points))
    line = pl.pallas_call(
        functools.partial(line_kernel, count, width),
        out_shape=jax.ShapeDtypeStruct(line_shape(count, width, far), jnp.float32),
        compiler_params=pltpu.CompilerParams(vmem_limit_bytes=2 * MIB + 16 * far * high * wide),
    )(block, *blocks)
    steps = list(range(1, mid * rep))
    plane = [send(line, "plane", k) for k in steps[1:] + steps[:1]]
    totals = [((2 * nvec, width), jnp.float32)] * pair
    *total, row_feat, scale = call(
        functools.partial(first_kernel, pair, count),
        [line],
        totals + [((2 * rows, stack_rows(feat)), jnp.bfloat16), ((feat, LANES), jnp.float32)],
        lengthscales[:, None],
        points,
        *row_points,
    )

    def middle(total, lines, first):
        numbers = list(range(first, pair))
        if not lines or not numbers:
            return total
        total, lines = lax.optimization_barrier((total, lines))
        body = functools.partial(middle_kernel, numbers, count)
        return [*total[:first], *call(body, lines, totals[first:], scale, row_feat, *total[first:])]

    total = middle(total, plane[:-2], 0)
    total = middle(total, plane[-2:-1], 1)
    total, plane[-1:] = lax.optimization_barrier((total, plane[-1:]))

    def finish(k, total):
        lines = plane[-1:] if k else plane[-2:]
        body = functools.partial(last_kernel, count, k)
        (part,) = call(body, lines, [((nvec, width), jnp.float32)], scale, row_feat, total[k])
        return part

    parts = []
    for k in range(1, pair):
        part = finish(k, total)
        total, part = lax.optimization_barrier((total, part))
        parts.append(part)
    result = finish(0, total)
    for k, part in enumerate(parts, 1):
        back = [(target, source) for source, target in permutation(sizes, "pair", k)]
        result = result + lax.ppermute(part, AXES, back)
    return result


def solution(mesh):
    sizes = split_blocks(mesh.shape["blk"], mesh.shape["rep"])
    return jax.shard_map(
        functools.partial(per_device, sizes),
        mesh=mesh,
        in_specs=(P(None, AXES), P(None, AXES), P()),
        out_specs=P(None, AXES),
        check_vma=False,
    )
```

```python
import functools
import math

import jax
import jax.numpy as jnp
from jax import lax
from jax.experimental import pallas as pl
from jax.experimental.pallas import tpu as pltpu
from jax.sharding import PartitionSpec as P

AXES = ("blk", "rep")
LANES = 128
MIB = 1024 * 1024


def split_blocks(blk, rep):
    pair = 2 if blk % 2 == 0 else 1
    line = blk // pair
    mid = max(d for d in range(1, line + 1) if line % d == 0 and d * d <= line)
    return line // mid, mid, pair, rep


def partner(index, step, size):
    return index ^ step if size & (size - 1) == 0 else (index + step) % size


def permutation(sizes, axis, step):
    far, mid, pair, rep = sizes
    pairs = []
    for target in range(far * mid * pair * rep):
        rest, q = divmod(target, rep)
        rest, p = divmod(rest, pair)
        f, m = divmod(rest, mid)
        if axis == "far":
            f = partner(f, step, far)
        elif axis == "pair":
            p = partner(p, step, pair)
        else:
            m, q = divmod(partner(m * rep + q, step, mid * rep), rep)
        pairs.append((((f * mid + m) * pair + p) * rep + q, target))
    return pairs


def three_parts(value):
    first = value.astype(jnp.bfloat16).astype(jnp.float32)
    second = (value - first).astype(jnp.bfloat16).astype(jnp.float32)
    return first, second, value - first - second


def stack_rows(feat):
    return 6 * feat + 16


def norm_rows(values):
    width = next(value.shape[1] for value in values if not isinstance(value, float))
    halves = []
    for half in (values[:8], values[8:]):
        line = lax.broadcasted_iota(jnp.int32, (8, width), 0)
        rows = jnp.zeros((8, width), jnp.float32)
        for arrays in (False, True):
            for k, value in enumerate(half):
                if isinstance(value, float) != arrays:
                    rows = jnp.where(line == k, value, rows)
        halves.append(rows)
    return jnp.concatenate(halves, axis=0)


def norm_parts(z, first):
    high = jnp.sum(first * first, axis=0, keepdims=True)
    low = jnp.sum((z - first) * (z + first), axis=0, keepdims=True)
    one = high.astype(jnp.bfloat16).astype(jnp.float32)
    left = (high - one) + low
    two = left.astype(jnp.bfloat16).astype(jnp.float32)
    return one, two, left - two


def column_stack(z):
    a, b, c = three_parts(z)
    norms = norm_rows([*norm_parts(z, a), 1.0, 1.0, 1.0, 3.0, 3.0, 3.0, 1.0])
    return jnp.concatenate([a, norms, a, b, a, c, b], axis=0)


def row_stack(z, tripled):
    norms = norm_parts(z, three_parts(z)[0])
    a, b, c = three_parts(z * (-6.0 if tripled else -2.0))
    if tripled:
        norms = norm_rows([3.0] * 3 + [0.0] * 3 + [*norms])
    else:
        norms = norm_rows([1.0] * 3 + [*norms] + [0.0] * 3 + [1.0])
    return jnp.concatenate([a, norms, b, a, c, a, b], axis=0)


def packed_pieces(count, width):
    rest = width % LANES
    return LANES // rest if width > LANES and rest and LANES % rest == 0 and count % 8 == 0 else 0


def packed_shape(count, width):
    fit = packed_pieces(count, width)
    if not fit:
        return count, width
    return width // LANES * count + -(-(count // 8) // fit) * 8, LANES


def pack_kernel(block_ref, out_ref):
    block = block_ref[...]
    count, width = block.shape
    fit = packed_pieces(count, width)
    if not fit:
        out_ref[...] = block
        return
    full = width // LANES
    for k in range(full):
        out_ref[k * count : (k + 1) * count, :] = block[:, k * LANES : (k + 1) * LANES]
    base = full * count
    pieces = [block[at : at + 8, full * LANES :] for at in range(0, count, 8)]
    for first in range(0, len(pieces), fit):
        line = pieces[first : first + fit]
        line += [jnp.zeros_like(line[0])] * (fit - len(line))
        out_ref[base + first // fit * 8 : base + first // fit * 8 + 8, :] = jnp.concatenate(line, axis=1)


def line_shape(count, width, blocks):
    return -(-blocks * width // LANES) * count, LANES


def line_kernel(count, width, *refs):
    block_refs, out_ref = refs[:-1], refs[-1]
    fit = packed_pieces(count, width)
    full, rest = width // LANES, width % LANES
    if not fit:
        joined = [ref[...] for ref in block_refs]
    else:
        joined, at = [], 0
        for ref in block_refs:
            for k in range(full):
                out_ref[at : at + count, :] = ref[k * count : (k + 1) * count, :]
                at += count
            pieces = []
            for k in range(count // 8):
                begin = full * count + k // fit * 8
                pieces.append(ref[begin : begin + 8, k % fit * rest : (k % fit + 1) * rest])
            joined.append(jnp.concatenate(pieces, axis=0))
    begin = 0 if not fit else len(block_refs) * full * count
    over = -sum(item.shape[1] for item in joined) % LANES
    if over:
        joined.append(jnp.zeros((count, over), jnp.float32))
    tails = jnp.concatenate(joined, axis=1)
    for k in range(tails.shape[1] // LANES):
        out_ref[begin + k * count : begin + (k + 1) * count, :] = tails[:, k * LANES : (k + 1) * LANES]


def piece_values(scale, row_feat, piece):
    feat = scale.shape[0]
    rows = row_feat.shape[0] // 2
    col_feat = column_stack(piece[:feat] * scale).astype(jnp.bfloat16)
    vec = piece[feat:]
    vec_high = vec.astype(jnp.bfloat16)
    vec_low = (vec - vec_high.astype(jnp.float32)).astype(jnp.bfloat16)
    vec_parts = jnp.concatenate([vec_high, vec_low], axis=0)
    both = jnp.dot(row_feat, col_feat, preferred_element_type=jnp.float32)
    square = jnp.maximum(both[:rows], 1e-30)
    root = square * lax.rsqrt(square)
    value = (jnp.maximum(both[rows:], 1.0) + root) * jnp.exp2(root * (-1.0 / math.log(2.0)))
    high = value.astype(jnp.bfloat16)
    low = (value - high.astype(jnp.float32)).astype(jnp.bfloat16)
    return [high, low], [vec_parts, vec_parts]


def add_columns(total, scale, row_feat, line_refs, count):
    def products(pieces):
        values, vectors = [], []
        for piece in pieces:
            value, vector = piece_values(scale, row_feat, piece)
            values += value
            vectors += vector
        values, vectors = jnp.concatenate(values, axis=1), jnp.concatenate(vectors, axis=1)
        return lax.dot_general(vectors, values, (((1,), (1,)), ((), ())), preferred_element_type=jnp.float32)

    numbers = [ref.shape[0] // count for ref in line_refs]
    if sum(numbers) <= 16:
        pieces = [ref[k * count : (k + 1) * count, :] for ref, number in zip(line_refs, numbers) for k in range(number)]
        return total + products(pieces)
    for ref, number in zip(line_refs, numbers):

        def add(k, total, ref=ref):
            return total + products([ref[pl.ds(pl.multiple_of(k * count, 8), count), :]])

        total = lax.fori_loop(0, number, add, total)
    return total


def first_kernel(nrow, count, scale_ref, *refs):
    row_refs, line_refs = refs[:nrow], refs[nrow : -2 - nrow]
    total_refs, feat_ref, scale_out = refs[-2 - nrow : -2], refs[-2], refs[-1]
    feat, width = row_refs[0].shape
    scale = jnp.broadcast_to(jnp.sqrt(jnp.float32(5.0 / 3.0)) / scale_ref[...], (feat, LANES))
    scale_out[...] = scale
    for k, ref in enumerate(row_refs):
        z = ref[...] * scale[:, :1]
        begin = 2 * k * width
        feat_ref[begin : begin + width, :] = row_stack(z, True).T.astype(jnp.bfloat16)
        feat_ref[begin + width : begin + 2 * width, :] = row_stack(z, False).T.astype(jnp.bfloat16)
    for k, ref in enumerate(total_refs):
        rows = feat_ref[2 * k * width : 2 * (k + 1) * width, :]
        ref[...] = add_columns(jnp.zeros(ref.shape, jnp.float32), scale, rows, line_refs, count)


def middle_kernel(numbers, count, scale_ref, feat_ref, *refs):
    many = len(numbers)
    before_refs, line_refs, total_refs = refs[:many], refs[many:-many], refs[-many:]
    width = total_refs[0].shape[1]
    for k, before, after in zip(numbers, before_refs, total_refs):
        rows = feat_ref[2 * k * width : 2 * (k + 1) * width, :]
        after[...] = add_columns(before[...], scale_ref[...], rows, line_refs, count)


def last_kernel(count, number, scale_ref, feat_ref, before_ref, *refs):
    nvec, width = refs[-1].shape
    rows = feat_ref[2 * number * width : 2 * (number + 1) * width, :]
    part = add_columns(before_ref[...], scale_ref[...], rows, refs[:-1], count)
    refs[-1][...] = part[:nvec] + part[nvec:]


def limits(rows, cols):
    return {
        "compiler_params": pltpu.CompilerParams(vmem_limit_bytes=4 * MIB + 4096 * rows + 2048 * cols),
        "cost_estimate": pl.CostEstimate(flops=0, bytes_accessed=0, transcendentals=0),
    }


def per_device(sizes, points, vectors, lengthscales):
    far, mid, pair, rep = sizes
    (feat, width), nvec = points.shape, vectors.shape[0]
    count, rows = feat + nvec, pair * width
    high, wide = packed_shape(count, width)

    def send(item, axis, step):
        return lax.ppermute(item, AXES, permutation(sizes, axis, step))

    def call(body, lines, out_shape, *operands):
        cols = sum(line.shape[0] for line in lines) // count * LANES
        return pl.pallas_call(
            body,
            out_shape=[jax.ShapeDtypeStruct(shape, dtype) for shape, dtype in out_shape],
            **limits(rows, cols),
        )(*operands, *lines)

    block = pl.pallas_call(
        pack_kernel,
        out_shape=jax.ShapeDtypeStruct((high, wide), jnp.float32),
        compiler_params=pltpu.CompilerParams(vmem_limit_bytes=2 * MIB),
    )(jnp.concatenate([points, vectors], axis=0))
    later_points, block = lax.optimization_barrier((points, block))
    blocks = [send(block, "far", k) for k in [*range(2, far), 1][: far - 1]]
    row_points = [send(later_points, "pair", k) for k in range(1, pair)]
    blocks, row_points = lax.optimization_barrier((blocks, row_points))
    line = pl.pallas_call(
        functools.partial(line_kernel, count, width),
        out_shape=jax.ShapeDtypeStruct(line_shape(count, width, far), jnp.float32),
        compiler_params=pltpu.CompilerParams(vmem_limit_bytes=2 * MIB + 16 * far * high * wide),
    )(block, *blocks)
    steps = list(range(1, mid * rep))
    plane = [send(line, "plane", k) for k in steps[:1] + steps[:0:-1]]
    totals = [((2 * nvec, width), jnp.float32)] * pair
    *total, row_feat, scale = call(
        functools.partial(first_kernel, pair, count),
        [line],
        totals + [((2 * rows, stack_rows(feat)), jnp.bfloat16), ((feat, LANES), jnp.float32)],
        lengthscales[:, None],
        points,
        *row_points,
    )

    def middle(total, lines, first):
        numbers = list(range(first, pair))
        if not lines or not numbers:
            return total
        total, lines = lax.optimization_barrier((total, lines))
        body = functools.partial(middle_kernel, numbers, count)
        return [*total[:first], *call(body, lines, totals[first:], scale, row_feat, *total[first:])]

    total = middle(total, plane[:-2], 0)
    total = middle(total, plane[-2:-1], 1)
    total, plane[-1:] = lax.optimization_barrier((total, plane[-1:]))

    def finish(k, total):
        lines = plane[-1:] if k else plane[-2:]
        body = functools.partial(last_kernel, count, k)
        (part,) = call(body, lines, [((nvec, width), jnp.float32)], scale, row_feat, total[k])
        return part

    parts = []
    for k in range(1, pair):
        part = finish(k, total)
        total, part = lax.optimization_barrier((total, part))
        parts.append(part)
    result = finish(0, total)
    for k, part in enumerate(parts, 1):
        back = [(target, source) for source, target in permutation(sizes, "pair", k)]
        result = result + lax.ppermute(part, AXES, back)
    return result


def solution(mesh):
    sizes = split_blocks(mesh.shape["blk"], mesh.shape["rep"])
    return jax.shard_map(
        functools.partial(per_device, sizes),
        mesh=mesh,
        in_specs=(P(None, AXES), P(None, AXES), P()),
        out_specs=P(None, AXES),
        check_vma=False,
    )
```

```python
import functools
import math

import jax
import jax.numpy as jnp
from jax import lax
from jax.experimental import pallas as pl
from jax.experimental.pallas import tpu as pltpu
from jax.sharding import PartitionSpec as P

AXES = ("blk", "rep")
LANES = 128
MIB = 1024 * 1024


def split_blocks(blk, rep):
    pair = 2 if blk % 2 == 0 else 1
    line = blk // pair
    mid = max(d for d in range(1, line + 1) if line % d == 0 and d * d <= line)
    return line // mid, mid, pair, rep


def partner(index, step, size):
    return index ^ step if size & (size - 1) == 0 else (index + step) % size


def permutation(sizes, axis, step):
    far, mid, pair, rep = sizes
    pairs = []
    for target in range(far * mid * pair * rep):
        rest, q = divmod(target, rep)
        rest, p = divmod(rest, pair)
        f, m = divmod(rest, mid)
        if axis == "far":
            f = partner(f, step, far)
        elif axis == "pair":
            p = partner(p, step, pair)
        else:
            m, q = divmod(partner(m * rep + q, step, mid * rep), rep)
        pairs.append((((f * mid + m) * pair + p) * rep + q, target))
    return pairs


def three_parts(value):
    first = value.astype(jnp.bfloat16).astype(jnp.float32)
    second = (value - first).astype(jnp.bfloat16).astype(jnp.float32)
    return first, second, value - first - second


def stack_rows(feat):
    return 6 * feat + 16


def norm_rows(values):
    width = next(value.shape[1] for value in values if not isinstance(value, float))
    halves = []
    for half in (values[:8], values[8:]):
        line = lax.broadcasted_iota(jnp.int32, (8, width), 0)
        rows = jnp.zeros((8, width), jnp.float32)
        for arrays in (False, True):
            for k, value in enumerate(half):
                if isinstance(value, float) != arrays:
                    rows = jnp.where(line == k, value, rows)
        halves.append(rows)
    return jnp.concatenate(halves, axis=0)


def norm_parts(z, first):
    high = jnp.sum(first * first, axis=0, keepdims=True)
    low = jnp.sum((z - first) * (z + first), axis=0, keepdims=True)
    one = high.astype(jnp.bfloat16).astype(jnp.float32)
    left = (high - one) + low
    two = left.astype(jnp.bfloat16).astype(jnp.float32)
    return one, two, left - two


def column_stack(z):
    a, b, c = three_parts(z)
    norms = norm_rows([*norm_parts(z, a), 1.0, 1.0, 1.0, 3.0, 3.0, 3.0, 1.0])
    return jnp.concatenate([a, norms, a, b, a, c, b], axis=0)


def row_stack(z, tripled):
    norms = norm_parts(z, three_parts(z)[0])
    a, b, c = three_parts(z * (-6.0 if tripled else -2.0))
    if tripled:
        norms = norm_rows([3.0] * 3 + [0.0] * 3 + [*norms])
    else:
        norms = norm_rows([1.0] * 3 + [*norms] + [0.0] * 3 + [1.0])
    return jnp.concatenate([a, norms, b, a, c, a, b], axis=0)


def packed_pieces(count, width):
    rest = width % LANES
    return LANES // rest if width > LANES and rest and LANES % rest == 0 and count % 8 == 0 else 0


def packed_shape(count, width):
    fit = packed_pieces(count, width)
    if not fit:
        return count, width
    return width // LANES * count + -(-(count // 8) // fit) * 8, LANES


def pack_kernel(block_ref, out_ref):
    block = block_ref[...]
    count, width = block.shape
    fit = packed_pieces(count, width)
    if not fit:
        out_ref[...] = block
        return
    full = width // LANES
    for k in range(full):
        out_ref[k * count : (k + 1) * count, :] = block[:, k * LANES : (k + 1) * LANES]
    base = full * count
    pieces = [block[at : at + 8, full * LANES :] for at in range(0, count, 8)]
    for first in range(0, len(pieces), fit):
        line = pieces[first : first + fit]
        line += [jnp.zeros_like(line[0])] * (fit - len(line))
        out_ref[base + first // fit * 8 : base + first // fit * 8 + 8, :] = jnp.concatenate(line, axis=1)


def line_shape(count, width, blocks):
    return -(-blocks * width // LANES) * count, LANES


def line_kernel(count, width, *refs):
    block_refs, out_ref = refs[:-1], refs[-1]
    fit = packed_pieces(count, width)
    full, rest = width // LANES, width % LANES
    if not fit:
        joined = [ref[...] for ref in block_refs]
    else:
        joined, at = [], 0
        for ref in block_refs:
            for k in range(full):
                out_ref[at : at + count, :] = ref[k * count : (k + 1) * count, :]
                at += count
            pieces = []
            for k in range(count // 8):
                begin = full * count + k // fit * 8
                pieces.append(ref[begin : begin + 8, k % fit * rest : (k % fit + 1) * rest])
            joined.append(jnp.concatenate(pieces, axis=0))
    begin = 0 if not fit else len(block_refs) * full * count
    over = -sum(item.shape[1] for item in joined) % LANES
    if over:
        joined.append(jnp.zeros((count, over), jnp.float32))
    tails = jnp.concatenate(joined, axis=1)
    for k in range(tails.shape[1] // LANES):
        out_ref[begin + k * count : begin + (k + 1) * count, :] = tails[:, k * LANES : (k + 1) * LANES]


def lines_kernel(count, width, *refs):
    line_kernel(count, width, *refs[:-2], refs[-2])
    line_kernel(count, width, *refs[1:-2], refs[-1])


def piece_values(scale, row_feat, piece):
    feat = scale.shape[0]
    rows = row_feat.shape[0] // 2
    col_feat = column_stack(piece[:feat] * scale).astype(jnp.bfloat16)
    vec = piece[feat:]
    vec_high = vec.astype(jnp.bfloat16)
    vec_low = (vec - vec_high.astype(jnp.float32)).astype(jnp.bfloat16)
    vec_parts = jnp.concatenate([vec_high, vec_low], axis=0)
    both = jnp.dot(row_feat, col_feat, preferred_element_type=jnp.float32)
    square = jnp.maximum(both[:rows], 1e-30)
    root = square * lax.rsqrt(square)
    value = (jnp.maximum(both[rows:], 1.0) + root) * jnp.exp2(root * (-1.0 / math.log(2.0)))
    high = value.astype(jnp.bfloat16)
    low = (value - high.astype(jnp.float32)).astype(jnp.bfloat16)
    return [high, low], [vec_parts, vec_parts]


def add_columns(total, scale, row_feat, line_refs, count):
    def products(pieces):
        values, vectors = [], []
        for piece in pieces:
            value, vector = piece_values(scale, row_feat, piece)
            values += value
            vectors += vector
        values, vectors = jnp.concatenate(values, axis=1), jnp.concatenate(vectors, axis=1)
        return lax.dot_general(vectors, values, (((1,), (1,)), ((), ())), preferred_element_type=jnp.float32)

    numbers = [ref.shape[0] // count for ref in line_refs]
    if sum(numbers) <= 16:
        pieces = [ref[k * count : (k + 1) * count, :] for ref, number in zip(line_refs, numbers) for k in range(number)]
        return total + products(pieces)
    for ref, number in zip(line_refs, numbers):

        def add(k, total, ref=ref):
            return total + products([ref[pl.ds(pl.multiple_of(k * count, 8), count), :]])

        total = lax.fori_loop(0, number, add, total)
    return total


def first_kernel(nrow, count, scale_ref, *refs):
    row_refs, line_refs = refs[:nrow], refs[nrow : -2 - nrow]
    total_refs, feat_ref, scale_out = refs[-2 - nrow : -2], refs[-2], refs[-1]
    feat, width = row_refs[0].shape
    scale = jnp.broadcast_to(jnp.sqrt(jnp.float32(5.0 / 3.0)) / scale_ref[...], (feat, LANES))
    scale_out[...] = scale
    for k, ref in enumerate(row_refs):
        z = ref[...] * scale[:, :1]
        begin = 2 * k * width
        feat_ref[begin : begin + width, :] = row_stack(z, True).T.astype(jnp.bfloat16)
        feat_ref[begin + width : begin + 2 * width, :] = row_stack(z, False).T.astype(jnp.bfloat16)
    for k, ref in enumerate(total_refs):
        rows = feat_ref[2 * k * width : 2 * (k + 1) * width, :]
        ref[...] = add_columns(jnp.zeros(ref.shape, jnp.float32), scale, rows, line_refs, count)


def middle_kernel(numbers, count, scale_ref, feat_ref, *refs):
    many = len(numbers)
    before_refs, line_refs, total_refs = refs[:many], refs[many:-many], refs[-many:]
    width = total_refs[0].shape[1]
    for k, before, after in zip(numbers, before_refs, total_refs):
        rows = feat_ref[2 * k * width : 2 * (k + 1) * width, :]
        after[...] = add_columns(before[...], scale_ref[...], rows, line_refs, count)


def last_kernel(count, number, scale_ref, feat_ref, before_ref, *refs):
    nvec, width = refs[-1].shape
    rows = feat_ref[2 * number * width : 2 * (number + 1) * width, :]
    part = add_columns(before_ref[...], scale_ref[...], rows, refs[:-1], count)
    refs[-1][...] = part[:nvec] + part[nvec:]


def limits(rows, cols):
    return {
        "compiler_params": pltpu.CompilerParams(vmem_limit_bytes=4 * MIB + 4096 * rows + 2048 * cols),
        "cost_estimate": pl.CostEstimate(flops=0, bytes_accessed=0, transcendentals=0),
    }


def per_device(sizes, points, vectors, lengthscales):
    far, mid, pair, rep = sizes
    (feat, width), nvec = points.shape, vectors.shape[0]
    count, rows = feat + nvec, pair * width
    high, wide = packed_shape(count, width)

    def send(item, axis, step):
        return lax.ppermute(item, AXES, permutation(sizes, axis, step))

    def call(body, lines, out_shape, *operands):
        cols = sum(line.shape[0] for line in lines) // count * LANES
        return pl.pallas_call(
            body,
            out_shape=[jax.ShapeDtypeStruct(shape, dtype) for shape, dtype in out_shape],
            **limits(rows, cols),
        )(*operands, *lines)

    block = pl.pallas_call(
        pack_kernel,
        out_shape=jax.ShapeDtypeStruct((high, wide), jnp.float32),
        compiler_params=pltpu.CompilerParams(vmem_limit_bytes=2 * MIB),
    )(jnp.concatenate([points, vectors], axis=0))
    later_points, block = lax.optimization_barrier((points, block))
    blocks = [send(block, "far", k) for k in [*range(2, far), 1][: far - 1]]
    steps = list(range(1, mid * rep))
    ahead = [send(block, "plane", k) for k in steps[:1]] if blocks else []
    row_points = [send(later_points, "pair", k) for k in range(1, pair)]
    blocks, ahead, row_points = lax.optimization_barrier((blocks, ahead, row_points))

    def lines_of(body, blocks, numbers):
        return pl.pallas_call(
            functools.partial(body, count, width),
            out_shape=[jax.ShapeDtypeStruct(line_shape(count, width, k), jnp.float32) for k in numbers],
            compiler_params=pltpu.CompilerParams(vmem_limit_bytes=2 * MIB + 32 * len(blocks) * high * wide),
        )(*blocks)

    if ahead:
        line, short = lines_of(lines_kernel, [block] + blocks, [far, far - 1])
    else:
        (line,) = lines_of(line_kernel, [block] + blocks, [far])
        short = line
    plane = [send(line, "plane", k) for k in steps[1:]] + [send(short, "plane", k) for k in steps[:1]]
    lines = [line] + [lines_of(line_kernel, [item], [1])[0] for item in ahead]
    totals = [((2 * nvec, width), jnp.float32)] * pair
    *total, row_feat, scale = call(
        functools.partial(first_kernel, pair, count),
        lines,
        totals + [((2 * rows, stack_rows(feat)), jnp.bfloat16), ((feat, LANES), jnp.float32)],
        lengthscales[:, None],
        points,
        *row_points,
    )

    def middle(total, lines, first):
        numbers = list(range(first, pair))
        if not lines or not numbers:
            return total
        total, lines = lax.optimization_barrier((total, lines))
        body = functools.partial(middle_kernel, numbers, count)
        return [*total[:first], *call(body, lines, totals[first:], scale, row_feat, *total[first:])]

    total = middle(total, plane[:-2], 0)
    total = middle(total, plane[-2:-1], 1)
    total, plane[-1:] = lax.optimization_barrier((total, plane[-1:]))

    def finish(k, total):
        lines = plane[-1:] if k else plane[-2:]
        body = functools.partial(last_kernel, count, k)
        (part,) = call(body, lines, [((nvec, width), jnp.float32)], scale, row_feat, total[k])
        return part

    parts = []
    for k in range(1, pair):
        part = finish(k, total)
        total, part = lax.optimization_barrier((total, part))
        parts.append(part)
    result = finish(0, total)
    for k, part in enumerate(parts, 1):
        back = [(target, source) for source, target in permutation(sizes, "pair", k)]
        result = result + lax.ppermute(part, AXES, back)
    return result


def solution(mesh):
    sizes = split_blocks(mesh.shape["blk"], mesh.shape["rep"])
    return jax.shard_map(
        functools.partial(per_device, sizes),
        mesh=mesh,
        in_specs=(P(None, AXES), P(None, AXES), P()),
        out_specs=P(None, AXES),
        check_vma=False,
    )
```

```python
import functools
import math

import jax
import jax.numpy as jnp
from jax import lax
from jax.experimental import pallas as pl
from jax.experimental.pallas import tpu as pltpu
from jax.sharding import PartitionSpec as P

AXES = ("blk", "rep")
LANES = 128
MIB = 1024 * 1024


def split_blocks(blk, rep):
    pair = 2 if blk % 2 == 0 else 1
    line = blk // pair
    mid = max(d for d in range(1, line + 1) if line % d == 0 and d * d <= line)
    return line // mid, mid, pair, rep


def partner(index, step, size):
    return index ^ step if size & (size - 1) == 0 else (index + step) % size


def permutation(sizes, axis, step):
    far, mid, pair, rep = sizes
    pairs = []
    for target in range(far * mid * pair * rep):
        rest, q = divmod(target, rep)
        rest, p = divmod(rest, pair)
        f, m = divmod(rest, mid)
        if axis == "far":
            f = partner(f, step, far)
        elif axis == "pair":
            p = partner(p, step, pair)
        else:
            m, q = divmod(partner(m * rep + q, step, mid * rep), rep)
        pairs.append((((f * mid + m) * pair + p) * rep + q, target))
    return pairs


def three_parts(value):
    first = value.astype(jnp.bfloat16).astype(jnp.float32)
    second = (value - first).astype(jnp.bfloat16).astype(jnp.float32)
    return first, second, value - first - second


def stack_rows(feat):
    return 6 * feat + 16


def norm_rows(values):
    width = next(value.shape[1] for value in values if not isinstance(value, float))
    halves = []
    for half in (values[:8], values[8:]):
        line = lax.broadcasted_iota(jnp.int32, (8, width), 0)
        rows = jnp.zeros((8, width), jnp.float32)
        for arrays in (False, True):
            for k, value in enumerate(half):
                if isinstance(value, float) != arrays:
                    rows = jnp.where(line == k, value, rows)
        halves.append(rows)
    return jnp.concatenate(halves, axis=0)


def norm_parts(z, first):
    high = jnp.sum(first * first, axis=0, keepdims=True)
    low = jnp.sum((z - first) * (z + first), axis=0, keepdims=True)
    one = high.astype(jnp.bfloat16).astype(jnp.float32)
    left = (high - one) + low
    two = left.astype(jnp.bfloat16).astype(jnp.float32)
    return one, two, left - two


def column_stack(z):
    a, b, c = three_parts(z)
    norms = norm_rows([*norm_parts(z, a), 1.0, 1.0, 1.0, 3.0, 3.0, 3.0, 1.0])
    return jnp.concatenate([a, norms, a, b, a, c, b], axis=0)


def row_stack(z, tripled):
    norms = norm_parts(z, three_parts(z)[0])
    a, b, c = three_parts(z * (-6.0 if tripled else -2.0))
    if tripled:
        norms = norm_rows([3.0] * 3 + [0.0] * 3 + [*norms])
    else:
        norms = norm_rows([1.0] * 3 + [*norms] + [0.0] * 3 + [1.0])
    return jnp.concatenate([a, norms, b, a, c, a, b], axis=0)


def packed_pieces(count, width):
    rest = width % LANES
    return LANES // rest if width > LANES and rest and LANES % rest == 0 and count % 8 == 0 else 0


def packed_shape(count, width):
    fit = packed_pieces(count, width)
    if not fit:
        return count, width
    return width // LANES * count + -(-(count // 8) // fit) * 8, LANES


def pack_kernel(block_ref, out_ref):
    block = block_ref[...]
    count, width = block.shape
    fit = packed_pieces(count, width)
    if not fit:
        out_ref[...] = block
        return
    full = width // LANES
    for k in range(full):
        out_ref[k * count : (k + 1) * count, :] = block[:, k * LANES : (k + 1) * LANES]
    base = full * count
    pieces = [block[at : at + 8, full * LANES :] for at in range(0, count, 8)]
    for first in range(0, len(pieces), fit):
        line = pieces[first : first + fit]
        line += [jnp.zeros_like(line[0])] * (fit - len(line))
        out_ref[base + first // fit * 8 : base + first // fit * 8 + 8, :] = jnp.concatenate(line, axis=1)


def line_shape(count, width, blocks):
    return -(-blocks * width // LANES) * count, LANES


def line_kernel(count, width, *refs):
    block_refs, out_ref = refs[:-1], refs[-1]
    fit = packed_pieces(count, width)
    full, rest = width // LANES, width % LANES
    if not fit:
        joined = [ref[...] for ref in block_refs]
    else:
        joined, at = [], 0
        for ref in block_refs:
            for k in range(full):
                out_ref[at : at + count, :] = ref[k * count : (k + 1) * count, :]
                at += count
            pieces = []
            for k in range(count // 8):
                begin = full * count + k // fit * 8
                pieces.append(ref[begin : begin + 8, k % fit * rest : (k % fit + 1) * rest])
            joined.append(jnp.concatenate(pieces, axis=0))
    begin = 0 if not fit else len(block_refs) * full * count
    over = -sum(item.shape[1] for item in joined) % LANES
    if over:
        joined.append(jnp.zeros((count, over), jnp.float32))
    tails = jnp.concatenate(joined, axis=1)
    for k in range(tails.shape[1] // LANES):
        out_ref[begin + k * count : begin + (k + 1) * count, :] = tails[:, k * LANES : (k + 1) * LANES]


def piece_values(scale, row_feat, piece):
    feat = scale.shape[0]
    rows = row_feat.shape[0] // 2
    col_feat = column_stack(piece[:feat] * scale).astype(jnp.bfloat16)
    vec = piece[feat:]
    vec_high = vec.astype(jnp.bfloat16)
    vec_low = (vec - vec_high.astype(jnp.float32)).astype(jnp.bfloat16)
    vec_parts = jnp.concatenate([vec_high, vec_low], axis=0)
    both = jnp.dot(row_feat, col_feat, preferred_element_type=jnp.float32)
    square = jnp.maximum(both[:rows], 1e-30)
    root = square * lax.rsqrt(square)
    value = (jnp.maximum(both[rows:], 1.0) + root) * jnp.exp2(root * (-1.0 / math.log(2.0)))
    high = value.astype(jnp.bfloat16)
    low = (value - high.astype(jnp.float32)).astype(jnp.bfloat16)
    return [high, low], [vec_parts, vec_parts]


def add_columns(total, scale, row_feat, line_refs, count):
    def products(pieces):
        values, vectors = [], []
        for piece in pieces:
            value, vector = piece_values(scale, row_feat, piece)
            values += value
            vectors += vector
        values, vectors = jnp.concatenate(values, axis=1), jnp.concatenate(vectors, axis=1)
        return lax.dot_general(vectors, values, (((1,), (1,)), ((), ())), preferred_element_type=jnp.float32)

    numbers = [ref.shape[0] // count for ref in line_refs]
    if sum(numbers) <= 16:
        pieces = [ref[k * count : (k + 1) * count, :] for ref, number in zip(line_refs, numbers) for k in range(number)]
        for piece in pieces:
            total = total + products([piece])
        return total
    for ref, number in zip(line_refs, numbers):

        def add(k, total, ref=ref):
            return total + products([ref[pl.ds(pl.multiple_of(k * count, 8), count), :]])

        total = lax.fori_loop(0, number, add, total)
    return total


def first_kernel(nrow, count, scale_ref, *refs):
    row_refs, line_refs = refs[:nrow], refs[nrow : -2 - nrow]
    total_refs, feat_ref, scale_out = refs[-2 - nrow : -2], refs[-2], refs[-1]
    feat, width = row_refs[0].shape
    scale = jnp.broadcast_to(jnp.sqrt(jnp.float32(5.0 / 3.0)) / scale_ref[...], (feat, LANES))
    scale_out[...] = scale
    for k, ref in enumerate(row_refs):
        z = ref[...] * scale[:, :1]
        begin = 2 * k * width
        feat_ref[begin : begin + width, :] = row_stack(z, True).T.astype(jnp.bfloat16)
        feat_ref[begin + width : begin + 2 * width, :] = row_stack(z, False).T.astype(jnp.bfloat16)
    for k, ref in enumerate(total_refs):
        rows = feat_ref[2 * k * width : 2 * (k + 1) * width, :]
        ref[...] = add_columns(jnp.zeros(ref.shape, jnp.float32), scale, rows, line_refs, count)


def middle_kernel(numbers, count, scale_ref, feat_ref, *refs):
    many = len(numbers)
    before_refs, line_refs, total_refs = refs[:many], refs[many:-many], refs[-many:]
    width = total_refs[0].shape[1]
    for k, before, after in zip(numbers, before_refs, total_refs):
        rows = feat_ref[2 * k * width : 2 * (k + 1) * width, :]
        after[...] = add_columns(before[...], scale_ref[...], rows, line_refs, count)


def last_kernel(count, number, scale_ref, feat_ref, before_ref, *refs):
    nvec, width = refs[-1].shape
    rows = feat_ref[2 * number * width : 2 * (number + 1) * width, :]
    part = add_columns(before_ref[...], scale_ref[...], rows, refs[:-1], count)
    refs[-1][...] = part[:nvec] + part[nvec:]


def limits(rows, cols):
    return {
        "compiler_params": pltpu.CompilerParams(vmem_limit_bytes=4 * MIB + 4096 * rows + 2048 * cols),
        "cost_estimate": pl.CostEstimate(flops=0, bytes_accessed=0, transcendentals=0),
    }


def per_device(sizes, points, vectors, lengthscales):
    far, mid, pair, rep = sizes
    (feat, width), nvec = points.shape, vectors.shape[0]
    count, rows = feat + nvec, pair * width
    high, wide = packed_shape(count, width)

    def send(item, axis, step):
        return lax.ppermute(item, AXES, permutation(sizes, axis, step))

    def call(body, lines, out_shape, *operands):
        cols = sum(line.shape[0] for line in lines) // count * LANES
        return pl.pallas_call(
            body,
            out_shape=[jax.ShapeDtypeStruct(shape, dtype) for shape, dtype in out_shape],
            **limits(rows, cols),
        )(*operands, *lines)

    block = pl.pallas_call(
        pack_kernel,
        out_shape=jax.ShapeDtypeStruct((high, wide), jnp.float32),
        compiler_params=pltpu.CompilerParams(vmem_limit_bytes=2 * MIB),
    )(jnp.concatenate([points, vectors], axis=0))
    later_points, block = lax.optimization_barrier((points, block))
    blocks = [send(block, "far", k) for k in [*range(2, far), 1][: far - 1]]
    row_points = [send(later_points, "pair", k) for k in range(1, pair)]
    blocks, row_points = lax.optimization_barrier((blocks, row_points))
    line = pl.pallas_call(
        functools.partial(line_kernel, count, width),
        out_shape=jax.ShapeDtypeStruct(line_shape(count, width, far), jnp.float32),
        compiler_params=pltpu.CompilerParams(vmem_limit_bytes=2 * MIB + 16 * far * high * wide),
    )(block, *blocks)
    steps = list(range(1, mid * rep))
    plane = [send(line, "plane", k) for k in steps[1:] + steps[:1]]
    totals = [((2 * nvec, width), jnp.float32)] * pair
    *total, row_feat, scale = call(
        functools.partial(first_kernel, pair, count),
        [line],
        totals + [((2 * rows, stack_rows(feat)), jnp.bfloat16), ((feat, LANES), jnp.float32)],
        lengthscales[:, None],
        points,
        *row_points,
    )

    def middle(total, lines, first):
        numbers = list(range(first, pair))
        if not lines or not numbers:
            return total
        total, lines = lax.optimization_barrier((total, lines))
        body = functools.partial(middle_kernel, numbers, count)
        return [*total[:first], *call(body, lines, totals[first:], scale, row_feat, *total[first:])]

    total = middle(total, plane[:-2], 0)
    total = middle(total, plane[-2:-1], 1)
    total, plane[-1:] = lax.optimization_barrier((total, plane[-1:]))

    def finish(k, total):
        lines = plane[-1:] if k else plane[-2:]
        body = functools.partial(last_kernel, count, k)
        (part,) = call(body, lines, [((nvec, width), jnp.float32)], scale, row_feat, total[k])
        return part

    parts = []
    for k in range(1, pair):
        part = finish(k, total)
        total, part = lax.optimization_barrier((total, part))
        parts.append(part)
    result = finish(0, total)
    for k, part in enumerate(parts, 1):
        back = [(target, source) for source, target in permutation(sizes, "pair", k)]
        result = result + lax.ppermute(part, AXES, back)
    return result


def solution(mesh):
    sizes = split_blocks(mesh.shape["blk"], mesh.shape["rep"])
    return jax.shard_map(
        functools.partial(per_device, sizes),
        mesh=mesh,
        in_specs=(P(None, AXES), P(None, AXES), P()),
        out_specs=P(None, AXES),
        check_vma=False,
    )
```

```python
import functools
import math

import jax
import jax.numpy as jnp
from jax import lax
from jax.experimental import pallas as pl
from jax.experimental.pallas import tpu as pltpu
from jax.sharding import PartitionSpec as P

AXES = ("blk", "rep")
LANES = 128
MIB = 1024 * 1024


def split_blocks(blk, rep):
    pair = 2 if blk % 2 == 0 else 1
    line = blk // pair
    mid = max(d for d in range(1, line + 1) if line % d == 0 and d * d <= line)
    return line // mid, mid, pair, rep


def partner(index, step, size):
    return index ^ step if size & (size - 1) == 0 else (index + step) % size


def permutation(sizes, axis, step):
    far, mid, pair, rep = sizes
    pairs = []
    for target in range(far * mid * pair * rep):
        rest, q = divmod(target, rep)
        rest, p = divmod(rest, pair)
        f, m = divmod(rest, mid)
        if axis == "far":
            f = partner(f, step, far)
        elif axis == "pair":
            p = partner(p, step, pair)
        else:
            m, q = divmod(partner(m * rep + q, step, mid * rep), rep)
        pairs.append((((f * mid + m) * pair + p) * rep + q, target))
    return pairs


def three_parts(value):
    first = value.astype(jnp.bfloat16).astype(jnp.float32)
    second = (value - first).astype(jnp.bfloat16).astype(jnp.float32)
    return first, second, value - first - second


def stack_rows(feat):
    return 6 * feat + 16


def norm_rows(values):
    width = next(value.shape[1] for value in values if not isinstance(value, float))
    halves = []
    for half in (values[:8], values[8:]):
        line = lax.broadcasted_iota(jnp.int32, (8, width), 0)
        rows = jnp.zeros((8, width), jnp.float32)
        for arrays in (False, True):
            for k, value in enumerate(half):
                if isinstance(value, float) != arrays:
                    rows = jnp.where(line == k, value, rows)
        halves.append(rows)
    return jnp.concatenate(halves, axis=0)


def norm_parts(z, first):
    high = jnp.sum(first * first, axis=0, keepdims=True)
    low = jnp.sum((z - first) * (z + first), axis=0, keepdims=True)
    one = high.astype(jnp.bfloat16).astype(jnp.float32)
    left = (high - one) + low
    two = left.astype(jnp.bfloat16).astype(jnp.float32)
    return one, two, left - two


def column_stack(z):
    a, b, c = three_parts(z)
    norms = norm_rows([*norm_parts(z, a), 1.0, 1.0, 1.0, 3.0, 3.0, 3.0, 1.0])
    return jnp.concatenate([a, norms, a, b, a, c, b], axis=0)


def row_stack(z, tripled):
    norms = norm_parts(z, three_parts(z)[0])
    a, b, c = three_parts(z * (-6.0 if tripled else -2.0))
    if tripled:
        norms = norm_rows([3.0] * 3 + [0.0] * 3 + [*norms])
    else:
        norms = norm_rows([1.0] * 3 + [*norms] + [0.0] * 3 + [1.0])
    return jnp.concatenate([a, norms, b, a, c, a, b], axis=0)


def packed_pieces(count, width):
    rest = width % LANES
    return LANES // rest if width > LANES and rest and LANES % rest == 0 and count % 8 == 0 else 0


def packed_shape(count, width):
    fit = packed_pieces(count, width)
    if not fit:
        return count, width
    return width // LANES * count + -(-(count // 8) // fit) * 8, LANES


def pack_kernel(block_ref, out_ref):
    block = block_ref[...]
    count, width = block.shape
    fit = packed_pieces(count, width)
    if not fit:
        out_ref[...] = block
        return
    full = width // LANES
    for k in range(full):
        out_ref[k * count : (k + 1) * count, :] = block[:, k * LANES : (k + 1) * LANES]
    base = full * count
    pieces = [block[at : at + 8, full * LANES :] for at in range(0, count, 8)]
    for first in range(0, len(pieces), fit):
        line = pieces[first : first + fit]
        line += [jnp.zeros_like(line[0])] * (fit - len(line))
        out_ref[base + first // fit * 8 : base + first // fit * 8 + 8, :] = jnp.concatenate(line, axis=1)


def line_shape(count, width, blocks):
    return -(-blocks * width // LANES) * count, LANES


def line_kernel(count, width, *refs):
    block_refs, out_ref = refs[:-1], refs[-1]
    fit = packed_pieces(count, width)
    full, rest = width // LANES, width % LANES
    if not fit:
        joined = [ref[...] for ref in block_refs]
    else:
        joined, at = [], 0
        for ref in block_refs:
            for k in range(full):
                out_ref[at : at + count, :] = ref[k * count : (k + 1) * count, :]
                at += count
            pieces = []
            for k in range(count // 8):
                begin = full * count + k // fit * 8
                pieces.append(ref[begin : begin + 8, k % fit * rest : (k % fit + 1) * rest])
            joined.append(jnp.concatenate(pieces, axis=0))
    begin = 0 if not fit else len(block_refs) * full * count
    over = -sum(item.shape[1] for item in joined) % LANES
    if over:
        joined.append(jnp.zeros((count, over), jnp.float32))
    tails = jnp.concatenate(joined, axis=1)
    for k in range(tails.shape[1] // LANES):
        out_ref[begin + k * count : begin + (k + 1) * count, :] = tails[:, k * LANES : (k + 1) * LANES]


def piece_values(scale, row_feat, piece):
    feat = scale.shape[0]
    rows = row_feat.shape[0] // 2
    col_feat = column_stack(piece[:feat] * scale).astype(jnp.bfloat16)
    vec = piece[feat:]
    vec_high = vec.astype(jnp.bfloat16)
    vec_low = (vec - vec_high.astype(jnp.float32)).astype(jnp.bfloat16)
    vec_parts = jnp.concatenate([vec_high, vec_low], axis=0)
    both = jnp.dot(row_feat, col_feat, preferred_element_type=jnp.float32)
    square = jnp.maximum(both[:rows], 1e-30)
    root = square * lax.rsqrt(square)
    value = (jnp.maximum(both[rows:], 1.0) + root) * jnp.exp2(root * (-1.0 / math.log(2.0)))
    high = value.astype(jnp.bfloat16)
    low = (value - high.astype(jnp.float32)).astype(jnp.bfloat16)
    return [high, low], [vec_parts, vec_parts]


def add_columns(total, scale, row_feat, line_refs, count):
    def products(pieces):
        values, vectors = [], []
        for piece in pieces:
            value, vector = piece_values(scale, row_feat, piece)
            values += value
            vectors += vector
        values, vectors = jnp.concatenate(values, axis=1), jnp.concatenate(vectors, axis=1)
        return lax.dot_general(vectors, values, (((1,), (1,)), ((), ())), preferred_element_type=jnp.float32)

    numbers = [ref.shape[0] // count for ref in line_refs]
    if sum(numbers) <= 16:
        pieces = [ref[k * count : (k + 1) * count, :] for ref, number in zip(line_refs, numbers) for k in range(number)]
        for piece in pieces:
            total = total + products([piece])
        return total
    for ref, number in zip(line_refs, numbers):

        def add(k, total, ref=ref):
            return total + products([ref[pl.ds(pl.multiple_of(k * count, 8), count), :]])

        total = lax.fori_loop(0, number, add, total)
    return total


def first_kernel(nrow, count, scale_ref, *refs):
    row_refs, line_refs = refs[:nrow], refs[nrow : -2 - nrow]
    total_refs, feat_ref, scale_out = refs[-2 - nrow : -2], refs[-2], refs[-1]
    feat, width = row_refs[0].shape
    scale = jnp.broadcast_to(jnp.sqrt(jnp.float32(5.0 / 3.0)) / scale_ref[...], (feat, LANES))
    scale_out[...] = scale
    for k, ref in enumerate(row_refs):
        z = ref[...] * scale[:, :1]
        begin = 2 * k * width
        feat_ref[begin : begin + width, :] = row_stack(z, True).T.astype(jnp.bfloat16)
        feat_ref[begin + width : begin + 2 * width, :] = row_stack(z, False).T.astype(jnp.bfloat16)
    for k, ref in enumerate(total_refs):
        rows = feat_ref[2 * k * width : 2 * (k + 1) * width, :]
        ref[...] = add_columns(jnp.zeros(ref.shape, jnp.float32), scale, rows, line_refs, count)


def middle_kernel(numbers, count, scale_ref, feat_ref, *refs):
    many = len(numbers)
    before_refs, line_refs, total_refs = refs[:many], refs[many:-many], refs[-many:]
    width = total_refs[0].shape[1]
    for k, before, after in zip(numbers, before_refs, total_refs):
        rows = feat_ref[2 * k * width : 2 * (k + 1) * width, :]
        after[...] = add_columns(before[...], scale_ref[...], rows, line_refs, count)


def last_kernel(count, number, scale_ref, feat_ref, before_ref, *refs):
    nvec, width = refs[-1].shape
    rows = feat_ref[2 * number * width : 2 * (number + 1) * width, :]
    part = add_columns(before_ref[...], scale_ref[...], rows, refs[:-1], count)
    refs[-1][...] = part[:nvec] + part[nvec:]


def sum_kernel(*refs):
    total = refs[0][...]
    for ref in refs[1:-1]:
        total = total + ref[...]
    refs[-1][...] = total


def limits(rows, cols):
    return {
        "compiler_params": pltpu.CompilerParams(vmem_limit_bytes=4 * MIB + 4096 * rows + 2048 * cols),
        "cost_estimate": pl.CostEstimate(flops=0, bytes_accessed=0, transcendentals=0),
    }


def per_device(sizes, points, vectors, lengthscales):
    far, mid, pair, rep = sizes
    (feat, width), nvec = points.shape, vectors.shape[0]
    count, rows = feat + nvec, pair * width
    high, wide = packed_shape(count, width)

    def send(item, axis, step):
        return lax.ppermute(item, AXES, permutation(sizes, axis, step))

    def call(body, lines, out_shape, *operands):
        cols = sum(line.shape[0] for line in lines) // count * LANES
        return pl.pallas_call(
            body,
            out_shape=[jax.ShapeDtypeStruct(shape, dtype) for shape, dtype in out_shape],
            **limits(rows, cols),
        )(*operands, *lines)

    block = pl.pallas_call(
        pack_kernel,
        out_shape=jax.ShapeDtypeStruct((high, wide), jnp.float32),
        compiler_params=pltpu.CompilerParams(vmem_limit_bytes=2 * MIB),
    )(jnp.concatenate([points, vectors], axis=0))
    later_points, block = lax.optimization_barrier((points, block))
    blocks = [send(block, "far", k) for k in [*range(2, far), 1][: far - 1]]
    row_points = [send(later_points, "pair", k) for k in range(1, pair)]
    blocks, row_points = lax.optimization_barrier((blocks, row_points))
    line = pl.pallas_call(
        functools.partial(line_kernel, count, width),
        out_shape=jax.ShapeDtypeStruct(line_shape(count, width, far), jnp.float32),
        compiler_params=pltpu.CompilerParams(vmem_limit_bytes=2 * MIB + 16 * far * high * wide),
    )(block, *blocks)
    steps = list(range(1, mid * rep))
    plane = [send(line, "plane", k) for k in steps[1:] + steps[:1]]
    totals = [((2 * nvec, width), jnp.float32)] * pair
    *total, row_feat, scale = call(
        functools.partial(first_kernel, pair, count),
        [line],
        totals + [((2 * rows, stack_rows(feat)), jnp.bfloat16), ((feat, LANES), jnp.float32)],
        lengthscales[:, None],
        points,
        *row_points,
    )

    def middle(total, lines, first):
        numbers = list(range(first, pair))
        if not lines or not numbers:
            return total
        total, lines = lax.optimization_barrier((total, lines))
        body = functools.partial(middle_kernel, numbers, count)
        return [*total[:first], *call(body, lines, totals[first:], scale, row_feat, *total[first:])]

    total = middle(total, plane[:-2], 0)
    total = middle(total, plane[-2:-1], 1)
    total, plane[-1:] = lax.optimization_barrier((total, plane[-1:]))

    def finish(k, total):
        lines = plane[-1:] if k else plane[-2:]
        body = functools.partial(last_kernel, count, k)
        (part,) = call(body, lines, [((nvec, width), jnp.float32)], scale, row_feat, total[k])
        return part

    parts = []
    for k in range(1, pair):
        part = finish(k, total)
        total, part = lax.optimization_barrier((total, part))
        parts.append(part)
    result = finish(0, total)
    others = []
    for k, part in enumerate(parts, 1):
        back = [(target, source) for source, target in permutation(sizes, "pair", k)]
        others.append(lax.ppermute(part, AXES, back))
    return pl.pallas_call(
        sum_kernel,
        out_shape=jax.ShapeDtypeStruct((nvec, width), jnp.float32),
        compiler_params=pltpu.CompilerParams(vmem_limit_bytes=2 * MIB),
    )(result, *others)


def solution(mesh):
    sizes = split_blocks(mesh.shape["blk"], mesh.shape["rep"])
    return jax.shard_map(
        functools.partial(per_device, sizes),
        mesh=mesh,
        in_specs=(P(None, AXES), P(None, AXES), P()),
        out_specs=P(None, AXES),
        check_vma=False,
    )
```

```python
import functools
import math

import jax
import jax.numpy as jnp
from jax import lax
from jax.experimental import pallas as pl
from jax.experimental.pallas import tpu as pltpu
from jax.sharding import PartitionSpec as P

AXES = ("blk", "rep")
LANES = 128
MIB = 1024 * 1024


def split_blocks(blk, rep):
    pair = 2 if blk % 2 == 0 else 1
    line = blk // pair
    mid = max(d for d in range(1, line + 1) if line % d == 0 and d * d <= line)
    return line // mid, mid, pair, rep


def partner(index, step, size):
    return index ^ step if size & (size - 1) == 0 else (index + step) % size


def permutation(sizes, axis, step):
    far, mid, pair, rep = sizes
    pairs = []
    for target in range(far * mid * pair * rep):
        rest, q = divmod(target, rep)
        rest, p = divmod(rest, pair)
        f, m = divmod(rest, mid)
        if axis == "far":
            f = partner(f, step, far)
        elif axis == "pair":
            p = partner(p, step, pair)
        else:
            m, q = divmod(partner(m * rep + q, step, mid * rep), rep)
        pairs.append((((f * mid + m) * pair + p) * rep + q, target))
    return pairs


def three_parts(value):
    first = value.astype(jnp.bfloat16).astype(jnp.float32)
    second = (value - first).astype(jnp.bfloat16).astype(jnp.float32)
    return first, second, value - first - second


def stack_rows(feat):
    return 6 * feat + 16


def norm_rows(values):
    width = next(value.shape[1] for value in values if not isinstance(value, float))
    halves = []
    for half in (values[:8], values[8:]):
        line = lax.broadcasted_iota(jnp.int32, (8, width), 0)
        rows = jnp.zeros((8, width), jnp.float32)
        for arrays in (False, True):
            for k, value in enumerate(half):
                if isinstance(value, float) != arrays:
                    rows = jnp.where(line == k, value, rows)
        halves.append(rows)
    return jnp.concatenate(halves, axis=0)


def norm_parts(z, first):
    high = jnp.sum(first * first, axis=0, keepdims=True)
    low = jnp.sum((z - first) * (z + first), axis=0, keepdims=True)
    one = high.astype(jnp.bfloat16).astype(jnp.float32)
    left = (high - one) + low
    two = left.astype(jnp.bfloat16).astype(jnp.float32)
    return one, two, left - two


def column_stack(z):
    a, b, c = three_parts(z)
    norms = norm_rows([*norm_parts(z, a), 1.0, 1.0, 1.0, 3.0, 3.0, 3.0, 1.0])
    return jnp.concatenate([a, norms, a, b, a, c, b], axis=0)


def row_stack(z, tripled):
    norms = norm_parts(z, three_parts(z)[0])
    a, b, c = three_parts(z * (-6.0 if tripled else -2.0))
    if tripled:
        norms = norm_rows([3.0] * 3 + [0.0] * 3 + [*norms])
    else:
        norms = norm_rows([1.0] * 3 + [*norms] + [0.0] * 3 + [1.0])
    return jnp.concatenate([a, norms, b, a, c, a, b], axis=0)


def packed_pieces(count, width):
    rest = width % LANES
    return LANES // rest if width > LANES and rest and LANES % rest == 0 and count % 8 == 0 else 0


def packed_shape(count, width):
    fit = packed_pieces(count, width)
    if not fit:
        return count, width
    return width // LANES * count + -(-(count // 8) // fit) * 8, LANES


def pack_kernel(block_ref, out_ref):
    block = block_ref[...]
    count, width = block.shape
    fit = packed_pieces(count, width)
    if not fit:
        out_ref[...] = block
        return
    full = width // LANES
    for k in range(full):
        out_ref[k * count : (k + 1) * count, :] = block[:, k * LANES : (k + 1) * LANES]
    base = full * count
    pieces = [block[at : at + 8, full * LANES :] for at in range(0, count, 8)]
    for first in range(0, len(pieces), fit):
        line = pieces[first : first + fit]
        line += [jnp.zeros_like(line[0])] * (fit - len(line))
        out_ref[base + first // fit * 8 : base + first // fit * 8 + 8, :] = jnp.concatenate(line, axis=1)


def line_shape(count, width, blocks):
    return -(-blocks * width // LANES) * count, LANES


def line_kernel(count, width, *refs):
    block_refs, out_ref = refs[:-1], refs[-1]
    fit = packed_pieces(count, width)
    full, rest = width // LANES, width % LANES
    if not fit:
        joined = [ref[...] for ref in block_refs]
    else:
        joined, at = [], 0
        for ref in block_refs:
            for k in range(full):
                out_ref[at : at + count, :] = ref[k * count : (k + 1) * count, :]
                at += count
            pieces = []
            for k in range(count // 8):
                begin = full * count + k // fit * 8
                pieces.append(ref[begin : begin + 8, k % fit * rest : (k % fit + 1) * rest])
            joined.append(jnp.concatenate(pieces, axis=0))
    begin = 0 if not fit else len(block_refs) * full * count
    over = -sum(item.shape[1] for item in joined) % LANES
    if over:
        joined.append(jnp.zeros((count, over), jnp.float32))
    tails = jnp.concatenate(joined, axis=1)
    for k in range(tails.shape[1] // LANES):
        out_ref[begin + k * count : begin + (k + 1) * count, :] = tails[:, k * LANES : (k + 1) * LANES]


def piece_values(scale, row_feat, piece):
    feat = scale.shape[0]
    rows = row_feat.shape[0] // 2
    col_feat = column_stack(piece[:feat] * scale).astype(jnp.bfloat16)
    vec = piece[feat:]
    vec_high = vec.astype(jnp.bfloat16)
    vec_low = (vec - vec_high.astype(jnp.float32)).astype(jnp.bfloat16)
    vec_parts = jnp.concatenate([vec_high, vec_low], axis=0)
    both = jnp.dot(row_feat, col_feat, preferred_element_type=jnp.float32)
    square = jnp.maximum(both[:rows], 1e-30)
    root = square * lax.rsqrt(square)
    value = (jnp.maximum(both[rows:], 1.0) + root) * jnp.exp2(root * (-1.0 / math.log(2.0)))
    high = value.astype(jnp.bfloat16)
    low = (value - high.astype(jnp.float32)).astype(jnp.bfloat16)
    return [high, low], [vec_parts, vec_parts]


def add_columns(total, scale, row_feat, line_refs, count):
    def products(pieces):
        values, vectors = [], []
        for piece in pieces:
            value, vector = piece_values(scale, row_feat, piece)
            values += value
            vectors += vector
        values, vectors = jnp.concatenate(values, axis=1), jnp.concatenate(vectors, axis=1)
        return lax.dot_general(vectors, values, (((1,), (1,)), ((), ())), preferred_element_type=jnp.float32)

    numbers = [ref.shape[0] // count for ref in line_refs]
    if sum(numbers) <= 16:
        pieces = [ref[k * count : (k + 1) * count, :] for ref, number in zip(line_refs, numbers) for k in range(number)]
        for piece in pieces:
            total = total + products([piece])
        return total
    for ref, number in zip(line_refs, numbers):

        def add(k, total, ref=ref):
            return total + products([ref[pl.ds(pl.multiple_of(k * count, 8), count), :]])

        total = lax.fori_loop(0, number, add, total)
    return total


def first_kernel(nrow, count, scale_ref, *refs):
    row_refs, line_refs = refs[:nrow], refs[nrow : -2 - nrow]
    total_refs, feat_ref, scale_out = refs[-2 - nrow : -2], refs[-2], refs[-1]
    feat, width = row_refs[0].shape
    scale = jnp.broadcast_to(jnp.sqrt(jnp.float32(5.0 / 3.0)) / scale_ref[...], (feat, LANES))
    scale_out[...] = scale
    for k, ref in enumerate(row_refs):
        z = ref[...] * scale[:, :1]
        begin = 2 * k * width
        feat_ref[begin : begin + width, :] = row_stack(z, True).T.astype(jnp.bfloat16)
        feat_ref[begin + width : begin + 2 * width, :] = row_stack(z, False).T.astype(jnp.bfloat16)
    for k, ref in enumerate(total_refs):
        rows = feat_ref[2 * k * width : 2 * (k + 1) * width, :]
        ref[...] = add_columns(jnp.zeros(ref.shape, jnp.float32), scale, rows, line_refs, count)


def middle_kernel(numbers, count, scale_ref, feat_ref, *refs):
    many = len(numbers)
    before_refs, line_refs, total_refs = refs[:many], refs[many:-many], refs[-many:]
    width = total_refs[0].shape[1]
    for k, before, after in zip(numbers, before_refs, total_refs):
        rows = feat_ref[2 * k * width : 2 * (k + 1) * width, :]
        after[...] = add_columns(before[...], scale_ref[...], rows, line_refs, count)


def last_kernel(count, number, scale_ref, feat_ref, before_ref, *refs):
    nvec, width = refs[-1].shape
    rows = feat_ref[2 * number * width : 2 * (number + 1) * width, :]
    part = add_columns(before_ref[...], scale_ref[...], rows, refs[:-1], count)
    refs[-1][...] = part[:nvec] + part[nvec:]


def limits(rows, cols):
    return {
        "compiler_params": pltpu.CompilerParams(vmem_limit_bytes=4 * MIB + 4096 * rows + 2048 * cols),
        "cost_estimate": pl.CostEstimate(flops=0, bytes_accessed=0, transcendentals=0),
    }


def per_device(sizes, points, vectors, lengthscales):
    far, mid, pair, rep = sizes
    (feat, width), nvec = points.shape, vectors.shape[0]
    count, rows = feat + nvec, pair * width
    high, wide = packed_shape(count, width)

    def send(item, axis, step):
        return lax.ppermute(item, AXES, permutation(sizes, axis, step))

    def call(body, lines, out_shape, *operands):
        cols = sum(line.shape[0] for line in lines) // count * LANES
        return pl.pallas_call(
            body,
            out_shape=[jax.ShapeDtypeStruct(shape, dtype) for shape, dtype in out_shape],
            **limits(rows, cols),
        )(*operands, *lines)

    block = pl.pallas_call(
        pack_kernel,
        out_shape=jax.ShapeDtypeStruct((high, wide), jnp.float32),
        compiler_params=pltpu.CompilerParams(vmem_limit_bytes=2 * MIB),
    )(jnp.concatenate([points, vectors], axis=0))
    later_points, block = lax.optimization_barrier((points, block))
    blocks = [send(block, "far", k) for k in [*range(2, far), 1][: far - 1]]
    row_points = [send(later_points, "pair", k) for k in range(1, pair)]
    blocks = lax.optimization_barrier(blocks)
    line = pl.pallas_call(
        functools.partial(line_kernel, count, width),
        out_shape=jax.ShapeDtypeStruct(line_shape(count, width, far), jnp.float32),
        compiler_params=pltpu.CompilerParams(vmem_limit_bytes=2 * MIB + 16 * far * high * wide),
    )(block, *blocks)
    steps = list(range(1, mid * rep))
    plane = [send(line, "plane", k) for k in steps[1:] + steps[:1]]
    totals = [((2 * nvec, width), jnp.float32)] * pair
    *total, row_feat, scale = call(
        functools.partial(first_kernel, pair, count),
        [line],
        totals + [((2 * rows, stack_rows(feat)), jnp.bfloat16), ((feat, LANES), jnp.float32)],
        lengthscales[:, None],
        points,
        *row_points,
    )

    def middle(total, lines, first):
        numbers = list(range(first, pair))
        if not lines or not numbers:
            return total
        total, lines = lax.optimization_barrier((total, lines))
        body = functools.partial(middle_kernel, numbers, count)
        return [*total[:first], *call(body, lines, totals[first:], scale, row_feat, *total[first:])]

    total = middle(total, plane[:-2], 0)
    total = middle(total, plane[-2:-1], 1)
    total, plane[-1:] = lax.optimization_barrier((total, plane[-1:]))

    def finish(k, total):
        lines = plane[-1:] if k else plane[-2:]
        body = functools.partial(last_kernel, count, k)
        (part,) = call(body, lines, [((nvec, width), jnp.float32)], scale, row_feat, total[k])
        return part

    parts = []
    for k in range(1, pair):
        part = finish(k, total)
        total, part = lax.optimization_barrier((total, part))
        parts.append(part)
    result = finish(0, total)
    for k, part in enumerate(parts, 1):
        back = [(target, source) for source, target in permutation(sizes, "pair", k)]
        result = result + lax.ppermute(part, AXES, back)
    return result


def solution(mesh):
    sizes = split_blocks(mesh.shape["blk"], mesh.shape["rep"])
    return jax.shard_map(
        functools.partial(per_device, sizes),
        mesh=mesh,
        in_specs=(P(None, AXES), P(None, AXES), P()),
        out_specs=P(None, AXES),
        check_vma=False,
    )
```

```python
import functools
import math

import jax
import jax.numpy as jnp
from jax import lax
from jax.experimental import pallas as pl
from jax.experimental.pallas import tpu as pltpu
from jax.sharding import PartitionSpec as P

AXES = ("blk", "rep")
LANES = 128
MIB = 1024 * 1024


def split_blocks(blk, rep):
    pair = 2 if blk % 2 == 0 else 1
    line = blk // pair
    mid = max(d for d in range(1, line + 1) if line % d == 0 and d * d <= line)
    return line // mid, mid, pair, rep


def partner(index, step, size):
    return index ^ step if size & (size - 1) == 0 else (index + step) % size


def permutation(sizes, axis, step):
    far, mid, pair, rep = sizes
    pairs = []
    for target in range(far * mid * pair * rep):
        rest, q = divmod(target, rep)
        rest, p = divmod(rest, pair)
        f, m = divmod(rest, mid)
        if axis == "far":
            f = partner(f, step, far)
        elif axis == "pair":
            p = partner(p, step, pair)
        else:
            m, q = divmod(partner(m * rep + q, step, mid * rep), rep)
        pairs.append((((f * mid + m) * pair + p) * rep + q, target))
    return pairs


def three_parts(value):
    first = value.astype(jnp.bfloat16).astype(jnp.float32)
    second = (value - first).astype(jnp.bfloat16).astype(jnp.float32)
    return first, second, value - first - second


def stack_rows(feat):
    return 6 * feat + 16


def norm_rows(values):
    width = next(value.shape[1] for value in values if not isinstance(value, float))
    halves = []
    for half in (values[:8], values[8:]):
        line = lax.broadcasted_iota(jnp.int32, (8, width), 0)
        rows = jnp.zeros((8, width), jnp.float32)
        for arrays in (False, True):
            for k, value in enumerate(half):
                if isinstance(value, float) != arrays:
                    rows = jnp.where(line == k, value, rows)
        halves.append(rows)
    return jnp.concatenate(halves, axis=0)


def norm_parts(z, first):
    high = jnp.sum(first * first, axis=0, keepdims=True)
    low = jnp.sum((z - first) * (z + first), axis=0, keepdims=True)
    one = high.astype(jnp.bfloat16).astype(jnp.float32)
    left = (high - one) + low
    two = left.astype(jnp.bfloat16).astype(jnp.float32)
    return one, two, left - two


def column_stack(z):
    a, b, c = three_parts(z)
    norms = norm_rows([*norm_parts(z, a), 1.0, 1.0, 1.0, 3.0, 3.0, 3.0, 1.0])
    return jnp.concatenate([a, norms, a, b, a, c, b], axis=0)


def row_stack(z, tripled):
    norms = norm_parts(z, three_parts(z)[0])
    a, b, c = three_parts(z * (-6.0 if tripled else -2.0))
    if tripled:
        norms = norm_rows([3.0] * 3 + [0.0] * 3 + [*norms])
    else:
        norms = norm_rows([1.0] * 3 + [*norms] + [0.0] * 3 + [1.0])
    return jnp.concatenate([a, norms, b, a, c, a, b], axis=0)


def packed_pieces(count, width):
    rest = width % LANES
    return LANES // rest if width > LANES and rest and LANES % rest == 0 and count % 8 == 0 else 0


def packed_shape(count, width):
    fit = packed_pieces(count, width)
    if not fit:
        return count, width
    return width // LANES * count + -(-(count // 8) // fit) * 8, LANES


def pack_kernel(block_ref, out_ref):
    block = block_ref[...]
    count, width = block.shape
    fit = packed_pieces(count, width)
    if not fit:
        out_ref[...] = block
        return
    full = width // LANES
    for k in range(full):
        out_ref[k * count : (k + 1) * count, :] = block[:, k * LANES : (k + 1) * LANES]
    base = full * count
    pieces = [block[at : at + 8, full * LANES :] for at in range(0, count, 8)]
    for first in range(0, len(pieces), fit):
        line = pieces[first : first + fit]
        line += [jnp.zeros_like(line[0])] * (fit - len(line))
        out_ref[base + first // fit * 8 : base + first // fit * 8 + 8, :] = jnp.concatenate(line, axis=1)


def line_shape(count, width, blocks):
    return -(-blocks * width // LANES) * count, LANES


def line_kernel(count, width, *refs):
    block_refs, out_ref = refs[:-1], refs[-1]
    fit = packed_pieces(count, width)
    full, rest = width // LANES, width % LANES
    if not fit:
        joined = [ref[...] for ref in block_refs]
    else:
        joined, at = [], 0
        for ref in block_refs:
            for k in range(full):
                out_ref[at : at + count, :] = ref[k * count : (k + 1) * count, :]
                at += count
            pieces = []
            for k in range(count // 8):
                begin = full * count + k // fit * 8
                pieces.append(ref[begin : begin + 8, k % fit * rest : (k % fit + 1) * rest])
            joined.append(jnp.concatenate(pieces, axis=0))
    begin = 0 if not fit else len(block_refs) * full * count
    over = -sum(item.shape[1] for item in joined) % LANES
    if over:
        joined.append(jnp.zeros((count, over), jnp.float32))
    tails = jnp.concatenate(joined, axis=1)
    for k in range(tails.shape[1] // LANES):
        out_ref[begin + k * count : begin + (k + 1) * count, :] = tails[:, k * LANES : (k + 1) * LANES]


def piece_values(scale, row_feat, piece):
    feat = scale.shape[0]
    rows = row_feat.shape[0] // 2
    col_feat = column_stack(piece[:feat] * scale).astype(jnp.bfloat16)
    vec = piece[feat:]
    vec_high = vec.astype(jnp.bfloat16)
    vec_low = (vec - vec_high.astype(jnp.float32)).astype(jnp.bfloat16)
    vec_parts = jnp.concatenate([vec_high, vec_low], axis=0)
    both = jnp.dot(row_feat, col_feat, preferred_element_type=jnp.float32)
    square = jnp.maximum(both[:rows], 1e-30)
    root = square * lax.rsqrt(square)
    value = (jnp.maximum(both[rows:], 1.0) + root) * jnp.exp2(root * (-1.0 / math.log(2.0)))
    high = value.astype(jnp.bfloat16)
    low = (value - high.astype(jnp.float32)).astype(jnp.bfloat16)
    return [high, low], [vec_parts, vec_parts]


def add_columns(total, scale, row_feat, line_refs, count):
    def products(pieces):
        values, vectors = [], []
        for piece in pieces:
            value, vector = piece_values(scale, row_feat, piece)
            values += value
            vectors += vector
        values, vectors = jnp.concatenate(values, axis=1), jnp.concatenate(vectors, axis=1)
        return lax.dot_general(vectors, values, (((1,), (1,)), ((), ())), preferred_element_type=jnp.float32)

    numbers = [ref.shape[0] // count for ref in line_refs]
    if sum(numbers) <= 16:
        pieces = [ref[k * count : (k + 1) * count, :] for ref, number in zip(line_refs, numbers) for k in range(number)]
        for piece in pieces:
            total = total + products([piece])
        return total
    for ref, number in zip(line_refs, numbers):

        def add(k, total, ref=ref):
            return total + products([ref[pl.ds(pl.multiple_of(k * count, 8), count), :]])

        total = lax.fori_loop(0, number, add, total)
    return total


def first_kernel(nrow, count, scale_ref, *refs):
    row_refs, line_refs = refs[:nrow], refs[nrow : -2 - nrow]
    total_refs, feat_ref, scale_out = refs[-2 - nrow : -2], refs[-2], refs[-1]
    feat, width = row_refs[0].shape
    scale = jnp.broadcast_to(jnp.sqrt(jnp.float32(5.0 / 3.0)) / scale_ref[...], (feat, LANES))
    scale_out[...] = scale
    for k, ref in enumerate(row_refs):
        z = ref[...] * scale[:, :1]
        begin = 2 * k * width
        feat_ref[begin : begin + width, :] = row_stack(z, True).T.astype(jnp.bfloat16)
        feat_ref[begin + width : begin + 2 * width, :] = row_stack(z, False).T.astype(jnp.bfloat16)
    for k, ref in enumerate(total_refs):
        rows = feat_ref[2 * k * width : 2 * (k + 1) * width, :]
        ref[...] = add_columns(jnp.zeros(ref.shape, jnp.float32), scale, rows, line_refs, count)


def middle_kernel(numbers, count, scale_ref, feat_ref, *refs):
    many = len(numbers)
    before_refs, line_refs, total_refs = refs[:many], refs[many:-many], refs[-many:]
    width = total_refs[0].shape[1]
    for k, before, after in zip(numbers, before_refs, total_refs):
        rows = feat_ref[2 * k * width : 2 * (k + 1) * width, :]
        after[...] = add_columns(before[...], scale_ref[...], rows, line_refs, count)


def last_kernel(count, number, scale_ref, feat_ref, before_ref, *refs):
    nvec, width = refs[-1].shape
    rows = feat_ref[2 * number * width : 2 * (number + 1) * width, :]
    part = add_columns(before_ref[...], scale_ref[...], rows, refs[:-1], count)
    refs[-1][...] = part[:nvec] + part[nvec:]


def limits(rows, cols):
    return {
        "compiler_params": pltpu.CompilerParams(vmem_limit_bytes=4 * MIB + 4096 * rows + 2048 * cols),
        "cost_estimate": pl.CostEstimate(flops=0, bytes_accessed=0, transcendentals=0),
    }


def per_device(sizes, points, vectors, lengthscales):
    far, mid, pair, rep = sizes
    (feat, width), nvec = points.shape, vectors.shape[0]
    count, rows = feat + nvec, pair * width
    high, wide = packed_shape(count, width)

    def send(item, axis, step):
        return lax.ppermute(item, AXES, permutation(sizes, axis, step))

    def call(body, lines, out_shape, *operands):
        cols = sum(line.shape[0] for line in lines) // count * LANES
        return pl.pallas_call(
            body,
            out_shape=[jax.ShapeDtypeStruct(shape, dtype) for shape, dtype in out_shape],
            **limits(rows, cols),
        )(*operands, *lines)

    block = pl.pallas_call(
        pack_kernel,
        out_shape=jax.ShapeDtypeStruct((high, wide), jnp.float32),
        compiler_params=pltpu.CompilerParams(vmem_limit_bytes=2 * MIB),
    )(jnp.concatenate([points, vectors], axis=0))
    later_points, block = lax.optimization_barrier((points, block))
    blocks = [send(block, "far", k) for k in [*range(2, far), 1][: far - 1]]
    row_points = [send(later_points, "pair", k) for k in range(1, pair)]
    blocks = lax.optimization_barrier(blocks)
    line = pl.pallas_call(
        functools.partial(line_kernel, count, width),
        out_shape=jax.ShapeDtypeStruct(line_shape(count, width, far), jnp.float32),
        compiler_params=pltpu.CompilerParams(vmem_limit_bytes=2 * MIB + 16 * far * high * wide),
    )(block, *blocks)
    steps = list(range(1, mid * rep))
    plane = [send(line, "plane", k) for k in steps[1:] + steps[:1]]
    totals = [((2 * nvec, width), jnp.float32)] * pair
    *total, row_feat, scale = call(
        functools.partial(first_kernel, pair, count),
        [line],
        totals + [((2 * rows, stack_rows(feat)), jnp.bfloat16), ((feat, LANES), jnp.float32)],
        lengthscales[:, None],
        points,
        *row_points,
    )

    def middle(total, lines, first):
        numbers = list(range(first, pair))
        if not lines or not numbers:
            return total
        total, lines = lax.optimization_barrier((total, lines))
        body = functools.partial(middle_kernel, numbers, count)
        return [*total[:first], *call(body, lines, totals[first:], scale, row_feat, *total[first:])]

    total = middle(total, plane[:-2], 0)
    total, plane[-2:] = lax.optimization_barrier((total, plane[-2:]))

    def finish(k, total):
        lines = plane[-2:]
        body = functools.partial(last_kernel, count, k)
        (part,) = call(body, lines, [((nvec, width), jnp.float32)], scale, row_feat, total[k])
        return part

    parts = []
    for k in range(1, pair):
        part = finish(k, total)
        total, part = lax.optimization_barrier((total, part))
        parts.append(part)
    result = finish(0, total)
    for k, part in enumerate(parts, 1):
        back = [(target, source) for source, target in permutation(sizes, "pair", k)]
        result = result + lax.ppermute(part, AXES, back)
    return result


def solution(mesh):
    sizes = split_blocks(mesh.shape["blk"], mesh.shape["rep"])
    return jax.shard_map(
        functools.partial(per_device, sizes),
        mesh=mesh,
        in_specs=(P(None, AXES), P(None, AXES), P()),
        out_specs=P(None, AXES),
        check_vma=False,
    )
```

```python
import functools
import math

import jax
import jax.numpy as jnp
from jax import lax
from jax.experimental import pallas as pl
from jax.experimental.pallas import tpu as pltpu
from jax.sharding import PartitionSpec as P

AXES = ("blk", "rep")
LANES = 128
MIB = 1024 * 1024


def split_blocks(blk, rep):
    pair = 2 if blk % 2 == 0 else 1
    line = blk // pair
    mid = max(d for d in range(1, line + 1) if line % d == 0 and d * d <= line)
    return line // mid, mid, pair, rep


def partner(index, step, size):
    return index ^ step if size & (size - 1) == 0 else (index + step) % size


def permutation(sizes, axis, step):
    far, mid, pair, rep = sizes
    pairs = []
    for target in range(far * mid * pair * rep):
        rest, q = divmod(target, rep)
        rest, p = divmod(rest, pair)
        f, m = divmod(rest, mid)
        if axis == "far":
            f = partner(f, step, far)
        elif axis == "pair":
            p = partner(p, step, pair)
        else:
            m, q = divmod(partner(m * rep + q, step, mid * rep), rep)
        pairs.append((((f * mid + m) * pair + p) * rep + q, target))
    return pairs


def three_parts(value):
    first = value.astype(jnp.bfloat16).astype(jnp.float32)
    second = (value - first).astype(jnp.bfloat16).astype(jnp.float32)
    return first, second, value - first - second


def stack_rows(feat):
    return 6 * feat + 16


def norm_rows(values):
    width = next(value.shape[1] for value in values if not isinstance(value, float))
    halves = []
    for half in (values[:8], values[8:]):
        line = lax.broadcasted_iota(jnp.int32, (8, width), 0)
        rows = jnp.zeros((8, width), jnp.float32)
        for arrays in (False, True):
            for k, value in enumerate(half):
                if isinstance(value, float) != arrays:
                    rows = jnp.where(line == k, value, rows)
        halves.append(rows)
    return jnp.concatenate(halves, axis=0)


def norm_parts(z, first):
    high = jnp.sum(first * first, axis=0, keepdims=True)
    low = jnp.sum((z - first) * (z + first), axis=0, keepdims=True)
    one = high.astype(jnp.bfloat16).astype(jnp.float32)
    left = (high - one) + low
    two = left.astype(jnp.bfloat16).astype(jnp.float32)
    return one, two, left - two


def column_stack(z):
    a, b, c = three_parts(z)
    norms = norm_rows([*norm_parts(z, a), 1.0, 1.0, 1.0, 3.0, 3.0, 3.0, 1.0])
    return jnp.concatenate([a, norms, a, b, a, c, b], axis=0)


def row_stack(z, tripled):
    norms = norm_parts(z, three_parts(z)[0])
    a, b, c = three_parts(z * (-6.0 if tripled else -2.0))
    if tripled:
        norms = norm_rows([3.0] * 3 + [0.0] * 3 + [*norms])
    else:
        norms = norm_rows([1.0] * 3 + [*norms] + [0.0] * 3 + [1.0])
    return jnp.concatenate([a, norms, b, a, c, a, b], axis=0)


def packed_pieces(count, width):
    rest = width % LANES
    return LANES // rest if width > LANES and rest and LANES % rest == 0 and count % 8 == 0 else 0


def packed_shape(count, width):
    fit = packed_pieces(count, width)
    if not fit:
        return count, width
    return width // LANES * count + -(-(count // 8) // fit) * 8, LANES


def pack_kernel(block_ref, out_ref):
    block = block_ref[...]
    count, width = block.shape
    fit = packed_pieces(count, width)
    if not fit:
        out_ref[...] = block
        return
    full = width // LANES
    for k in range(full):
        out_ref[k * count : (k + 1) * count, :] = block[:, k * LANES : (k + 1) * LANES]
    base = full * count
    pieces = [block[at : at + 8, full * LANES :] for at in range(0, count, 8)]
    for first in range(0, len(pieces), fit):
        line = pieces[first : first + fit]
        line += [jnp.zeros_like(line[0])] * (fit - len(line))
        out_ref[base + first // fit * 8 : base + first // fit * 8 + 8, :] = jnp.concatenate(line, axis=1)


def line_shape(count, width, blocks):
    return -(-blocks * width // LANES) * count, LANES


def line_kernel(count, width, *refs):
    block_refs, out_ref = refs[:-1], refs[-1]
    fit = packed_pieces(count, width)
    full, rest = width // LANES, width % LANES
    if not fit:
        joined = [ref[...] for ref in block_refs]
    else:
        joined, at = [], 0
        for ref in block_refs:
            for k in range(full):
                out_ref[at : at + count, :] = ref[k * count : (k + 1) * count, :]
                at += count
            pieces = []
            for k in range(count // 8):
                begin = full * count + k // fit * 8
                pieces.append(ref[begin : begin + 8, k % fit * rest : (k % fit + 1) * rest])
            joined.append(jnp.concatenate(pieces, axis=0))
    begin = 0 if not fit else len(block_refs) * full * count
    over = -sum(item.shape[1] for item in joined) % LANES
    if over:
        joined.append(jnp.zeros((count, over), jnp.float32))
    tails = jnp.concatenate(joined, axis=1)
    for k in range(tails.shape[1] // LANES):
        out_ref[begin + k * count : begin + (k + 1) * count, :] = tails[:, k * LANES : (k + 1) * LANES]


def piece_values(scale, row_feat, piece):
    feat = scale.shape[0]
    rows = row_feat.shape[0] // 2
    col_feat = column_stack(piece[:feat] * scale).astype(jnp.bfloat16)
    vec = piece[feat:]
    vec_high = vec.astype(jnp.bfloat16)
    vec_low = (vec - vec_high.astype(jnp.float32)).astype(jnp.bfloat16)
    vec_parts = jnp.concatenate([vec_high, vec_low], axis=0)
    both = jnp.dot(row_feat, col_feat, preferred_element_type=jnp.float32)
    square = jnp.maximum(both[:rows], 1e-30)
    root = square * lax.rsqrt(square)
    value = (jnp.maximum(both[rows:], 1.0) + root) * jnp.exp2(root * (-1.0 / math.log(2.0)))
    high = value.astype(jnp.bfloat16)
    low = (value - high.astype(jnp.float32)).astype(jnp.bfloat16)
    return [high, low], [vec_parts, vec_parts]


def add_columns(total, scale, row_feat, line_refs, count):
    def products(pieces):
        values, vectors = [], []
        for piece in pieces:
            value, vector = piece_values(scale, row_feat, piece)
            values += value
            vectors += vector
        values, vectors = jnp.concatenate(values, axis=1), jnp.concatenate(vectors, axis=1)
        return lax.dot_general(vectors, values, (((1,), (1,)), ((), ())), preferred_element_type=jnp.float32)

    numbers = [ref.shape[0] // count for ref in line_refs]
    if sum(numbers) <= 16:
        pieces = [ref[k * count : (k + 1) * count, :] for ref, number in zip(line_refs, numbers) for k in range(number)]
        for piece in pieces:
            total = total + products([piece])
        return total
    for ref, number in zip(line_refs, numbers):

        def add(k, total, ref=ref):
            return total + products([ref[pl.ds(pl.multiple_of(k * count, 8), count), :]])

        total = lax.fori_loop(0, number, add, total)
    return total


def first_kernel(nrow, count, scale_ref, *refs):
    row_refs, line_refs = refs[:nrow], refs[nrow : -2 - nrow]
    total_refs, feat_ref, scale_out = refs[-2 - nrow : -2], refs[-2], refs[-1]
    feat, width = row_refs[0].shape
    scale = jnp.broadcast_to(jnp.sqrt(jnp.float32(5.0 / 3.0)) / scale_ref[...], (feat, LANES))
    scale_out[...] = scale
    for k, ref in enumerate(row_refs):
        z = ref[...] * scale[:, :1]
        begin = 2 * k * width
        feat_ref[begin : begin + width, :] = row_stack(z, True).T.astype(jnp.bfloat16)
        feat_ref[begin + width : begin + 2 * width, :] = row_stack(z, False).T.astype(jnp.bfloat16)
    for k, ref in enumerate(total_refs):
        rows = feat_ref[2 * k * width : 2 * (k + 1) * width, :]
        ref[...] = add_columns(jnp.zeros(ref.shape, jnp.float32), scale, rows, line_refs, count)


def middle_kernel(numbers, count, scale_ref, feat_ref, *refs):
    many = len(numbers)
    before_refs, line_refs, total_refs = refs[:many], refs[many:-many], refs[-many:]
    width = total_refs[0].shape[1]
    for k, before, after in zip(numbers, before_refs, total_refs):
        rows = feat_ref[2 * k * width : 2 * (k + 1) * width, :]
        after[...] = add_columns(before[...], scale_ref[...], rows, line_refs, count)


def last_kernel(count, number, scale_ref, feat_ref, before_ref, *refs):
    nvec, width = refs[-1].shape
    rows = feat_ref[2 * number * width : 2 * (number + 1) * width, :]
    part = add_columns(before_ref[...], scale_ref[...], rows, refs[:-1], count)
    refs[-1][...] = part[:nvec] + part[nvec:]


def limits(rows, cols):
    return {
        "compiler_params": pltpu.CompilerParams(vmem_limit_bytes=4 * MIB + 4096 * rows + 2048 * cols),
        "cost_estimate": pl.CostEstimate(flops=0, bytes_accessed=0, transcendentals=0),
    }


def per_device(sizes, points, vectors, lengthscales):
    far, mid, pair, rep = sizes
    (feat, width), nvec = points.shape, vectors.shape[0]
    count, rows = feat + nvec, pair * width
    high, wide = packed_shape(count, width)

    def send(item, axis, step):
        return lax.ppermute(item, AXES, permutation(sizes, axis, step))

    def call(body, lines, out_shape, *operands):
        cols = sum(line.shape[0] for line in lines) // count * LANES
        return pl.pallas_call(
            body,
            out_shape=[jax.ShapeDtypeStruct(shape, dtype) for shape, dtype in out_shape],
            **limits(rows, cols),
        )(*operands, *lines)

    block = pl.pallas_call(
        pack_kernel,
        out_shape=jax.ShapeDtypeStruct((high, wide), jnp.float32),
        compiler_params=pltpu.CompilerParams(vmem_limit_bytes=2 * MIB),
    )(jnp.concatenate([points, vectors], axis=0))
    later_points, block = lax.optimization_barrier((points, block))
    blocks = [send(block, "far", k) for k in reversed(range(1, far))]
    row_points = [send(later_points, "pair", k) for k in range(1, pair)]
    blocks = lax.optimization_barrier(blocks)
    line = pl.pallas_call(
        functools.partial(line_kernel, count, width),
        out_shape=jax.ShapeDtypeStruct(line_shape(count, width, far), jnp.float32),
        compiler_params=pltpu.CompilerParams(vmem_limit_bytes=2 * MIB + 16 * far * high * wide),
    )(block, *blocks)
    steps = list(range(1, mid * rep))
    plane = [send(line, "plane", k) for k in steps[1:] + steps[:1]]
    totals = [((2 * nvec, width), jnp.float32)] * pair
    *total, row_feat, scale = call(
        functools.partial(first_kernel, pair, count),
        [line],
        totals + [((2 * rows, stack_rows(feat)), jnp.bfloat16), ((feat, LANES), jnp.float32)],
        lengthscales[:, None],
        points,
        *row_points,
    )

    def middle(total, lines, first):
        numbers = list(range(first, pair))
        if not lines or not numbers:
            return total
        total, lines = lax.optimization_barrier((total, lines))
        body = functools.partial(middle_kernel, numbers, count)
        return [*total[:first], *call(body, lines, totals[first:], scale, row_feat, *total[first:])]

    total = middle(total, plane[:-2], 0)
    total = middle(total, plane[-2:-1], 1)
    total, plane[-1:] = lax.optimization_barrier((total, plane[-1:]))

    def finish(k, total):
        lines = plane[-1:] if k else plane[-2:]
        body = functools.partial(last_kernel, count, k)
        (part,) = call(body, lines, [((nvec, width), jnp.float32)], scale, row_feat, total[k])
        return part

    parts = []
    for k in range(1, pair):
        part = finish(k, total)
        total, part = lax.optimization_barrier((total, part))
        parts.append(part)
    result = finish(0, total)
    for k, part in enumerate(parts, 1):
        back = [(target, source) for source, target in permutation(sizes, "pair", k)]
        result = result + lax.ppermute(part, AXES, back)
    return result


def solution(mesh):
    sizes = split_blocks(mesh.shape["blk"], mesh.shape["rep"])
    return jax.shard_map(
        functools.partial(per_device, sizes),
        mesh=mesh,
        in_specs=(P(None, AXES), P(None, AXES), P()),
        out_specs=P(None, AXES),
        check_vma=False,
    )
```

```python
import functools
import math

import jax
import jax.numpy as jnp
from jax import lax
from jax.experimental import pallas as pl
from jax.experimental.pallas import tpu as pltpu
from jax.sharding import PartitionSpec as P

AXES = ("blk", "rep")
LANES = 128
MIB = 1024 * 1024


def split_blocks(blk, rep):
    pair = 2 if blk % 2 == 0 else 1
    line = blk // pair
    mid = max(d for d in range(1, line + 1) if line % d == 0 and d * d <= line)
    return line // mid, mid, pair, rep


def partner(index, step, size):
    return index ^ step if size & (size - 1) == 0 else (index + step) % size


def permutation(sizes, axis, step):
    far, mid, pair, rep = sizes
    pairs = []
    for target in range(far * mid * pair * rep):
        rest, q = divmod(target, rep)
        rest, p = divmod(rest, pair)
        f, m = divmod(rest, mid)
        if axis == "far":
            f = partner(f, step, far)
        elif axis == "pair":
            p = partner(p, step, pair)
        else:
            m, q = divmod(partner(m * rep + q, step, mid * rep), rep)
        pairs.append((((f * mid + m) * pair + p) * rep + q, target))
    return pairs


def three_parts(value):
    first = value.astype(jnp.bfloat16).astype(jnp.float32)
    second = (value - first).astype(jnp.bfloat16).astype(jnp.float32)
    return first, second, value - first - second


def stack_rows(feat):
    return 6 * feat + 16


def norm_rows(values):
    width = next(value.shape[1] for value in values if not isinstance(value, float))
    halves = []
    for half in (values[:8], values[8:]):
        line = lax.broadcasted_iota(jnp.int32, (8, width), 0)
        rows = jnp.zeros((8, width), jnp.float32)
        for arrays in (False, True):
            for k, value in enumerate(half):
                if isinstance(value, float) != arrays:
                    rows = jnp.where(line == k, value, rows)
        halves.append(rows)
    return jnp.concatenate(halves, axis=0)


def norm_parts(z, first):
    high = jnp.sum(first * first, axis=0, keepdims=True)
    low = jnp.sum((z - first) * (z + first), axis=0, keepdims=True)
    one = high.astype(jnp.bfloat16).astype(jnp.float32)
    left = (high - one) + low
    two = left.astype(jnp.bfloat16).astype(jnp.float32)
    return one, two, left - two


def column_stack(z):
    a, b, c = three_parts(z)
    norms = norm_rows([*norm_parts(z, a), 1.0, 1.0, 1.0, 3.0, 3.0, 3.0, 1.0])
    return jnp.concatenate([a, norms, a, b, a, c, b], axis=0)


def row_stack(z, tripled):
    norms = norm_parts(z, three_parts(z)[0])
    a, b, c = three_parts(z * (-6.0 if tripled else -2.0))
    if tripled:
        norms = norm_rows([3.0] * 3 + [0.0] * 3 + [*norms])
    else:
        norms = norm_rows([1.0] * 3 + [*norms] + [0.0] * 3 + [1.0])
    return jnp.concatenate([a, norms, b, a, c, a, b], axis=0)


def packed_pieces(count, width):
    rest = width % LANES
    return LANES // rest if width > LANES and rest and LANES % rest == 0 and count % 8 == 0 else 0


def packed_shape(count, width):
    fit = packed_pieces(count, width)
    if not fit:
        return count, width
    return width // LANES * count + -(-(count // 8) // fit) * 8, LANES


def pack_kernel(block_ref, out_ref):
    block = block_ref[...]
    count, width = block.shape
    fit = packed_pieces(count, width)
    if not fit:
        out_ref[...] = block
        return
    full = width // LANES
    for k in range(full):
        out_ref[k * count : (k + 1) * count, :] = block[:, k * LANES : (k + 1) * LANES]
    base = full * count
    pieces = [block[at : at + 8, full * LANES :] for at in range(0, count, 8)]
    for first in range(0, len(pieces), fit):
        line = pieces[first : first + fit]
        line += [jnp.zeros_like(line[0])] * (fit - len(line))
        out_ref[base + first // fit * 8 : base + first // fit * 8 + 8, :] = jnp.concatenate(line, axis=1)


def line_shape(count, width, blocks):
    return -(-blocks * width // LANES) * count, LANES


def line_kernel(count, width, *refs):
    block_refs, out_ref = refs[:-1], refs[-1]
    fit = packed_pieces(count, width)
    full, rest = width // LANES, width % LANES
    if not fit:
        joined = [ref[...] for ref in block_refs]
    else:
        joined, at = [], 0
        for ref in block_refs:
            for k in range(full):
                out_ref[at : at + count, :] = ref[k * count : (k + 1) * count, :]
                at += count
            pieces = []
            for k in range(count // 8):
                begin = full * count + k // fit * 8
                pieces.append(ref[begin : begin + 8, k % fit * rest : (k % fit + 1) * rest])
            joined.append(jnp.concatenate(pieces, axis=0))
    begin = 0 if not fit else len(block_refs) * full * count
    over = -sum(item.shape[1] for item in joined) % LANES
    if over:
        joined.append(jnp.zeros((count, over), jnp.float32))
    tails = jnp.concatenate(joined, axis=1)
    for k in range(tails.shape[1] // LANES):
        out_ref[begin + k * count : begin + (k + 1) * count, :] = tails[:, k * LANES : (k + 1) * LANES]


def piece_values(scale, row_feat, piece):
    feat = scale.shape[0]
    rows = row_feat.shape[0] // 2
    col_feat = column_stack(piece[:feat] * scale).astype(jnp.bfloat16)
    vec = piece[feat:]
    vec_high = vec.astype(jnp.bfloat16)
    vec_low = (vec - vec_high.astype(jnp.float32)).astype(jnp.bfloat16)
    vec_parts = jnp.concatenate([vec_high, vec_low], axis=0)
    both = jnp.dot(row_feat, col_feat, preferred_element_type=jnp.float32)
    square = jnp.maximum(both[:rows], 1e-30)
    root = square * lax.rsqrt(square)
    value = (jnp.maximum(both[rows:], 1.0) + root) * jnp.exp2(root * (-1.0 / math.log(2.0)))
    high = value.astype(jnp.bfloat16)
    low = (value - high.astype(jnp.float32)).astype(jnp.bfloat16)
    return [high, low], [vec_parts, vec_parts]


def add_columns(total, scale, row_feat, line_refs, count):
    def products(pieces):
        values, vectors = [], []
        for piece in pieces:
            value, vector = piece_values(scale, row_feat, piece)
            values += value
            vectors += vector
        values, vectors = jnp.concatenate(values, axis=1), jnp.concatenate(vectors, axis=1)
        return lax.dot_general(vectors, values, (((1,), (1,)), ((), ())), preferred_element_type=jnp.float32)

    numbers = [ref.shape[0] // count for ref in line_refs]
    if sum(numbers) <= 16:
        pieces = [ref[k * count : (k + 1) * count, :] for ref, number in zip(line_refs, numbers) for k in range(number)]
        for piece in pieces:
            total = total + products([piece])
        return total
    for ref, number in zip(line_refs, numbers):

        def add(k, total, ref=ref):
            return total + products([ref[pl.ds(pl.multiple_of(k * count, 8), count), :]])

        total = lax.fori_loop(0, number, add, total)
    return total


def first_kernel(nrow, count, scale_ref, *refs):
    row_refs, line_refs = refs[:nrow], refs[nrow : -2 - nrow]
    total_refs, feat_ref, scale_out = refs[-2 - nrow : -2], refs[-2], refs[-1]
    feat, width = row_refs[0].shape
    scale = jnp.broadcast_to(jnp.sqrt(jnp.float32(5.0 / 3.0)) / scale_ref[...], (feat, LANES))
    scale_out[...] = scale
    for k, ref in enumerate(row_refs):
        z = ref[...] * scale[:, :1]
        begin = 2 * k * width
        feat_ref[begin : begin + width, :] = row_stack(z, True).T.astype(jnp.bfloat16)
        feat_ref[begin + width : begin + 2 * width, :] = row_stack(z, False).T.astype(jnp.bfloat16)
    for k, ref in enumerate(total_refs):
        rows = feat_ref[2 * k * width : 2 * (k + 1) * width, :]
        ref[...] = add_columns(jnp.zeros(ref.shape, jnp.float32), scale, rows, line_refs, count)


def middle_kernel(numbers, count, scale_ref, feat_ref, *refs):
    many = len(numbers)
    before_refs, line_refs, total_refs = refs[:many], refs[many:-many], refs[-many:]
    width = total_refs[0].shape[1]
    for k, before, after in zip(numbers, before_refs, total_refs):
        rows = feat_ref[2 * k * width : 2 * (k + 1) * width, :]
        after[...] = add_columns(before[...], scale_ref[...], rows, line_refs, count)


def last_kernel(count, number, scale_ref, feat_ref, before_ref, *refs):
    nvec, width = refs[-1].shape
    rows = feat_ref[2 * number * width : 2 * (number + 1) * width, :]
    part = add_columns(before_ref[...], scale_ref[...], rows, refs[:-1], count)
    refs[-1][...] = part[:nvec] + part[nvec:]


def sum_kernel(*refs):
    total = refs[0][...]
    for ref in refs[1:-1]:
        total = total + ref[...]
    refs[-1][...] = total


def limits(rows, cols):
    return {
        "compiler_params": pltpu.CompilerParams(vmem_limit_bytes=4 * MIB + 4096 * rows + 2048 * cols),
        "cost_estimate": pl.CostEstimate(flops=0, bytes_accessed=0, transcendentals=0),
    }


def per_device(sizes, points, vectors, lengthscales):
    far, mid, pair, rep = sizes
    (feat, width), nvec = points.shape, vectors.shape[0]
    count, rows = feat + nvec, pair * width
    high, wide = packed_shape(count, width)

    def send(item, axis, step):
        return lax.ppermute(item, AXES, permutation(sizes, axis, step))

    def call(body, lines, out_shape, *operands):
        cols = sum(line.shape[0] for line in lines) // count * LANES
        return pl.pallas_call(
            body,
            out_shape=[jax.ShapeDtypeStruct(shape, dtype) for shape, dtype in out_shape],
            **limits(rows, cols),
        )(*operands, *lines)

    block = pl.pallas_call(
        pack_kernel,
        out_shape=jax.ShapeDtypeStruct((high, wide), jnp.float32),
        compiler_params=pltpu.CompilerParams(vmem_limit_bytes=2 * MIB),
    )(jnp.concatenate([points, vectors], axis=0))
    later_points, block = lax.optimization_barrier((points, block))
    blocks = [send(block, "far", k) for k in [*range(2, far), 1][: far - 1]]
    row_points = [send(later_points, "pair", k) for k in range(1, pair)]
    blocks = lax.optimization_barrier(blocks)
    line = pl.pallas_call(
        functools.partial(line_kernel, count, width),
        out_shape=jax.ShapeDtypeStruct(line_shape(count, width, far), jnp.float32),
        compiler_params=pltpu.CompilerParams(vmem_limit_bytes=2 * MIB + 16 * far * high * wide),
    )(block, *blocks)
    steps = list(range(1, mid * rep))
    plane = [send(line, "plane", k) for k in steps[1:] + steps[:1]]
    totals = [((2 * nvec, width), jnp.float32)] * pair
    *total, row_feat, scale = call(
        functools.partial(first_kernel, pair, count),
        [line],
        totals + [((2 * rows, stack_rows(feat)), jnp.bfloat16), ((feat, LANES), jnp.float32)],
        lengthscales[:, None],
        points,
        *row_points,
    )

    def middle(total, lines, first):
        numbers = list(range(first, pair))
        if not lines or not numbers:
            return total
        total, lines = lax.optimization_barrier((total, lines))
        body = functools.partial(middle_kernel, numbers, count)
        return [*total[:first], *call(body, lines, totals[first:], scale, row_feat, *total[first:])]

    total = middle(total, plane[:-2], 0)
    total = middle(total, plane[-2:-1], 1)
    total, plane[-1:] = lax.optimization_barrier((total, plane[-1:]))

    def finish(k, total):
        lines = plane[-1:] if k else plane[-2:]
        body = functools.partial(last_kernel, count, k)
        (part,) = call(body, lines, [((nvec, width), jnp.float32)], scale, row_feat, total[k])
        return part

    parts = []
    for k in range(1, pair):
        part = finish(k, total)
        total, part = lax.optimization_barrier((total, part))
        parts.append(part)
    result = finish(0, total)
    others = []
    for k, part in enumerate(parts, 1):
        back = [(target, source) for source, target in permutation(sizes, "pair", k)]
        others.append(lax.ppermute(part, AXES, back))
    return pl.pallas_call(
        sum_kernel,
        out_shape=jax.ShapeDtypeStruct((nvec, width), jnp.float32),
        compiler_params=pltpu.CompilerParams(vmem_limit_bytes=2 * MIB),
    )(result, *others)


def solution(mesh):
    sizes = split_blocks(mesh.shape["blk"], mesh.shape["rep"])
    return jax.shard_map(
        functools.partial(per_device, sizes),
        mesh=mesh,
        in_specs=(P(None, AXES), P(None, AXES), P()),
        out_specs=P(None, AXES),
        check_vma=False,
    )
```
